32 devices in a mesh: dp: 2 (over core), fsdp: 16 (over z, y, x).
Axes of the slice: x: 2, y: 2, z: 4, core: 2. Of those that a mesh axis runs over, the one named last changes fastest.
Arguments:
- pixels: float32 [32, 6, 3, 50176], P(('dp', 'fsdp')), may hold values from -14 to 14
- running_mean: float32 [6], replicated, may hold values from -1.5 to 1.5
- running_variance: float32 [6], replicated, may hold values from 0.5 to 2
- momentum: float32 [6], replicated, may hold values from 0.5 to 0.95
- keep_count: int32 [32], P(('dp', 'fsdp')), may hold values from 59 to 236, as said below
- visible_index: int32 [32, 236], P(('dp', 'fsdp')), may hold values from 0 to 587, as said below
- encoder_flat: float32 [8269824], P('fsdp'), may hold values from -5 to 5
- decoder_flat: float32 [4337664], P('fsdp'), may hold values from -5 to 5
Outputs:
- masked_loss: float32 [], replicated
- pixel_grad: float32 [32, 6, 3, 50176], P(('dp', 'fsdp'))
- encoder_grad: float32 [8269824], P('fsdp')
- decoder_grad: float32 [4337664], P('fsdp')
- next_mean: float32 [6], replicated
- next_variance: float32 [6], replicated
The draws below stay inside these ranges and needn't reach their ends.
Inputs may be any that keep to these rules, and one draw needn't show every extreme that they name: `keep_count`: in every draw some item has exactly 236 visible tokens and another exactly 59. `visible_index`: each row holds distinct token numbers.
All inputs are finite; a program needn't handle non-finite values.
Results may differ from the reference program's by a relative error of at most 0.0003.
Values sent between devices are 32-bit elements; how exact they have to be, the bound alone decides.
No kernel may reach another device: no remote copies, remote signals or barrier semaphores. Data moves between devices by JAX's collectives and lax.ppermute only.
A program may use at most 384 MiB of HBM per device.

```python
import math
import jax
import jax.numpy as jnp
from jax import lax

D_ENC = 768
HEADS_E = 12
MLP_E = 3072
D_DEC = 512
HEADS_D = 16
MLP_D = 2048
BANDS = 6
PATCH = 16
FRAMES = 3
GRID = 14
TOK_ITEM = 588
AREA = 50176
PIX = 1536
KEEP_MAX = 236
KEEP_MIN = 59
ITEMS = 32
P_ENC = 8269824
P_DEC = 4337664


def block_shapes_drawn(width, hidden):
    return [(width,), (width,), (width, 3 * width), (width,), (width,), (width, width), (width,), (width,), (width,), (width, hidden), (hidden,), (hidden, width), (width,)]


def block_rules(width, hidden, keys_seen):
    return [(0.1, 1.0), (0.1, 0.0), (width ** (-0.5), 0.0), (0.1, 0.0), (0.1, 0.0), (math.sqrt(keys_seen / width) / 2.0, 0.0), (0.1, 0.0), (0.1, 1.0), (0.1, 0.0), (width ** (-0.5), 0.0), (0.1, 0.0), (hidden ** (-0.5), 0.0), (0.1, 0.0)]


def encoder_shapes_drawn():
    return [(PIX, D_ENC), (D_ENC,)] + block_shapes_drawn(D_ENC, MLP_E) + [(D_ENC,), (D_ENC,)]


def encoder_rules():
    return [(PIX ** (-0.5), 0.0), (0.1, 0.0)] + block_rules(D_ENC, MLP_E, KEEP_MAX) + [(0.1, 1.0), (0.1, 0.0)]


def decoder_shapes_drawn():
    return [(D_ENC, D_DEC), (D_DEC,), (D_DEC,)] + block_shapes_drawn(D_DEC, MLP_D) + [(D_DEC,), (D_DEC,), (D_DEC, PIX), (PIX,)]


def decoder_rules():
    return [(D_ENC ** (-0.5), 0.0), (0.1, 0.0), (1.0, 0.0)] + block_rules(D_DEC, MLP_D, TOK_ITEM) + [(0.1, 1.0), (0.1, 0.0), (D_DEC ** (-0.5), 0.0), (0.1, 0.0)]


def flat_layout(shapes, rules, total):
    scales = []
    shifts = []
    used = 0
    for piece_shape, rule in zip(shapes, rules):
        length = math.prod(piece_shape)
        scales.append(jnp.full((length,), rule[0], jnp.float32))
        shifts.append(jnp.full((length,), rule[1], jnp.float32))
        used += length
    scales.append(jnp.ones((total - used,), jnp.float32))
    shifts.append(jnp.zeros((total - used,), jnp.float32))
    return (jnp.concatenate(scales), jnp.concatenate(shifts))


def draw_pixels(key, part):
    key = jax.random.fold_in(key, 11)
    key_offset, key_scale, key_noise = jax.random.split(key, 3)
    full_shape = (ITEMS, BANDS, FRAMES, AREA)
    offsets = jax.random.uniform(key_offset, (ITEMS, BANDS), jnp.float32, -2.0, 2.0)
    scales = jnp.exp(jax.random.uniform(key_scale, (ITEMS, BANDS), jnp.float32, math.log(0.5), math.log(2.0)))
    noise = jnp.clip(jax.random.normal(key_noise, full_shape, jnp.float32), -6.0, 6.0)
    return offsets[:, :, None, None] + scales[:, :, None, None] * noise


def draw_keep_count(key, part):
    key = jax.random.fold_in(key, 13)
    key_counts, key_first, key_second = jax.random.split(key, 3)
    counts = jax.random.randint(key_counts, (ITEMS,), KEEP_MIN, KEEP_MAX + 1)
    first = jax.random.randint(key_first, (), 0, ITEMS)
    second = (first + 1 + jax.random.randint(key_second, (), 0, ITEMS - 1)) % ITEMS
    counts = counts.at[first].set(KEEP_MAX).at[second].set(KEEP_MIN)
    return counts.astype(jnp.int32)


def draw_visible_index(key, part):
    key = jax.random.fold_in(key, 17)
    item_keys = jax.random.split(key, ITEMS)

    def one_order(item_key):
        return jax.random.permutation(item_key, TOK_ITEM)
    orders = jax.vmap(one_order)(item_keys)
    return orders[:, :KEEP_MAX].astype(jnp.int32)


def draw_encoder_flat(key, part):
    key = jax.random.fold_in(key, 5)
    scales, shifts = flat_layout(encoder_shapes_drawn(), encoder_rules(), P_ENC)
    noise = jnp.clip(jax.random.normal(key, (P_ENC,), jnp.float32), -4.0, 4.0)
    return shifts + scales * noise


def draw_decoder_flat(key, part):
    key = jax.random.fold_in(key, 7)
    scales, shifts = flat_layout(decoder_shapes_drawn(), decoder_rules(), P_DEC)
    noise = jnp.clip(jax.random.normal(key, (P_DEC,), jnp.float32), -4.0, 4.0)
    return shifts + scales * noise


def setup_inputs(seed: int = 0) -> dict:
    seeds = jax.random.split(jax.random.key(seed), 9)
    return {
        "pixels": draw_pixels(jax.random.fold_in(seeds[8], 71), 0),
        "running_mean": jnp.clip(jax.random.uniform(seeds[1], (BANDS,), jnp.float32, -1.5, 1.5), -1.5, 1.5),
        "running_variance": jnp.clip(jnp.exp(jax.random.uniform(seeds[2], (BANDS,), jnp.float32, math.log(0.5), math.log(2.0))), 0.5, 2.0),
        "momentum": jnp.clip(jax.random.uniform(seeds[3], (BANDS,), jnp.float32, 0.5, 0.95), 0.5, 0.95),
        "keep_count": draw_keep_count(jax.random.fold_in(seeds[8], 71), 0),
        "visible_index": draw_visible_index(jax.random.fold_in(seeds[8], 71), 0),
        "encoder_flat": draw_encoder_flat(jax.random.fold_in(seeds[8], 71), 0),
        "decoder_flat": draw_decoder_flat(jax.random.fold_in(seeds[8], 71), 0),
    }


EPS_NORM = 1e-06
MASKED_SCORE = -1e+30

@jax.custom_vjp
def low(v):
    return lax.optimization_barrier(v.astype(jnp.bfloat16)).astype(jnp.float32)

@jax.custom_vjp
def low_back(v):
    return v

def low_keep(v):
    return (low(v), None)

def low_pass(kept, grad):
    return (grad,)

def back_keep(v):
    return (v, None)

def back_low(kept, grad):
    return (low(grad),)
low.defvjp(low_keep, low_pass)
low_back.defvjp(back_keep, back_low)

def matmul(left, right):
    return jnp.dot(left, right, precision=lax.Precision.HIGHEST, preferred_element_type=jnp.float32)

def block_shapes(width, hidden):
    return [(width,), (width,), (width, 3 * width), (width,), (width,), (width, width), (width,), (width,), (width,), (width, hidden), (hidden,), (hidden, width), (width,)]

def encoder_shapes():
    return [(PIX, D_ENC), (D_ENC,)] + block_shapes(D_ENC, MLP_E) + [(D_ENC,), (D_ENC,)]

def decoder_shapes():
    return [(D_ENC, D_DEC), (D_DEC,), (D_DEC,)] + block_shapes(D_DEC, MLP_D) + [(D_DEC,), (D_DEC,), (D_DEC, PIX), (PIX,)]

def unpack(flat, shapes):
    pieces = []
    offset = 0
    for piece_shape in shapes:
        length = math.prod(piece_shape)
        pieces.append(flat[offset:offset + length].reshape(piece_shape))
        offset += length
    return pieces

def sincos_part(width, positions):
    frequency = 1.0 / 10000.0 ** (jnp.arange(width // 2).astype(jnp.float32) / (width / 2.0))
    angles = positions[:, None] * frequency[None, :]
    return jnp.concatenate([jnp.sin(angles), jnp.cos(angles)], axis=1)

def position_table(width):
    token_ids = jnp.arange(TOK_ITEM).astype(jnp.int32)
    frame_pos = (token_ids // (GRID * GRID)).astype(jnp.float32)
    row_pos = (token_ids // GRID % GRID).astype(jnp.float32)
    column_pos = (token_ids % GRID).astype(jnp.float32)
    return jnp.concatenate([sincos_part(width // 16 * 4, frame_pos), sincos_part(width // 16 * 6, row_pos), sincos_part(width // 16 * 6, column_pos)], axis=1)

def layer_norm(values, gain, shift):
    centre = lax.optimization_barrier(jnp.mean(values, axis=-1, keepdims=True))
    spread = lax.optimization_barrier(jnp.mean(jnp.square(values - centre), axis=-1, keepdims=True))
    return (values - centre) * lax.rsqrt(spread + EPS_NORM) * gain + shift

def attend_core(queries, keys, values, key_bias):
    scaling = 1.0 / math.sqrt(queries.shape[-1])
    scores = jnp.einsum('qhd,khd->hqk', queries, keys, precision=lax.Precision.HIGHEST) * scaling + key_bias[None, None, :]
    row_top = lax.optimization_barrier(jnp.max(scores, axis=-1, keepdims=True))
    weights = jnp.exp(scores - row_top)
    weights = weights / lax.optimization_barrier(jnp.sum(weights, axis=-1, keepdims=True))
    return jnp.einsum('hqk,khd->qhd', weights, values, precision=lax.Precision.HIGHEST)

def transformer_block(stream, params, head_count, key_bias):
    first_gain, first_shift, qkv_weight, query_bias, value_bias, out_weight, out_bias, second_gain, second_shift, up_weight, up_bias, down_weight, down_bias = params
    row_count, model_width = stream.shape
    head_size = model_width // head_count
    normed = layer_norm(stream, first_gain, first_shift)
    joined = matmul(normed, qkv_weight)
    queries = (joined[:, :model_width] + query_bias).reshape(row_count, head_count, head_size)
    keys = joined[:, model_width:2 * model_width].reshape(row_count, head_count, head_size)
    values = (joined[:, 2 * model_width:] + value_bias).reshape(row_count, head_count, head_size)
    mixed = jax.checkpoint(attend_core)(queries, keys, values, key_bias).reshape(row_count, model_width)
    stream = stream + matmul(mixed, out_weight) + out_bias
    normed = layer_norm(stream, second_gain, second_shift)
    hidden = jax.nn.gelu(matmul(normed, up_weight) + up_bias, approximate=False)
    return stream + matmul(hidden, down_weight) + down_bias

def normalize(pixel_block, running_mean, running_variance):
    inverse = lax.rsqrt(running_variance + EPS_NORM)
    return (pixel_block - running_mean[None, :, None, None]) * inverse[None, :, None, None]

def patchify(normed):
    items_here = normed.shape[0]
    grid_view = normed.reshape(items_here, BANDS, FRAMES, GRID, PATCH, GRID, PATCH)
    return grid_view.transpose(0, 2, 3, 5, 1, 4, 6).reshape(items_here, TOK_ITEM, PIX)

def encode_item(encoder, patch_one, chosen, keep_one):
    slots = jnp.arange(KEEP_MAX).astype(jnp.int32)
    key_bias = jnp.where(slots < keep_one, 0.0, MASKED_SCORE).astype(jnp.float32)
    visible = jnp.take(patch_one, chosen, axis=0)
    places = jnp.take(position_table(D_ENC), chosen, axis=0)
    stream = matmul(visible, encoder[0]) + encoder[1] + places
    stream = transformer_block(stream, encoder[2:15], HEADS_E, key_bias)
    return layer_norm(stream, encoder[15], encoder[16])

def decode_item(decoder, encoded, patch_one, chosen, keep_one):
    slots = jnp.arange(KEEP_MAX).astype(jnp.int32)
    live = (slots < keep_one).astype(jnp.float32)
    token_ids = jnp.arange(TOK_ITEM).astype(jnp.int32)
    placer = (chosen[:, None] == token_ids[None, :]).astype(jnp.float32) * live[:, None]
    hidden_mask = 1.0 - lax.optimization_barrier(jnp.sum(placer, axis=0))
    latent = matmul(encoded, decoder[0]) + decoder[1]
    stream = jnp.einsum('st,sd->td', placer, latent, precision=lax.Precision.HIGHEST)
    stream = stream + hidden_mask[:, None] * decoder[2][None, :] + position_table(D_DEC)
    stream = transformer_block(stream, decoder[3:16], HEADS_D, jnp.zeros((TOK_ITEM,), jnp.float32))
    normed = layer_norm(stream, decoder[16], decoder[17])
    predicted = matmul(normed, decoder[18]) + decoder[19]
    error = predicted - patch_one
    squared = jnp.sum(hidden_mask[:, None] * error * error)
    return (squared / (PATCH * PATCH), squared)

def reference(pixels, running_mean, running_variance, momentum, keep_count, visible_index, encoder_flat, decoder_flat):

    def total(pixel_block, encoder_full, decoder_full):
        encoder = unpack(encoder_full, encoder_shapes())
        decoder = unpack(decoder_full, decoder_shapes())
        patches = patchify(normalize(pixel_block, running_mean, running_variance))

        def one_item(inputs):
            patch_one, chosen, keep_one = inputs
            encoded = encode_item(encoder, patch_one, chosen, keep_one)
            return decode_item(decoder, encoded, patch_one, chosen, keep_one)
        objectives, squares = lax.map(one_item, (patches, visible_index, keep_count))
        return (jnp.sum(objectives), jnp.sum(squares))
    objective, pull_back, squared = jax.vjp(total, pixels, encoder_flat, decoder_flat, has_aux=True)
    pixel_grad, encoder_grad, decoder_grad = pull_back(jnp.ones((), jnp.float32))
    masked_total = jnp.sum(TOK_ITEM - keep_count).astype(jnp.float32)
    masked_loss = squared / (masked_total * PIX)
    band_mean = lax.optimization_barrier(jnp.mean(pixels, axis=(0, 2, 3)))
    band_square = lax.optimization_barrier(jnp.mean(pixels * pixels, axis=(0, 2, 3)))
    band_var = band_square - band_mean * band_mean
    next_mean = (1.0 - momentum) * running_mean + momentum * band_mean
    next_variance = (1.0 - momentum) * running_variance + momentum * band_var
    return (masked_loss, pixel_grad, encoder_grad, decoder_grad, next_mean, next_variance)
```

```python
import math

import jax
import jax.numpy as jnp
from jax import lax
from jax.sharding import PartitionSpec as P

D_ENC = 768
HEADS_E = 12
MLP_E = 3072
D_DEC = 512
HEADS_D = 16
MLP_D = 2048
BANDS = 6
PATCH = 16
FRAMES = 3
GRID = 14
TOK_ITEM = 588
IMG = 224
PIX = 1536
KEEP_MAX = 236


EPS_NORM = 1e-06
MASKED_SCORE = -1e30
PREC = lax.Precision.HIGH


def matmul(left, right):
    return jnp.dot(left, right, precision=PREC, preferred_element_type=jnp.float32)


def block_shapes(width, hidden):
    return [
        (width,),
        (width,),
        (width, 3 * width),
        (width,),
        (width,),
        (width, width),
        (width,),
        (width,),
        (width,),
        (width, hidden),
        (hidden,),
        (hidden, width),
        (width,),
    ]


def encoder_shapes():
    return [(PIX, D_ENC), (D_ENC,)] + block_shapes(D_ENC, MLP_E) + [(D_ENC,), (D_ENC,)]


def decoder_shapes():
    return (
        [(D_ENC, D_DEC), (D_DEC,), (D_DEC,)]
        + block_shapes(D_DEC, MLP_D)
        + [(D_DEC,), (D_DEC,), (D_DEC, PIX), (PIX,)]
    )


def unpack(flat, shapes):
    pieces = []
    offset = 0
    for piece_shape in shapes:
        length = math.prod(piece_shape)
        pieces.append(flat[offset : offset + length].reshape(piece_shape))
        offset += length
    return pieces


def sincos_part(width, positions):
    frequency = 1.0 / 10000.0 ** (jnp.arange(width // 2).astype(jnp.float32) / (width / 2.0))
    angles = positions[:, None] * frequency[None, :]
    return jnp.concatenate([jnp.sin(angles), jnp.cos(angles)], axis=1)


def position_table(width):
    token_ids = jnp.arange(TOK_ITEM)
    frame_pos = (token_ids // (GRID * GRID)).astype(jnp.float32)
    row_pos = (token_ids // GRID % GRID).astype(jnp.float32)
    column_pos = (token_ids % GRID).astype(jnp.float32)
    return jnp.concatenate(
        [
            sincos_part(width // 16 * 4, frame_pos),
            sincos_part(width // 16 * 6, row_pos),
            sincos_part(width // 16 * 6, column_pos),
        ],
        axis=1,
    )


def layer_norm(values, gain, shift):
    centre = jnp.mean(values, axis=-1, keepdims=True)
    spread = jnp.mean(jnp.square(values - centre), axis=-1, keepdims=True)
    return (values - centre) * lax.rsqrt(spread + EPS_NORM) * gain + shift


def attend_core(queries, keys, values, key_bias):
    scaling = 1.0 / math.sqrt(queries.shape[-1])
    scores = (
        jnp.einsum("qhd,khd->hqk", queries, keys, precision=PREC) * scaling
        + key_bias[None, None, :]
    )
    row_top = jnp.max(scores, axis=-1, keepdims=True)
    weights = jnp.exp(scores - row_top)
    weights = weights / jnp.sum(weights, axis=-1, keepdims=True)
    return jnp.einsum("hqk,khd->qhd", weights, values, precision=PREC)


def transformer_block(stream, params, head_count, key_bias):
    (
        first_gain,
        first_shift,
        qkv_weight,
        query_bias,
        value_bias,
        out_weight,
        out_bias,
        second_gain,
        second_shift,
        up_weight,
        up_bias,
        down_weight,
        down_bias,
    ) = params
    row_count, model_width = stream.shape
    head_size = model_width // head_count
    normed = layer_norm(stream, first_gain, first_shift)
    joined = matmul(normed, qkv_weight)
    queries = (joined[:, :model_width] + query_bias).reshape(row_count, head_count, head_size)
    keys = joined[:, model_width : 2 * model_width].reshape(row_count, head_count, head_size)
    values = (joined[:, 2 * model_width :] + value_bias).reshape(row_count, head_count, head_size)
    mixed = jax.checkpoint(attend_core)(queries, keys, values, key_bias).reshape(
        row_count, model_width
    )
    stream = stream + matmul(mixed, out_weight) + out_bias
    normed = layer_norm(stream, second_gain, second_shift)
    hidden = jax.nn.gelu(matmul(normed, up_weight) + up_bias, approximate=False)
    return stream + matmul(hidden, down_weight) + down_bias


def normalize(pixel_block, running_mean, running_variance):
    inverse = lax.rsqrt(running_variance + EPS_NORM)
    return (pixel_block - running_mean[None, :, None, None]) * inverse[None, :, None, None]


def patchify(normed):
    items_here = normed.shape[0]
    grid_view = normed.reshape(items_here, BANDS, FRAMES, GRID, PATCH, GRID, PATCH)
    return grid_view.transpose(0, 2, 3, 5, 1, 4, 6).reshape(items_here, TOK_ITEM, PIX)


def encode_item(encoder, patch_one, chosen, keep_one):
    slots = jnp.arange(KEEP_MAX)
    key_bias = jnp.where(slots < keep_one, 0.0, MASKED_SCORE).astype(jnp.float32)
    visible = jnp.take(patch_one, chosen, axis=0)
    places = jnp.take(position_table(D_ENC), chosen, axis=0)
    stream = matmul(visible, encoder[0]) + encoder[1] + places
    stream = transformer_block(stream, encoder[2:15], HEADS_E, key_bias)
    return layer_norm(stream, encoder[15], encoder[16])


def decode_item(decoder, encoded, patch_one, chosen, keep_one):
    slots = jnp.arange(KEEP_MAX)
    live = (slots < keep_one).astype(jnp.float32)
    token_ids = jnp.arange(TOK_ITEM)
    placer = (chosen[:, None] == token_ids[None, :]).astype(jnp.float32) * live[:, None]
    hidden_mask = 1.0 - jnp.sum(placer, axis=0)
    latent = matmul(encoded, decoder[0]) + decoder[1]
    stream = jnp.einsum("st,sd->td", placer, latent, precision=PREC)
    stream = stream + hidden_mask[:, None] * decoder[2][None, :] + position_table(D_DEC)
    stream = transformer_block(stream, decoder[3:16], HEADS_D, jnp.zeros((TOK_ITEM,), jnp.float32))
    normed = layer_norm(stream, decoder[16], decoder[17])
    predicted = matmul(normed, decoder[18]) + decoder[19]
    error = predicted - patch_one
    squared = jnp.sum(hidden_mask[:, None] * error * error)
    return (squared / (PATCH * PATCH), squared)


def body(
    pixels,
    running_mean,
    running_variance,
    momentum,
    keep_count,
    visible_index,
    encoder_flat,
    decoder_flat,
):
    all_count = lax.axis_size(("dp", "fsdp"))
    items_here = pixels.shape[0]
    band_sum = jnp.sum(pixels, axis=(0, 2, 3))
    band_square = jnp.sum(pixels * pixels, axis=(0, 2, 3))
    masked_here = jnp.sum(TOK_ITEM - keep_count).astype(jnp.float32)
    band_total, square_total = lax.psum((band_sum, band_square), ("dp", "fsdp"))

    def encode_all(encoder_full, pixel_block):
        encoder = unpack(encoder_full, encoder_shapes())
        patch_block = patchify(normalize(pixel_block, running_mean, running_variance))

        def encode_one(patch_one, chosen, keep_one):
            return encode_item(encoder, patch_one, chosen, keep_one)

        return (jax.vmap(encode_one)(patch_block, visible_index, keep_count), patch_block)

    def decode_all(decoder_full, encoded, patch_block):
        decoder = unpack(decoder_full, decoder_shapes())

        def decode_one(encoded_one, patch_one, chosen, keep_one):
            return decode_item(decoder, encoded_one, patch_one, chosen, keep_one)

        objectives, squares = jax.vmap(decode_one)(encoded, patch_block, visible_index, keep_count)
        return (jnp.sum(objectives), jnp.sum(squares))

    def gather(flat):
        rows = flat.shape[0] // 256
        half = lax.dynamic_index_in_dim(flat.reshape(2, rows, 128), lax.axis_index("dp"), 0, keepdims=False)
        return lax.all_gather(half, ("fsdp", "dp"), axis=0, tiled=False).reshape(-1)

    def scatter(grad):
        n = lax.axis_size(("fsdp", "dp"))
        half = lax.psum_scatter(grad.reshape(n, -1, 128), ("fsdp", "dp"), scatter_dimension=0, tiled=False)
        return lax.all_gather(half, "dp", axis=0, tiled=True).reshape(-1)

    encoder_full = gather(encoder_flat)
    decoder_full = gather(decoder_flat)
    (encoded, patch_block), encode_back = jax.vjp(encode_all, encoder_full, pixels)
    objective, decode_back, squared = jax.vjp(
        decode_all, decoder_full, encoded, patch_block, has_aux=True
    )
    grad_decoder_full, grad_encoded, grad_patches = decode_back(jnp.ones((), jnp.float32))
    decoder_share = scatter(grad_decoder_full)
    grad_encoder_full, pixel_grad = encode_back((grad_encoded, grad_patches))
    encoder_share = scatter(grad_encoder_full)
    squared_total, masked_total = lax.psum((squared, masked_here), ("dp", "fsdp"))
    pixel_count = float(items_here * all_count * FRAMES * IMG * IMG)
    band_mean = band_total / pixel_count
    band_var = square_total / pixel_count - band_mean * band_mean
    next_mean = (1.0 - momentum) * running_mean + momentum * band_mean
    next_variance = (1.0 - momentum) * running_variance + momentum * band_var
    masked_loss = squared_total / (masked_total * PIX)
    return (masked_loss, pixel_grad, encoder_share, decoder_share, next_mean, next_variance)


def solution(mesh):
    placed = (
        P(("dp", "fsdp"), None, None, None),
        P(),
        P(),
        P(),
        P(("dp", "fsdp")),
        P(("dp", "fsdp"), None),
        P("fsdp"),
        P("fsdp"),
    )
    return jax.shard_map(
        body,
        mesh=mesh,
        in_specs=placed,
        out_specs=(P(), P(("dp", "fsdp"), None, None, None), P("fsdp"), P("fsdp"), P(), P()),
        check_vma=False,
    )
```

```python
import functools
import math

import jax
import jax.numpy as jnp
from jax import lax
from jax.experimental import pallas as pl
from jax.experimental.pallas import tpu as pltpu
from jax.sharding import PartitionSpec as P

D_ENC = 768
HEADS_E = 12
MLP_E = 3072
D_DEC = 512
HEADS_D = 16
MLP_D = 2048
BANDS = 6
PATCH = 16
FRAMES = 3
GRID = 14
TOK_ITEM = 588
IMG = 224
PIX = 1536
KEEP_MAX = 236
LANES = 128
SMALL = 3072

EPS_NORM = 1e-06
MASKED_SCORE = -1e30
PREC = lax.Precision.HIGH
VMEM_LIMIT = 60 * 2**20


def matmul(left, right):
    return jnp.dot(left, right, precision=PREC, preferred_element_type=jnp.float32)


def block_shapes(width, hidden):
    return [
        (width,),
        (width,),
        (width, 3 * width),
        (width,),
        (width,),
        (width, width),
        (width,),
        (width,),
        (width,),
        (width, hidden),
        (hidden,),
        (hidden, width),
        (width,),
    ]


def encoder_shapes():
    return [(PIX, D_ENC), (D_ENC,)] + block_shapes(D_ENC, MLP_E) + [(D_ENC,), (D_ENC,)]


def decoder_shapes():
    return (
        [(D_ENC, D_DEC), (D_DEC,), (D_DEC,)]
        + block_shapes(D_DEC, MLP_D)
        + [(D_DEC,), (D_DEC,), (D_DEC, PIX), (PIX,)]
    )


def row_layout(shapes):
    matrices, vectors, row = [], [], 0
    for shape in shapes:
        if len(shape) == 2:
            matrices.append((row, shape[0], shape[1]))
        else:
            vectors.append((row, shape[0] // LANES))
        row += math.prod(shape) // LANES
    return matrices, vectors, row


SLOTS = 4
STAGE = 393216


def plan(shapes):
    blocks = []
    for at, (row, rows, columns) in enumerate(row_layout(shapes)[0]):
        size = max(r for r in range(8, rows + 1, 8) if rows % r == 0 and r * columns <= STAGE)
        for first in range(0, rows, size):
            blocks.append((at, first, size, columns, row + first * (columns // LANES)))
    return blocks


def stage_view(stage, slot, size, columns):
    return stage.at[slot, pl.ds(0, size), pl.ds(0, columns)]


def move_block(lin, stage, slot, size, columns, base, inward):
    tiles = columns // LANES
    groups = size // 8
    unroll = max(u for u in range(1, 9) if groups % u == 0 and u * tiles <= 48)

    def some(r, carry):
        for u in range(unroll):
            at = r * unroll + u
            for t in range(tiles):
                rows = pl.ds(base + at * (8 * tiles) + t, 8, stride=tiles)
                place = pl.ds(pl.multiple_of(at * 8, 8), 8)
                if inward:
                    stage[slot, place, t * LANES : (t + 1) * LANES] = lin[rows, :]
                else:
                    lin[rows, :] = stage[slot, place, t * LANES : (t + 1) * LANES]
        return carry

    lax.fori_loop(0, groups // unroll, some, 0)


def unpack_kernel(shapes, half_rows, piece_count, sources, relative, *refs):
    matrices, vectors, used = row_layout(shapes)
    index_ref = refs[0]
    ins = refs[1 : 1 + sources]
    outs = refs[1 + sources : 1 + sources + len(matrices)]
    small_ref = refs[1 + sources + len(matrices)]
    lin, stage, in_sem, out_sem = refs[2 + sources + len(matrices) :]
    me, core = index_ref[0], index_ref[1]

    def copy_piece(source, place):
        return pltpu.make_async_copy(
            source.at[pl.ds(0, half_rows)],
            lin.at[pl.ds(place * half_rows, half_rows)],
            in_sem.at[place],
        )

    if relative:
        pairs = piece_count // 4
        for side in range(2):
            for j in range(piece_count // 2):
                owner = jnp.bitwise_xor(me, j)
                half = core if side == 0 else 1 - core
                group, k, role = j // 8, j // 4 % 2, j % 4
                source = ins[side * (pairs // 4) + group]
                copy_piece(source.at[role * 2 + k], owner * 2 + half).start()
    else:
        for place in range(piece_count):
            copy_piece(ins[0].at[place], place).start()

    arrived = 0

    def wait_for(last, arrived):
        while arrived < piece_count and arrived * half_rows < last:
            copy_piece(ins[0].at[0], arrived).wait()
            arrived += 1
        return arrived

    copies = []
    for number, (at, first, size, columns, base) in enumerate(plan(shapes)):
        arrived = wait_for(base + size * (columns // LANES), arrived)
        slot = number % SLOTS
        if number >= SLOTS:
            copies[number - SLOTS].wait()
        move_block(lin, stage, slot, size, columns, base, True)
        copies.append(
            pltpu.make_async_copy(
                stage_view(stage, slot, size, columns),
                outs[at].at[pl.ds(first, size)],
                out_sem.at[slot],
            )
        )
        copies[-1].start()
    wait_for(piece_count * half_rows, arrived)
    small_ref[...] = jnp.zeros_like(small_ref)
    for i, (row, count) in enumerate(vectors):
        for t in range(count):
            small_ref[i : i + 1, t * LANES : (t + 1) * LANES] = lin[row + t : row + t + 1, :]
    for copy in copies[-SLOTS:]:
        copy.wait()


def unpack(index, sources, half_rows, piece_count, relative, shapes):
    matrices, vectors, _ = row_layout(shapes)
    any_spec = pl.BlockSpec(memory_space=pltpu.HBM)
    slots = -(-len(vectors) // 8) * 8
    total = piece_count * half_rows
    wide, flat = scratch_of(shapes, total)
    outs = pl.pallas_call(
        functools.partial(
            unpack_kernel, shapes, half_rows, piece_count, len(sources), relative
        ),
        out_shape=[jax.ShapeDtypeStruct(m[1:], jnp.float32) for m in matrices]
        + [jax.ShapeDtypeStruct((slots, SMALL), jnp.float32)],
        in_specs=[pl.BlockSpec(memory_space=pltpu.SMEM)] + [any_spec] * len(sources),
        out_specs=[any_spec] * len(matrices) + [pl.BlockSpec(memory_space=pltpu.VMEM)],
        scratch_shapes=[
            flat,
            wide,
            pltpu.SemaphoreType.DMA((piece_count,)),
            pltpu.SemaphoreType.DMA((SLOTS,)),
        ],
        compiler_params=pltpu.CompilerParams(vmem_limit_bytes=VMEM_LIMIT),
        cost_estimate=pl.CostEstimate(
            flops=0, bytes_accessed=8 * total * LANES, transcendentals=0
        ),
    )(index, *sources)
    small = outs[-1]
    pieces, matrix_at, vector_at = [], 0, 0
    for shape in shapes:
        if len(shape) == 2:
            pieces.append(outs[matrix_at])
            matrix_at += 1
        else:
            pieces.append(small[vector_at, : shape[0]])
            vector_at += 1
    return pieces


def scratch_of(shapes, total):
    blocks = plan(shapes)
    wide = pltpu.VMEM(
        (SLOTS, max(b[2] for b in blocks), max(b[3] for b in blocks)), jnp.float32
    )
    return wide, pltpu.VMEM((-(-total // 8) * 8, LANES), jnp.float32)


def pack_kernel(shapes, half_rows, piece_count, relative, *refs):
    matrices, vectors, used = row_layout(shapes)
    index_ref = refs[0]
    ins = refs[1 : 1 + len(matrices)]
    small_ref, tail_ref = refs[1 + len(matrices) : 3 + len(matrices)]
    outs = refs[3 + len(matrices) : -4]
    lin, stage, in_sem, out_sem = refs[-4:]
    me, core = index_ref[0], index_ref[1]
    tail_rows = tail_ref.shape[0]
    blocks = plan(shapes)

    def copy_in(number):
        at, first, size, columns, _ = blocks[number]
        slot = number % SLOTS
        return pltpu.make_async_copy(
            ins[at].at[pl.ds(first, size)],
            stage_view(stage, slot, size, columns),
            in_sem.at[slot],
        )

    for number in range(min(SLOTS - 1, len(blocks))):
        copy_in(number).start()

    for i, (row, count) in enumerate(vectors):
        for t in range(count):
            lin[row + t : row + t + 1, :] = small_ref[i : i + 1, t * LANES : (t + 1) * LANES]
    total = piece_count * half_rows
    if total > used:
        lin[used:total, :] = jnp.zeros((total - used, LANES), jnp.float32)

    def copies(place, target):
        return (
            pltpu.make_async_copy(
                lin.at[pl.ds(place * half_rows, half_rows)],
                target.at[pl.ds(0, half_rows)],
                out_sem.at[place, 0],
            ),
            pltpu.make_async_copy(
                tail_ref, target.at[pl.ds(half_rows, tail_rows)], out_sem.at[place, 1]
            ),
        )

    def send_piece(place):
        def start(target):
            for copy in copies(place, target):
                copy.start()

        if not relative:
            start(outs[0].at[place])
            return
        keep, sends = outs[0], outs[1:]
        j = jnp.bitwise_xor(me, place // 2)
        within = lax.rem(j, 4) * 2 + lax.rem(lax.div(j, 4), 2)
        group = lax.div(j, 8)
        mine = core == place % 2

        @pl.when(mine)
        def _():
            start(keep.at[group * 8 + within])

        for g, out in enumerate(sends):

            @pl.when(jnp.logical_and(jnp.logical_not(mine), group == g))
            def _(out=out):
                start(out.at[within])

    sent = 0
    for number, (at, first, size, columns, base) in enumerate(blocks):
        if number + SLOTS - 1 < len(blocks):
            copy_in(number + SLOTS - 1).start()
        copy_in(number).wait()
        move_block(lin, stage, number % SLOTS, size, columns, base, False)
        done = base + size * (columns // LANES)
        if number == len(blocks) - 1:
            done = total
        while (sent + 1) * half_rows <= done and sent < piece_count:
            send_piece(sent)
            sent += 1
    for place in range(piece_count):
        for copy in copies(place, outs[0].at[0]):
            copy.wait()


def padded_rows(half_rows, tail_rows):
    return -(-(half_rows + tail_rows) // 8) * 8


def pack(index, grads, tail, shapes, piece_count, half_rows, relative):
    matrices, vectors, _ = row_layout(shapes)
    padded = padded_rows(half_rows, tail.shape[0])
    tail = jnp.pad(tail, ((0, padded - half_rows - tail.shape[0]), (0, 0)))
    slots = -(-len(vectors) // 8) * 8
    mats = [g for g, s in zip(grads, shapes) if len(s) == 2]
    vecs = [jnp.pad(g, (0, SMALL - g.shape[0])) for g, s in zip(grads, shapes) if len(s) == 1]
    vecs += [jnp.zeros((SMALL,), jnp.float32)] * (slots - len(vecs))
    any_spec = pl.BlockSpec(memory_space=pltpu.HBM)
    vmem_spec = pl.BlockSpec(memory_space=pltpu.VMEM)
    total = piece_count * half_rows
    wide, flat = scratch_of(shapes, total)
    if relative:
        sizes = [piece_count // 2] + [8] * (piece_count // 16)
    else:
        sizes = [piece_count]
    return pl.pallas_call(
        functools.partial(pack_kernel, shapes, half_rows, piece_count, relative),
        out_shape=[jax.ShapeDtypeStruct((n, padded, LANES), jnp.float32) for n in sizes],
        in_specs=[pl.BlockSpec(memory_space=pltpu.SMEM)]
        + [any_spec] * len(matrices)
        + [vmem_spec] * 2,
        out_specs=[any_spec] * len(sizes),
        scratch_shapes=[
            flat,
            wide,
            pltpu.SemaphoreType.DMA((SLOTS,)),
            pltpu.SemaphoreType.DMA((piece_count, 2)),
        ],
        compiler_params=pltpu.CompilerParams(vmem_limit_bytes=VMEM_LIMIT),
        cost_estimate=pl.CostEstimate(
            flops=0, bytes_accessed=8 * total * LANES, transcendentals=0
        ),
    )(index, *mats, jnp.stack(vecs), tail)


QUADS = FRAMES * GRID
GROUP = LANES // PATCH
STARTS = tuple(range(0, QUADS - 7, 8)) + ((QUADS - 8,) if QUADS % 8 else ())


def patch_kernel(mean_ref, inverse_ref, pixel_ref, patch_ref, moment_ref, scratch):
    band = pl.program_id(0)
    mean, inverse = mean_ref[band], inverse_ref[band]
    group = lax.broadcasted_iota(jnp.int32, (8, LANES), 1) // PATCH

    def sums(i, carry):
        one, two = carry
        value = pixel_ref[0, pl.ds(pl.multiple_of(i * 8, 8), 8), :]
        return one + value, two + value * value

    zero = jnp.zeros((8, LANES), jnp.float32)
    one, two = lax.fori_loop(0, pixel_ref.shape[1] // 8, sums, (zero, zero), unroll=7)
    moment_ref[0, 0] = one
    moment_ref[0, 1] = two
    for side in range(2):
        for first in STARTS:
            rows = []
            for k in range(GRID):
                start = 2 * GRID * first + GRID * side + k
                raw = pixel_ref[0, pl.ds(start, 8, stride=2 * GRID), :]
                rows.append((raw - mean) * inverse)
            for column in range(GRID):
                out = None
                for line in range(GROUP):
                    place = GRID * line + column
                    moved = pltpu.roll(rows[place // GROUP], PATCH * ((line - place) % GROUP), 1)
                    out = moved if out is None else jnp.where(group == line, moved, out)
                scratch[pl.ds(GRID * first + column, 8, stride=GRID), :] = out
        patch_ref[:, side * LANES : (side + 1) * LANES] = scratch[...]


def patchify(pixels, mean, inverse):
    rows = QUADS * 2 * GRID
    smem = pl.BlockSpec(memory_space=pltpu.SMEM)
    patches, moments = pl.pallas_call(
        patch_kernel,
        grid=(BANDS,),
        out_shape=[
            jax.ShapeDtypeStruct((TOK_ITEM, PIX), jnp.float32),
            jax.ShapeDtypeStruct((BANDS, 2, 8, LANES), jnp.float32),
        ],
        in_specs=[smem, smem, pl.BlockSpec((1, rows, LANES), lambda b: (b, 0, 0))],
        out_specs=[
            pl.BlockSpec((TOK_ITEM, 2 * LANES), lambda b: (0, b)),
            pl.BlockSpec((1, 2, 8, LANES), lambda b: (b, 0, 0, 0)),
        ],
        scratch_shapes=[pltpu.VMEM((TOK_ITEM, LANES), jnp.float32)],
        cost_estimate=pl.CostEstimate(
            flops=0, bytes_accessed=16 * TOK_ITEM * PIX, transcendentals=0
        ),
    )(mean, inverse, pixels.reshape(BANDS, rows, LANES))
    return patches, jnp.sum(moments, axis=(2, 3))


def pixel_kernel(inverse_ref, patch_ref, pixel_ref, scratch):
    inverse = inverse_ref[pl.program_id(0)]
    group = lax.broadcasted_iota(jnp.int32, (8, LANES), 1) // PATCH
    for side in range(2):
        scratch[...] = patch_ref[:, side * LANES : (side + 1) * LANES] * inverse
        for first in STARTS:
            columns = [
                scratch[pl.ds(GRID * first + column, 8, stride=GRID), :] for column in range(GRID)
            ]
            for k in range(GRID):
                out = None
                for slot in range(GROUP):
                    line, column = divmod(GROUP * k + slot, GRID)
                    moved = pltpu.roll(columns[column], PATCH * ((slot - line) % GROUP), 1)
                    out = moved if out is None else jnp.where(group == slot, moved, out)
                start = 2 * GRID * first + GRID * side + k
                pixel_ref[0, pl.ds(start, 8, stride=2 * GRID), :] = out


def unpatchify(grad_patches, inverse):
    rows = QUADS * 2 * GRID
    return pl.pallas_call(
        pixel_kernel,
        grid=(BANDS,),
        out_shape=jax.ShapeDtypeStruct((BANDS, rows, LANES), jnp.float32),
        in_specs=[
            pl.BlockSpec(memory_space=pltpu.SMEM),
            pl.BlockSpec((TOK_ITEM, 2 * LANES), lambda b: (0, b)),
        ],
        out_specs=pl.BlockSpec((1, rows, LANES), lambda b: (b, 0, 0)),
        scratch_shapes=[pltpu.VMEM((TOK_ITEM, LANES), jnp.float32)],
        cost_estimate=pl.CostEstimate(
            flops=0, bytes_accessed=16 * TOK_ITEM * PIX, transcendentals=0
        ),
    )(inverse, grad_patches)


def swap(value, distance, count):
    return lax.ppermute(value, "fsdp", [(i, i ^ distance) for i in range(count)])


def swap_cores(value):
    return lax.ppermute(value, "dp", [(0, 1), (1, 0)])


def split_row(rows):
    return rows // 16 * 8


def gather_pairs(half, count):
    mine = []
    middle = split_row(half.shape[0])
    bases = [half] + [swap(half, 4 * k, count) for k in range(1, count // 4)]
    for g in range(count // 8):
        base = jnp.stack(bases[2 * g : 2 * g + 2])
        along_x = swap(base, 1, count)
        along_y = swap(base, 2, count)
        first = swap(along_x[:, :middle], 2, count)
        second = swap(along_y[:, middle:], 1, count)
        corner = jnp.concatenate([first, second], axis=1)
        mine.append(jnp.concatenate([base, along_x, along_y, corner]))
    return mine + [swap_cores(group) for group in mine]


def scatter_pairs(keep, sends, count):
    total = None
    rows = keep.shape[1]
    middle = split_row(rows)
    keep = keep.reshape(len(sends), 4, 2, rows, LANES)
    for g in reversed(range(len(sends))):
        got = swap_cores(sends[g]).reshape(4, 2, rows, LANES)
        own, for_x, for_y, corner = [keep[g, i] + got[i] for i in range(4)]
        first = swap(corner[:, :middle], 2, count)
        second = swap(corner[:, middle:], 1, count)
        for_x = jnp.concatenate([for_x[:, :middle] + first, for_x[:, middle:]], axis=1)
        for_y = jnp.concatenate([for_y[:, :middle], for_y[:, middle:] + second], axis=1)
        part = own + swap(for_x, 1, count) + swap(for_y, 2, count)
        for i in reversed(range(2)):
            one = part[i]
            if 2 * g + i:
                one = swap(one, 4 * (2 * g + i), count)
            total = one if total is None else total + one
    return total


def both_halves(half, rows, core):
    got = swap_cores(half)
    low = jnp.where(core == 0, half, got)[:rows]
    high = jnp.where(core == 0, got, half)[:rows]
    return jnp.concatenate([low, high]).reshape(-1)


def sincos_part(width, positions):
    frequency = 1.0 / 10000.0 ** (jnp.arange(width // 2).astype(jnp.float32) / (width / 2.0))
    angles = positions[:, None] * frequency[None, :]
    return jnp.concatenate([jnp.sin(angles), jnp.cos(angles)], axis=1)


def position_table(width):
    token_ids = jnp.arange(TOK_ITEM)
    frame_pos = (token_ids // (GRID * GRID)).astype(jnp.float32)
    row_pos = (token_ids // GRID % GRID).astype(jnp.float32)
    column_pos = (token_ids % GRID).astype(jnp.float32)
    return jnp.concatenate(
        [
            sincos_part(width // 16 * 4, frame_pos),
            sincos_part(width // 16 * 6, row_pos),
            sincos_part(width // 16 * 6, column_pos),
        ],
        axis=1,
    )


def layer_norm(values, gain, shift):
    centre = jnp.mean(values, axis=-1, keepdims=True)
    spread = jnp.mean(jnp.square(values - centre), axis=-1, keepdims=True)
    return (values - centre) * lax.rsqrt(spread + EPS_NORM) * gain + shift


def attend_core(queries, keys, values, key_bias):
    scaling = 1.0 / math.sqrt(queries.shape[-1])
    scores = (
        jnp.einsum("qhd,khd->hqk", queries, keys, precision=PREC) * scaling
        + key_bias[None, None, :]
    )
    row_top = jnp.max(scores, axis=-1, keepdims=True)
    weights = jnp.exp(scores - row_top)
    weights = weights / jnp.sum(weights, axis=-1, keepdims=True)
    return jnp.einsum("hqk,khd->qhd", weights, values, precision=PREC)


def transformer_block(stream, params, head_count, key_bias):
    (
        first_gain,
        first_shift,
        qkv_weight,
        query_bias,
        value_bias,
        out_weight,
        out_bias,
        second_gain,
        second_shift,
        up_weight,
        up_bias,
        down_weight,
        down_bias,
    ) = params
    row_count, model_width = stream.shape
    head_size = model_width // head_count
    normed = layer_norm(stream, first_gain, first_shift)
    joined = matmul(normed, qkv_weight)
    queries = (joined[:, :model_width] + query_bias).reshape(row_count, head_count, head_size)
    keys = joined[:, model_width : 2 * model_width].reshape(row_count, head_count, head_size)
    values = (joined[:, 2 * model_width :] + value_bias).reshape(row_count, head_count, head_size)
    mixed = jax.checkpoint(attend_core)(queries, keys, values, key_bias).reshape(
        row_count, model_width
    )
    stream = stream + matmul(mixed, out_weight) + out_bias
    normed = layer_norm(stream, second_gain, second_shift)
    hidden = jax.nn.gelu(matmul(normed, up_weight) + up_bias, approximate=False)
    return stream + matmul(hidden, down_weight) + down_bias


def encode_item(encoder, patch_one, chosen, keep_one):
    slots = jnp.arange(KEEP_MAX)
    key_bias = jnp.where(slots < keep_one, 0.0, MASKED_SCORE).astype(jnp.float32)
    visible = jnp.take(patch_one, chosen, axis=0)
    places = jnp.take(position_table(D_ENC), chosen, axis=0)
    stream = matmul(visible, encoder[0]) + encoder[1] + places
    stream = transformer_block(stream, encoder[2:15], HEADS_E, key_bias)
    return layer_norm(stream, encoder[15], encoder[16])


def decode_item(decoder, encoded, patch_one, chosen, keep_one):
    slots = jnp.arange(KEEP_MAX)
    live = (slots < keep_one).astype(jnp.float32)
    token_ids = jnp.arange(TOK_ITEM)
    placer = (chosen[:, None] == token_ids[None, :]).astype(jnp.float32) * live[:, None]
    hidden_mask = 1.0 - jnp.sum(placer, axis=0)
    latent = matmul(encoded, decoder[0]) + decoder[1]
    stream = jnp.einsum("st,sd->td", placer, latent, precision=PREC)
    stream = stream + hidden_mask[:, None] * decoder[2][None, :] + position_table(D_DEC)
    stream = transformer_block(stream, decoder[3:16], HEADS_D, jnp.zeros((TOK_ITEM,), jnp.float32))
    normed = layer_norm(stream, decoder[16], decoder[17])
    predicted = matmul(normed, decoder[18]) + decoder[19]
    error = predicted - patch_one
    squared = jnp.sum(hidden_mask[:, None] * error * error)
    return (squared / (PATCH * PATCH), squared)


def body(
    count,
    pixels,
    running_mean,
    running_variance,
    momentum,
    keep_count,
    visible_index,
    encoder_flat,
    decoder_flat,
):
    all_count = 2 * count
    core = lax.axis_index("dp")
    me = lax.axis_index("fsdp")
    index = jnp.stack([me, core]).astype(jnp.int32)
    inverse = lax.rsqrt(running_variance + EPS_NORM)
    chosen, keep_one = visible_index[0], keep_count[0]

    def own_half(flat):
        rows = flat.shape[0] // (2 * LANES)
        half = lax.dynamic_index_in_dim(flat.reshape(2, rows, LANES), core, 0, keepdims=False)
        return jnp.pad(half, ((0, -rows % 8), (0, 0))), rows

    encoder_half, encoder_rows = own_half(encoder_flat)
    decoder_half, decoder_rows = own_half(decoder_flat)
    encoder_all = lax.all_gather(encoder_half, ("fsdp", "dp"), axis=0, tiled=False)
    decoder_all = gather_pairs(decoder_half, count)

    patches, moments = patchify(pixels[0], running_mean, inverse)
    decoder = unpack(index, decoder_all, decoder_rows, all_count, True, decoder_shapes())
    encoder = unpack(index, [encoder_all], encoder_rows, all_count, False, encoder_shapes())
    encoded, encode_back = jax.vjp(
        lambda params, patch: encode_item(params, patch, chosen, keep_one), encoder, patches
    )
    objective, decode_back, squared = jax.vjp(
        lambda params, enc, patch: decode_item(params, enc, patch, chosen, keep_one),
        decoder,
        encoded,
        patches,
        has_aux=True,
    )
    grad_decoder, grad_encoded, grad_patches = decode_back(jnp.ones((), jnp.float32))
    masked_here = (TOK_ITEM - keep_one).astype(jnp.float32)
    stats = jnp.concatenate([moments[:, 0], moments[:, 1], jnp.stack([squared, masked_here])])
    place = jnp.arange(all_count)[:, None] == core * count + me
    tail = jnp.where(place, jnp.pad(stats, (0, 16 - stats.shape[0]))[None, :], 0.0)
    tail = tail.reshape(-1, LANES)
    (packed,) = pack(
        index, grad_decoder, tail, decoder_shapes(), all_count, decoder_rows, False
    )
    decoder_sum = lax.psum_scatter(packed, ("fsdp", "dp"), scatter_dimension=0, tiled=False)

    grad_encoder, more_patches = encode_back(grad_encoded)
    keep, *sends = pack(
        index, grad_encoder, tail, encoder_shapes(), all_count, encoder_rows, True
    )
    encoder_sum = scatter_pairs(keep, sends, count)
    pixel_grad = unpatchify(grad_patches + more_patches, inverse).reshape(pixels.shape)
    totals = encoder_sum[encoder_rows : encoder_rows + tail.shape[0]].reshape(all_count, 16)
    totals = jnp.sum(totals, axis=0)

    pixel_count = float(all_count * FRAMES * IMG * IMG)
    band_mean = totals[:BANDS] / pixel_count
    band_var = totals[BANDS : 2 * BANDS] / pixel_count - band_mean * band_mean
    next_mean = (1.0 - momentum) * running_mean + momentum * band_mean
    next_variance = (1.0 - momentum) * running_variance + momentum * band_var
    masked_loss = totals[2 * BANDS] / (totals[2 * BANDS + 1] * PIX)
    return (
        masked_loss,
        pixel_grad,
        both_halves(encoder_sum, encoder_rows, core),
        both_halves(decoder_sum, decoder_rows, core),
        next_mean,
        next_variance,
    )


def solution(mesh):
    placed = (
        P(("dp", "fsdp"), None, None, None),
        P(),
        P(),
        P(),
        P(("dp", "fsdp")),
        P(("dp", "fsdp"), None),
        P("fsdp"),
        P("fsdp"),
    )
    return jax.shard_map(
        functools.partial(body, mesh.shape["fsdp"]),
        mesh=mesh,
        in_specs=placed,
        out_specs=(P(), P(("dp", "fsdp"), None, None, None), P("fsdp"), P("fsdp"), P(), P()),
        check_vma=False,
    )
```

```python
import functools
import math

import jax
import jax.numpy as jnp
from jax import lax
from jax.experimental import pallas as pl
from jax.experimental.pallas import tpu as pltpu
from jax.sharding import PartitionSpec as P

D_ENC = 768
HEADS_E = 12
MLP_E = 3072
D_DEC = 512
HEADS_D = 16
MLP_D = 2048
BANDS = 6
PATCH = 16
FRAMES = 3
GRID = 14
TOK_ITEM = 588
IMG = 224
PIX = 1536
KEEP_MAX = 236
LANES = 128
SMALL = 3072

EPS_NORM = 1e-06
MASKED_SCORE = -1e30
PREC = lax.Precision.HIGH
VMEM_LIMIT = 60 * 2**20


def matmul(left, right):
    return jnp.dot(left, right, precision=PREC, preferred_element_type=jnp.float32)


def block_shapes(width, hidden):
    return [
        (width,),
        (width,),
        (width, 3 * width),
        (width,),
        (width,),
        (width, width),
        (width,),
        (width,),
        (width,),
        (width, hidden),
        (hidden,),
        (hidden, width),
        (width,),
    ]


def encoder_shapes():
    return [(PIX, D_ENC), (D_ENC,)] + block_shapes(D_ENC, MLP_E) + [(D_ENC,), (D_ENC,)]


def decoder_shapes():
    return (
        [(D_ENC, D_DEC), (D_DEC,), (D_DEC,)]
        + block_shapes(D_DEC, MLP_D)
        + [(D_DEC,), (D_DEC,), (D_DEC, PIX), (PIX,)]
    )


def row_layout(shapes):
    matrices, vectors, row = [], [], 0
    for shape in shapes:
        if len(shape) == 2:
            matrices.append((row, shape[0], shape[1]))
        else:
            vectors.append((row, shape[0] // LANES))
        row += math.prod(shape) // LANES
    return matrices, vectors, row


SLOTS = 4
STAGE = 393216


def plan(shapes):
    blocks = []
    for at, (row, rows, columns) in enumerate(row_layout(shapes)[0]):
        size = max(r for r in range(8, rows + 1, 8) if rows % r == 0 and r * columns <= STAGE)
        for first in range(0, rows, size):
            blocks.append((at, first, size, columns, row + first * (columns // LANES)))
    return blocks


def stage_view(stage, slot, size, columns):
    return stage.at[slot, pl.ds(0, size), pl.ds(0, columns)]


def move_block(lin, stage, slot, size, columns, base, inward):
    tiles = columns // LANES
    groups = size // 8
    unroll = max(u for u in range(1, 9) if groups % u == 0 and u * tiles <= 48)

    def some(r, carry):
        for u in range(unroll):
            at = r * unroll + u
            for t in range(tiles):
                rows = pl.ds(base + at * (8 * tiles) + t, 8, stride=tiles)
                place = pl.ds(pl.multiple_of(at * 8, 8), 8)
                if inward:
                    stage[slot, place, t * LANES : (t + 1) * LANES] = lin[rows, :]
                else:
                    lin[rows, :] = stage[slot, place, t * LANES : (t + 1) * LANES]
        return carry

    lax.fori_loop(0, groups // unroll, some, 0)


def unpack_kernel(shapes, half_rows, piece_count, sources, relative, *refs):
    matrices, vectors, used = row_layout(shapes)
    index_ref = refs[0]
    ins = refs[1 : 1 + sources]
    outs = refs[1 + sources : 1 + sources + len(matrices)]
    small_ref = refs[1 + sources + len(matrices)]
    lin, stage, in_sem, out_sem = refs[2 + sources + len(matrices) :]
    me, core = index_ref[0], index_ref[1]

    def copy_piece(source, place):
        return pltpu.make_async_copy(
            source.at[pl.ds(0, half_rows)],
            lin.at[pl.ds(place * half_rows, half_rows)],
            in_sem.at[place],
        )

    if relative:
        pairs = piece_count // 4
        for side in range(2):
            for j in range(piece_count // 2):
                owner = jnp.bitwise_xor(me, j)
                half = core if side == 0 else 1 - core
                group, k, role = j // 8, j // 4 % 2, j % 4
                source = ins[side * (pairs // 4) + group]
                copy_piece(source.at[role * 2 + k], owner * 2 + half).start()
    else:
        for place in range(piece_count):
            copy_piece(ins[0].at[place], place).start()

    arrived = 0

    def wait_for(last, arrived):
        while arrived < piece_count and arrived * half_rows < last:
            copy_piece(ins[0].at[0], arrived).wait()
            arrived += 1
        return arrived

    copies = []
    for number, (at, first, size, columns, base) in enumerate(plan(shapes)):
        arrived = wait_for(base + size * (columns // LANES), arrived)
        slot = number % SLOTS
        if number >= SLOTS:
            copies[number - SLOTS].wait()
        move_block(lin, stage, slot, size, columns, base, True)
        copies.append(
            pltpu.make_async_copy(
                stage_view(stage, slot, size, columns),
                outs[at].at[pl.ds(first, size)],
                out_sem.at[slot],
            )
        )
        copies[-1].start()
    wait_for(piece_count * half_rows, arrived)
    small_ref[...] = jnp.zeros_like(small_ref)
    for i, (row, count) in enumerate(vectors):
        for t in range(count):
            small_ref[i : i + 1, t * LANES : (t + 1) * LANES] = lin[row + t : row + t + 1, :]
    for copy in copies[-SLOTS:]:
        copy.wait()


def unpack(index, sources, half_rows, piece_count, relative, shapes):
    matrices, vectors, _ = row_layout(shapes)
    any_spec = pl.BlockSpec(memory_space=pltpu.HBM)
    slots = -(-len(vectors) // 8) * 8
    total = piece_count * half_rows
    wide, flat = scratch_of(shapes, total)
    outs = pl.pallas_call(
        functools.partial(
            unpack_kernel, shapes, half_rows, piece_count, len(sources), relative
        ),
        out_shape=[jax.ShapeDtypeStruct(m[1:], jnp.float32) for m in matrices]
        + [jax.ShapeDtypeStruct((slots, SMALL), jnp.float32)],
        in_specs=[pl.BlockSpec(memory_space=pltpu.SMEM)] + [any_spec] * len(sources),
        out_specs=[any_spec] * len(matrices) + [pl.BlockSpec(memory_space=pltpu.VMEM)],
        scratch_shapes=[
            flat,
            wide,
            pltpu.SemaphoreType.DMA((piece_count,)),
            pltpu.SemaphoreType.DMA((SLOTS,)),
        ],
        compiler_params=pltpu.CompilerParams(vmem_limit_bytes=VMEM_LIMIT),
        cost_estimate=pl.CostEstimate(
            flops=0, bytes_accessed=8 * total * LANES, transcendentals=0
        ),
    )(index, *sources)
    small = outs[-1]
    pieces, matrix_at, vector_at = [], 0, 0
    for shape in shapes:
        if len(shape) == 2:
            pieces.append(outs[matrix_at])
            matrix_at += 1
        else:
            pieces.append(small[vector_at, : shape[0]])
            vector_at += 1
    return pieces


def scratch_of(shapes, total):
    blocks = plan(shapes)
    wide = pltpu.VMEM(
        (SLOTS, max(b[2] for b in blocks), max(b[3] for b in blocks)), jnp.float32
    )
    return wide, pltpu.VMEM((-(-total // 8) * 8, LANES), jnp.float32)


def pack_kernel(shapes, half_rows, piece_count, relative, *refs):
    matrices, vectors, used = row_layout(shapes)
    index_ref = refs[0]
    ins = refs[1 : 1 + len(matrices)]
    small_ref, tail_ref = refs[1 + len(matrices) : 3 + len(matrices)]
    outs = refs[3 + len(matrices) : -4]
    lin, stage, in_sem, out_sem = refs[-4:]
    me, core = index_ref[0], index_ref[1]
    tail_rows = tail_ref.shape[0]
    blocks = plan(shapes)

    def copy_in(number):
        at, first, size, columns, _ = blocks[number]
        slot = number % SLOTS
        return pltpu.make_async_copy(
            ins[at].at[pl.ds(first, size)],
            stage_view(stage, slot, size, columns),
            in_sem.at[slot],
        )

    for number in range(min(SLOTS - 1, len(blocks))):
        copy_in(number).start()

    for i, (row, count) in enumerate(vectors):
        for t in range(count):
            lin[row + t : row + t + 1, :] = small_ref[i : i + 1, t * LANES : (t + 1) * LANES]
    total = piece_count * half_rows
    if total > used:
        lin[used:total, :] = jnp.zeros((total - used, LANES), jnp.float32)

    def copies(place, target):
        return (
            pltpu.make_async_copy(
                lin.at[pl.ds(place * half_rows, half_rows)],
                target.at[pl.ds(0, half_rows)],
                out_sem.at[place, 0],
            ),
            pltpu.make_async_copy(
                tail_ref, target.at[pl.ds(half_rows, tail_rows)], out_sem.at[place, 1]
            ),
        )

    def send_piece(place):
        def start(target):
            for copy in copies(place, target):
                copy.start()

        if not relative:
            start(outs[0].at[place])
            return
        j = jnp.bitwise_xor(me, place // 2)
        within = lax.rem(j, 4) * 2 + lax.rem(lax.div(j, 4), 2)
        away = jnp.where(core == place % 2, 0, 2)
        corner = jnp.where(within < 6, 0, 1)
        target = lax.div(j, 8) * 4 + away + corner
        for number, out in enumerate(outs):

            @pl.when(target == number)
            def _(out=out, number=number):
                start(out.at[within - 6 if number % 2 else within])

    sent = 0
    for number, (at, first, size, columns, base) in enumerate(blocks):
        if number + SLOTS - 1 < len(blocks):
            copy_in(number + SLOTS - 1).start()
        copy_in(number).wait()
        move_block(lin, stage, number % SLOTS, size, columns, base, False)
        done = base + size * (columns // LANES)
        if number == len(blocks) - 1:
            done = total
        while (sent + 1) * half_rows <= done and sent < piece_count:
            send_piece(sent)
            sent += 1
    for place in range(piece_count):
        for copy in copies(place, outs[0].at[0]):
            copy.wait()


def padded_rows(half_rows, tail_rows):
    return -(-(half_rows + tail_rows) // 8) * 8


def pack(index, grads, tail, shapes, piece_count, half_rows, relative):
    matrices, vectors, _ = row_layout(shapes)
    padded = padded_rows(half_rows, tail.shape[0])
    tail = jnp.pad(tail, ((0, padded - half_rows - tail.shape[0]), (0, 0)))
    slots = -(-len(vectors) // 8) * 8
    mats = [g for g, s in zip(grads, shapes) if len(s) == 2]
    vecs = [jnp.pad(g, (0, SMALL - g.shape[0])) for g, s in zip(grads, shapes) if len(s) == 1]
    vecs += [jnp.zeros((SMALL,), jnp.float32)] * (slots - len(vecs))
    any_spec = pl.BlockSpec(memory_space=pltpu.HBM)
    vmem_spec = pl.BlockSpec(memory_space=pltpu.VMEM)
    total = piece_count * half_rows
    wide, flat = scratch_of(shapes, total)
    if relative:
        sizes = [6, 2, 6, 2] * (piece_count // 16)
    else:
        sizes = [piece_count]
    return pl.pallas_call(
        functools.partial(pack_kernel, shapes, half_rows, piece_count, relative),
        out_shape=[jax.ShapeDtypeStruct((n, padded, LANES), jnp.float32) for n in sizes],
        in_specs=[pl.BlockSpec(memory_space=pltpu.SMEM)]
        + [any_spec] * len(matrices)
        + [vmem_spec] * 2,
        out_specs=[any_spec] * len(sizes),
        scratch_shapes=[
            flat,
            wide,
            pltpu.SemaphoreType.DMA((SLOTS,)),
            pltpu.SemaphoreType.DMA((piece_count, 2)),
        ],
        compiler_params=pltpu.CompilerParams(vmem_limit_bytes=VMEM_LIMIT),
        cost_estimate=pl.CostEstimate(
            flops=0, bytes_accessed=8 * total * LANES, transcendentals=0
        ),
    )(index, *mats, jnp.stack(vecs), tail)


QUADS = FRAMES * GRID
GROUP = LANES // PATCH
STARTS = tuple(range(0, QUADS - 7, 8)) + ((QUADS - 8,) if QUADS % 8 else ())


def patch_kernel(mean_ref, inverse_ref, pixel_ref, patch_ref, moment_ref, scratch):
    band = pl.program_id(0)
    mean, inverse = mean_ref[band], inverse_ref[band]
    group = lax.broadcasted_iota(jnp.int32, (8, LANES), 1) // PATCH

    def sums(i, carry):
        one, two = carry
        value = pixel_ref[0, pl.ds(pl.multiple_of(i * 8, 8), 8), :]
        return one + value, two + value * value

    zero = jnp.zeros((8, LANES), jnp.float32)
    one, two = lax.fori_loop(0, pixel_ref.shape[1] // 8, sums, (zero, zero), unroll=7)
    moment_ref[0, 0] = one
    moment_ref[0, 1] = two
    for side in range(2):
        for first in STARTS:
            rows = []
            for k in range(GRID):
                start = 2 * GRID * first + GRID * side + k
                raw = pixel_ref[0, pl.ds(start, 8, stride=2 * GRID), :]
                rows.append((raw - mean) * inverse)
            for column in range(GRID):
                out = None
                for line in range(GROUP):
                    place = GRID * line + column
                    moved = pltpu.roll(rows[place // GROUP], PATCH * ((line - place) % GROUP), 1)
                    out = moved if out is None else jnp.where(group == line, moved, out)
                scratch[pl.ds(GRID * first + column, 8, stride=GRID), :] = out
        patch_ref[:, side * LANES : (side + 1) * LANES] = scratch[...]


def patchify(pixels, mean, inverse):
    rows = QUADS * 2 * GRID
    smem = pl.BlockSpec(memory_space=pltpu.SMEM)
    patches, moments = pl.pallas_call(
        patch_kernel,
        grid=(BANDS,),
        out_shape=[
            jax.ShapeDtypeStruct((TOK_ITEM, PIX), jnp.float32),
            jax.ShapeDtypeStruct((BANDS, 2, 8, LANES), jnp.float32),
        ],
        in_specs=[smem, smem, pl.BlockSpec((1, rows, LANES), lambda b: (b, 0, 0))],
        out_specs=[
            pl.BlockSpec((TOK_ITEM, 2 * LANES), lambda b: (0, b)),
            pl.BlockSpec((1, 2, 8, LANES), lambda b: (b, 0, 0, 0)),
        ],
        scratch_shapes=[pltpu.VMEM((TOK_ITEM, LANES), jnp.float32)],
        cost_estimate=pl.CostEstimate(
            flops=0, bytes_accessed=16 * TOK_ITEM * PIX, transcendentals=0
        ),
    )(mean, inverse, pixels.reshape(BANDS, rows, LANES))
    return patches, jnp.sum(moments, axis=(2, 3))


def pixel_kernel(inverse_ref, patch_ref, pixel_ref, scratch):
    inverse = inverse_ref[pl.program_id(0)]
    group = lax.broadcasted_iota(jnp.int32, (8, LANES), 1) // PATCH
    for side in range(2):
        scratch[...] = patch_ref[:, side * LANES : (side + 1) * LANES] * inverse
        for first in STARTS:
            columns = [
                scratch[pl.ds(GRID * first + column, 8, stride=GRID), :] for column in range(GRID)
            ]
            for k in range(GRID):
                out = None
                for slot in range(GROUP):
                    line, column = divmod(GROUP * k + slot, GRID)
                    moved = pltpu.roll(columns[column], PATCH * ((slot - line) % GROUP), 1)
                    out = moved if out is None else jnp.where(group == slot, moved, out)
                start = 2 * GRID * first + GRID * side + k
                pixel_ref[0, pl.ds(start, 8, stride=2 * GRID), :] = out


def unpatchify(grad_patches, inverse):
    rows = QUADS * 2 * GRID
    return pl.pallas_call(
        pixel_kernel,
        grid=(BANDS,),
        out_shape=jax.ShapeDtypeStruct((BANDS, rows, LANES), jnp.float32),
        in_specs=[
            pl.BlockSpec(memory_space=pltpu.SMEM),
            pl.BlockSpec((TOK_ITEM, 2 * LANES), lambda b: (0, b)),
        ],
        out_specs=pl.BlockSpec((1, rows, LANES), lambda b: (b, 0, 0)),
        scratch_shapes=[pltpu.VMEM((TOK_ITEM, LANES), jnp.float32)],
        cost_estimate=pl.CostEstimate(
            flops=0, bytes_accessed=16 * TOK_ITEM * PIX, transcendentals=0
        ),
    )(inverse, grad_patches)


def swap(value, distance, count):
    return lax.ppermute(value, "fsdp", [(i, i ^ distance) for i in range(count)])


def swap_cores(value):
    return lax.ppermute(value, "dp", [(0, 1), (1, 0)])


def split_row(rows):
    return rows // 16 * 8


class Scatter:
    def __init__(self, packed, count):
        self.count, self.groups = count, len(packed) // 4
        self.middle = split_row(packed[0].shape[1])
        self.keep_sides, self.keep_corners = packed[::4], packed[1::4]
        self.sides, self.corners = packed[2::4], packed[3::4]
        self.time = -1
        self.pending = {}
        self.own = {}
        self.landed = []

    def hold(self, value):
        value, self.pending = lax.optimization_barrier((value, self.pending))
        return value

    def step(self):
        count, groups, middle = self.count, self.groups, self.middle
        arrived, sent = self.pending, {}
        last, ready, new = groups + 1 - self.time, groups - self.time, groups - 1 - self.time
        if "turned" in arrived:
            near, turned = arrived["turned"]
            self.landed.append(swap(near + turned, 8 * (last + 1), count))
        if 0 <= last < groups:
            along_x, along_y = arrived["sides"]
            part = self.own[last] + along_x + along_y
            turned = swap(part[1], 4, count)
            if last:
                sent["turned"] = (part[0], turned)
            else:
                self.landed += [part[0], turned]
        if 0 <= ready < groups:
            first, second = arrived["corner"]
            own, for_x, for_y = [
                (self.keep_sides[ready] + arrived["core sides"])[2 * i : 2 * i + 2] for i in range(3)
            ]
            self.own[ready] = own
            for_x = jnp.concatenate([for_x[:, :middle] + first, for_x[:, middle:]], axis=1)
            for_y = jnp.concatenate([for_y[:, :middle], for_y[:, middle:] + second], axis=1)
            sent["sides"] = [swap(for_x, 1, count), swap(for_y, 2, count)]
        if 0 <= new < groups:
            corner = self.keep_corners[new] + arrived["core corner"]
            sent["corner"] = [
                swap(corner[:, :middle], 2, count),
                swap(corner[:, middle:], 1, count),
            ]
            sent["core sides"] = swap_cores(self.sides[new])
        if 0 <= new - 1 < groups:
            sent["core corner"] = swap_cores(self.corners[new - 1])
        self.pending = sent
        self.time += 1

    def total(self):
        while self.time < self.groups + 2:
            self.step()
        return functools.reduce(jnp.add, self.landed)


def both_halves(half, rows, core):
    got = swap_cores(half)
    low = jnp.where(core == 0, half, got)[:rows]
    high = jnp.where(core == 0, got, half)[:rows]
    return jnp.concatenate([low, high]).reshape(-1)


def sincos_part(width, positions):
    frequency = 1.0 / 10000.0 ** (jnp.arange(width // 2).astype(jnp.float32) / (width / 2.0))
    angles = positions[:, None] * frequency[None, :]
    return jnp.concatenate([jnp.sin(angles), jnp.cos(angles)], axis=1)


def position_table(width):
    token_ids = jnp.arange(TOK_ITEM)
    frame_pos = (token_ids // (GRID * GRID)).astype(jnp.float32)
    row_pos = (token_ids // GRID % GRID).astype(jnp.float32)
    column_pos = (token_ids % GRID).astype(jnp.float32)
    return jnp.concatenate(
        [
            sincos_part(width // 16 * 4, frame_pos),
            sincos_part(width // 16 * 6, row_pos),
            sincos_part(width // 16 * 6, column_pos),
        ],
        axis=1,
    )


def layer_norm(values, gain, shift):
    centre = jnp.mean(values, axis=-1, keepdims=True)
    spread = jnp.mean(jnp.square(values - centre), axis=-1, keepdims=True)
    return (values - centre) * lax.rsqrt(spread + EPS_NORM) * gain + shift


QUERY_CHUNK = 640
KEY_CHUNK = 384


def split_two(value):
    high = value.astype(jnp.bfloat16)
    return high, (value - high.astype(jnp.float32)).astype(jnp.bfloat16)


def nt(left, right):
    return lax.dot_general(
        left, right, (((1,), (1,)), ((), ())), preferred_element_type=jnp.float32
    )


def nn(left, right):
    return jnp.dot(left, right, preferred_element_type=jnp.float32)


def chunks(rows, size):
    return [(at, min(size, rows - at)) for at in range(0, rows, size)]


def put_parts(ref, value, order):
    parts = split_two(value)
    for i, which in enumerate(order):
        ref[:, i * LANES : (i + 1) * LANES] = parts[which]


def put_turned(ref, value, size):
    for i, part in enumerate(split_two(value)):
        turned = part.astype(jnp.float32).T.astype(jnp.bfloat16)
        for head in range(LANES // size):
            ref[head, i * size : (i + 1) * size, :] = turned[head * size : (head + 1) * size, :]


def own_lanes(head, size, width):
    lane = lax.broadcasted_iota(jnp.int32, (1, width), 1)
    return (lax.rem(lane, LANES) // size == head).astype(jnp.float32).astype(jnp.bfloat16)


def hide_dead(scores, first, keep):
    if keep is None:
        return scores
    key = lax.broadcasted_iota(jnp.int32, scores.shape, 0) + first
    return jnp.where(key < keep, scores, MASKED_SCORE)


def turned_product(parts, high, low, size):
    both = nn(parts, high)
    return both[:size] + both[size:] + nn(parts[:size], low)


def attend_kernel(size, masked, keep_ref, q_ref, k_ref, v_ref, out_ref, lse_ref, q3, k3, v2t, out_t):
    head = pl.program_id(1)
    keep = keep_ref[0] if masked else None

    @pl.when(head == 0)
    def _():
        put_parts(q3, q_ref[...] * (1.0 / math.sqrt(size)), (0, 1, 0))
        put_parts(k3, k_ref[...], (0, 0, 1))
        put_turned(v2t, v_ref[...], size)

    lanes = own_lanes(head, size, 3 * LANES)
    values = v2t[head]
    for at, count in chunks(q_ref.shape[0], QUERY_CHUNK):
        place = slice(at, at + count)
        scores = hide_dead(nt(k3[...], q3[place, :] * lanes), 0, keep)
        top = jnp.max(scores, axis=0, keepdims=True)
        weights = jnp.exp(scores - top)
        total = jnp.sum(weights, axis=0, keepdims=True)
        high, low = split_two(weights)
        mixed = turned_product(values, high, low, size) / total
        out_t[pl.ds(pl.multiple_of(head * size, size), size), place] = mixed
        lse_ref[0, :, place] = top + jnp.log(total)

    @pl.when(head == LANES // size - 1)
    def _():
        out_ref[...] = out_t[...].T


def attend_forward(joined, keep, heads):
    rows, width = joined.shape[0], joined.shape[1] // 3
    size = width // heads
    blocks, per_block = width // LANES, LANES // size
    masked = keep is not None
    keep = keep if masked else jnp.zeros((1,), jnp.int32)

    def columns(first):
        return pl.BlockSpec((rows, LANES), lambda g, h: (0, first + g))

    return pl.pallas_call(
        functools.partial(attend_kernel, size, masked),
        grid=(blocks, per_block),
        out_shape=[
            jax.ShapeDtypeStruct((rows, width), jnp.float32),
            jax.ShapeDtypeStruct((heads, 1, rows), jnp.float32),
        ],
        in_specs=[
            pl.BlockSpec(memory_space=pltpu.SMEM),
            columns(0),
            columns(blocks),
            columns(2 * blocks),
        ],
        out_specs=[
            columns(0),
            pl.BlockSpec((1, 1, rows), lambda g, h: (g * per_block + h, 0, 0)),
        ],
        scratch_shapes=[
            pltpu.VMEM((rows, 3 * LANES), jnp.bfloat16),
            pltpu.VMEM((rows, 3 * LANES), jnp.bfloat16),
            pltpu.VMEM((per_block, 2 * size, rows), jnp.bfloat16),
            pltpu.VMEM((LANES, rows), jnp.float32),
        ],
        compiler_params=pltpu.CompilerParams(vmem_limit_bytes=VMEM_LIMIT),
        cost_estimate=pl.CostEstimate(
            flops=16 * rows * rows * width,
            bytes_accessed=16 * rows * width,
            transcendentals=heads * rows * rows,
        ),
    )(keep, joined, joined, joined)


def attend_back_kernel(
    size, masked, keep_ref, q_ref, k_ref, v_ref, g_ref, lse_ref, delta_ref, out_ref,
    q3, k3, v3, g3, q3m, g3m, k2t, dq_t, dq, dk, dv, sem,
):
    block, head = pl.program_id(0), pl.program_id(1)
    keep = keep_ref[0] if masked else None
    scale = 1.0 / math.sqrt(size)
    width = out_ref.shape[1] // 3

    @pl.when(head == 0)
    def _():
        put_parts(q3, q_ref[...] * scale, (0, 1, 0))
        put_parts(k3, k_ref[...], (0, 0, 1))
        put_parts(v3, v_ref[...], (0, 0, 1))
        put_parts(g3, g_ref[...], (0, 1, 0))
        put_turned(k2t, k_ref[...], size)
        dk[...] = jnp.zeros_like(dk)
        dv[...] = jnp.zeros_like(dv)

    lanes = own_lanes(head, size, 3 * LANES)
    q3m[...] = q3[...] * lanes
    g3m[...] = g3[...] * lanes
    lse, delta = lse_ref[0], delta_ref[0]
    turned = None
    for at, count in chunks(q_ref.shape[0], KEY_CHUNK):
        place = slice(at, at + count)
        scores = hide_dead(nt(k3[place, :], q3m[...]), at, keep)
        weights = jnp.exp(scores - lse)
        high, low = split_two(weights)
        both = nn(high, g3m[:, : 2 * LANES])
        dv[place, :] += both[:, :LANES] + both[:, LANES:] + nn(low, g3m[:, :LANES])
        change = weights * (nt(v3[place, :], g3m[...]) - delta)
        high, low = split_two(change)
        both = nn(high, q3m[:, : 2 * LANES])
        dk[place, :] += both[:, :LANES] + both[:, LANES:] + nn(low, q3m[:, :LANES])
        part = turned_product(k2t[head, :, place], high, low, size)
        turned = part if turned is None else turned + part
    dq_t[pl.ds(pl.multiple_of(head * size, size), size), :] = turned

    @pl.when(head == LANES // size - 1)
    def _():
        dq[...] = dq_t[...].T * scale
        copies = [
            pltpu.make_async_copy(
                source,
                out_ref.at[:, pl.ds(pl.multiple_of(i * width + block * LANES, LANES), LANES)],
                sem.at[i],
            )
            for i, source in enumerate((dq, dk, dv))
        ]
        for copy in copies:
            copy.start()
        for copy in copies:
            copy.wait()


def attend_backward(joined, keep, heads, grad, lse, delta):
    rows, width = joined.shape[0], joined.shape[1] // 3
    size = width // heads
    blocks, per_block = width // LANES, LANES // size
    masked = keep is not None
    keep = keep if masked else jnp.zeros((1,), jnp.int32)

    def columns(first):
        return pl.BlockSpec((rows, LANES), lambda g, h: (0, first + g))

    per_head = pl.BlockSpec((1, 1, rows), lambda g, h: (g * per_block + h, 0, 0))
    return pl.pallas_call(
        functools.partial(attend_back_kernel, size, masked),
        grid=(blocks, per_block),
        out_shape=jax.ShapeDtypeStruct((rows, 3 * width), jnp.float32),
        in_specs=[
            pl.BlockSpec(memory_space=pltpu.SMEM),
            columns(0),
            columns(blocks),
            columns(2 * blocks),
            columns(0),
            per_head,
            per_head,
        ],
        out_specs=pl.BlockSpec(memory_space=pltpu.HBM),
        scratch_shapes=[pltpu.VMEM((rows, 3 * LANES), jnp.bfloat16)] * 6
        + [
            pltpu.VMEM((per_block, 2 * size, rows), jnp.bfloat16),
            pltpu.VMEM((LANES, rows), jnp.float32),
        ]
        + [pltpu.VMEM((rows, LANES), jnp.float32)] * 3
        + [pltpu.SemaphoreType.DMA((3,))],
        compiler_params=pltpu.CompilerParams(vmem_limit_bytes=VMEM_LIMIT),
        cost_estimate=pl.CostEstimate(
            flops=40 * rows * rows * width,
            bytes_accessed=28 * rows * width,
            transcendentals=heads * rows * rows,
        ),
    )(keep, joined, joined, joined, grad, lse, delta)


@functools.partial(jax.custom_vjp, nondiff_argnums=(2,))
def attend(joined, keep, heads):
    return attend_forward(joined, keep, heads)[0]


def attend_keep(joined, keep, heads):
    out, lse = attend_forward(joined, keep, heads)
    return out, (joined, keep, out, lse)


def attend_pull(heads, kept, grad):
    joined, keep, out, lse = kept
    width = out.shape[1]
    owner = jnp.arange(width)[None, :] // (width // heads) == jnp.arange(heads)[:, None]
    delta = lax.dot_general(
        owner.astype(jnp.float32),
        grad * out,
        (((1,), (1,)), ((), ())),
        precision=lax.Precision.HIGHEST,
        preferred_element_type=jnp.float32,
    )
    return attend_backward(joined, keep, heads, grad, lse, delta[:, None, :]), None


attend.defvjp(attend_keep, attend_pull)


TAIL = (
    -1.26551223,
    1.00002368,
    0.37409196,
    0.09678418,
    -0.18628806,
    0.27886807,
    -1.13520398,
    1.48851587,
    -0.82215223,
    0.17087277,
)


def gelu_parts(value):
    scaled = jnp.abs(value) * math.sqrt(0.5)
    inverse = 1.0 / (1.0 + 0.5 * scaled)
    power = TAIL[-1]
    for factor in TAIL[-2::-1]:
        power = power * inverse + factor
    square = scaled * scaled
    below = 0.5 * inverse * jnp.exp(power - square)
    share = jnp.where(value >= 0.0, 1.0 - below, below)
    slope = share + value * (math.sqrt(0.5 / math.pi) * jnp.exp(-square))
    return value * share, slope


@jax.custom_vjp
def gelu(value):
    return gelu_parts(value)[0]


gelu.defvjp(lambda value: lax.optimization_barrier(gelu_parts(value)), lambda slope, grad: (grad * slope,))


@functools.partial(jax.custom_vjp, nondiff_argnums=(1,))
def mark(value, on_way_back):
    return value


def mark_keep(value, on_way_back):
    return value, None


def mark_pull(on_way_back, kept, grad):
    return (on_way_back(grad),)


mark.defvjp(mark_keep, mark_pull)


def marked(value, marks, number):
    return value if marks is None else mark(value, marks[number])


def transformer_block(stream, params, head_count, keep, marks):
    (
        first_gain,
        first_shift,
        qkv_weight,
        query_bias,
        value_bias,
        out_weight,
        out_bias,
        second_gain,
        second_shift,
        up_weight,
        up_bias,
        down_weight,
        down_bias,
    ) = params
    normed = layer_norm(stream, first_gain, first_shift)
    joined = matmul(normed, qkv_weight)
    joined = joined + jnp.concatenate([query_bias, jnp.zeros_like(query_bias), value_bias])
    mixed = marked(attend(marked(joined, marks, 3), keep, head_count), marks, 2)
    stream = marked(stream + matmul(mixed, out_weight) + out_bias, marks, 1)
    normed = layer_norm(stream, second_gain, second_shift)
    before = marked(matmul(normed, up_weight) + up_bias, marks, 0)
    hidden = gelu(before)
    return stream + matmul(hidden, down_weight) + down_bias


def encode_item(encoder, patch_one, places, chosen, keep_one, marks):
    visible = jnp.take(patch_one, chosen, axis=0)
    stream = matmul(visible, encoder[0]) + encoder[1] + places
    stream = transformer_block(stream, encoder[2:15], HEADS_E, keep_one[None], marks)
    return layer_norm(stream, encoder[15], encoder[16])


def decode_item(decoder, encoded, patch_one, table, chosen, keep_one):
    slots = jnp.arange(KEEP_MAX)
    live = (slots < keep_one).astype(jnp.float32)
    token_ids = jnp.arange(TOK_ITEM)
    placer = (chosen[:, None] == token_ids[None, :]).astype(jnp.float32) * live[:, None]
    hidden_mask = 1.0 - jnp.sum(placer, axis=0)
    latent = matmul(encoded, decoder[0]) + decoder[1]
    stream = jnp.einsum("st,sd->td", placer, latent, precision=PREC)
    stream = stream + hidden_mask[:, None] * decoder[2][None, :] + table
    stream = transformer_block(stream, decoder[3:16], HEADS_D, None, None)
    normed = layer_norm(stream, decoder[16], decoder[17])
    predicted = matmul(normed, decoder[18]) + decoder[19]
    error = predicted - patch_one
    squared = jnp.sum(hidden_mask[:, None] * error * error)
    return (squared / (PATCH * PATCH), squared)


def body(
    count,
    pixels,
    running_mean,
    running_variance,
    momentum,
    keep_count,
    visible_index,
    encoder_flat,
    decoder_flat,
):
    all_count = 2 * count
    core = lax.axis_index("dp")
    me = lax.axis_index("fsdp")
    index = jnp.stack([me, core]).astype(jnp.int32)
    inverse = lax.rsqrt(running_variance + EPS_NORM)
    chosen, keep_one = visible_index[0], keep_count[0]

    def own_half(flat):
        rows = flat.shape[0] // (2 * LANES)
        half = lax.dynamic_index_in_dim(flat.reshape(2, rows, LANES), core, 0, keepdims=False)
        return jnp.pad(half, ((0, -rows % 8), (0, 0))), rows

    encoder_half, encoder_rows = own_half(encoder_flat)
    decoder_half, decoder_rows = own_half(decoder_flat)
    encoder_all = lax.all_gather(encoder_half, ("fsdp", "dp"), axis=0, tiled=False)
    patches, moments = patchify(pixels[0], running_mean, inverse)
    encoder_all, decoder_half, patches, moments, places, table = lax.optimization_barrier(
        (
            encoder_all,
            decoder_half,
            patches,
            moments,
            jnp.take(position_table(D_ENC), chosen, axis=0),
            position_table(D_DEC),
        )
    )
    decoder_all = lax.all_gather(decoder_half, ("fsdp", "dp"), axis=0, tiled=False)

    scatters = []

    def go_on(grad):
        grad = scatters[0].hold(grad)
        scatters[0].step()
        return grad

    marks = [go_on] * 4
    encoder = unpack(index, [encoder_all], encoder_rows, all_count, False, encoder_shapes())
    encoded, encode_back = jax.vjp(
        lambda params, patch: encode_item(params, patch, places, chosen, keep_one, marks),
        encoder,
        patches,
    )
    decoder = unpack(index, [decoder_all], decoder_rows, all_count, False, decoder_shapes())
    objective, decode_back, squared = jax.vjp(
        lambda params, enc, patch: decode_item(params, enc, patch, table, chosen, keep_one),
        decoder,
        encoded,
        patches,
        has_aux=True,
    )
    grad_decoder, grad_encoded, grad_patches = decode_back(jnp.ones((), jnp.float32))
    masked_here = (TOK_ITEM - keep_one).astype(jnp.float32)
    stats = jnp.concatenate([moments[:, 0], moments[:, 1], jnp.stack([squared, masked_here])])
    place = jnp.arange(all_count)[:, None] == core * count + me
    tail = jnp.where(place, jnp.pad(stats, (0, 16 - stats.shape[0]))[None, :], 0.0)
    tail = tail.reshape(-1, LANES)
    packed = pack(
        index, grad_decoder, tail, decoder_shapes(), all_count, decoder_rows, True
    )
    scatters.append(Scatter(packed, count))
    scatters[0].step()
    grad_encoder, more_patches = encode_back(grad_encoded)
    decoder_sum = scatters[0].total()

    packed = pack(
        index, grad_encoder, tail, encoder_shapes(), all_count, encoder_rows, True
    )
    encoder_scatter = Scatter(packed, count)
    for _ in range(3):
        encoder_scatter.step()
    pixel_grad = unpatchify(grad_patches + more_patches, inverse).reshape(pixels.shape)
    pixel_grad = encoder_scatter.hold(pixel_grad)
    encoder_sum = encoder_scatter.total()
    totals = encoder_sum[encoder_rows : encoder_rows + tail.shape[0]].reshape(all_count, 16)
    totals = jnp.sum(totals, axis=0)

    pixel_count = float(all_count * FRAMES * IMG * IMG)
    band_mean = totals[:BANDS] / pixel_count
    band_var = totals[BANDS : 2 * BANDS] / pixel_count - band_mean * band_mean
    next_mean = (1.0 - momentum) * running_mean + momentum * band_mean
    next_variance = (1.0 - momentum) * running_variance + momentum * band_var
    masked_loss = totals[2 * BANDS] / (totals[2 * BANDS + 1] * PIX)
    return (
        masked_loss,
        pixel_grad,
        both_halves(encoder_sum, encoder_rows, core),
        both_halves(decoder_sum, decoder_rows, core),
        next_mean,
        next_variance,
    )


def solution(mesh):
    placed = (
        P(("dp", "fsdp"), None, None, None),
        P(),
        P(),
        P(),
        P(("dp", "fsdp")),
        P(("dp", "fsdp"), None),
        P("fsdp"),
        P("fsdp"),
    )
    return jax.shard_map(
        functools.partial(body, mesh.shape["fsdp"]),
        mesh=mesh,
        in_specs=placed,
        out_specs=(P(), P(("dp", "fsdp"), None, None, None), P("fsdp"), P("fsdp"), P(), P()),
        check_vma=False,
    )
```

```python
import functools
import math

import jax
import jax.numpy as jnp
from jax import lax
from jax.experimental import pallas as pl
from jax.experimental.pallas import tpu as pltpu
from jax.sharding import PartitionSpec as P

D_ENC = 768
HEADS_E = 12
MLP_E = 3072
D_DEC = 512
HEADS_D = 16
MLP_D = 2048
BANDS = 6
PATCH = 16
FRAMES = 3
GRID = 14
TOK_ITEM = 588
IMG = 224
PIX = 1536
KEEP_MAX = 236
LANES = 128
SMALL = 3072

EPS_NORM = 1e-06
MASKED_SCORE = -1e30
PREC = lax.Precision.HIGH
VMEM_LIMIT = 60 * 2**20


def matmul(left, right):
    return jnp.dot(left, right, precision=PREC, preferred_element_type=jnp.float32)


def block_shapes(width, hidden):
    return [
        (width,),
        (width,),
        (width, 3 * width),
        (width,),
        (width,),
        (width, width),
        (width,),
        (width,),
        (width,),
        (width, hidden),
        (hidden,),
        (hidden, width),
        (width,),
    ]


def encoder_shapes():
    return [(PIX, D_ENC), (D_ENC,)] + block_shapes(D_ENC, MLP_E) + [(D_ENC,), (D_ENC,)]


def decoder_shapes():
    return (
        [(D_ENC, D_DEC), (D_DEC,), (D_DEC,)]
        + block_shapes(D_DEC, MLP_D)
        + [(D_DEC,), (D_DEC,), (D_DEC, PIX), (PIX,)]
    )


def row_layout(shapes):
    matrices, vectors, row = [], [], 0
    for shape in shapes:
        if len(shape) == 2:
            matrices.append((row, shape[0], shape[1]))
        else:
            vectors.append((row, shape[0] // LANES))
        row += math.prod(shape) // LANES
    return matrices, vectors, row


SLOTS = 4
STAGE = 393216


def plan(shapes):
    blocks = []
    for at, (row, rows, columns) in enumerate(row_layout(shapes)[0]):
        size = max(r for r in range(8, rows + 1, 8) if rows % r == 0 and r * columns <= STAGE)
        for first in range(0, rows, size):
            blocks.append((at, first, size, columns, row + first * (columns // LANES)))
    return blocks


def stage_view(stage, slot, size, columns):
    return stage.at[slot, pl.ds(0, size), pl.ds(0, columns)]


def move_block(lin, stage, slot, size, columns, base, inward):
    tiles = columns // LANES
    groups = size // 8
    unroll = max(u for u in range(1, 9) if groups % u == 0 and u * tiles <= 48)

    def some(r, carry):
        for u in range(unroll):
            at = r * unroll + u
            for t in range(tiles):
                rows = pl.ds(base + at * (8 * tiles) + t, 8, stride=tiles)
                place = pl.ds(pl.multiple_of(at * 8, 8), 8)
                if inward:
                    stage[slot, place, t * LANES : (t + 1) * LANES] = lin[rows, :]
                else:
                    lin[rows, :] = stage[slot, place, t * LANES : (t + 1) * LANES]
        return carry

    lax.fori_loop(0, groups // unroll, some, 0)


def unpack_kernel(shapes, half_rows, piece_count, sources, relative, *refs):
    matrices, vectors, used = row_layout(shapes)
    index_ref = refs[0]
    ins = refs[1 : 1 + sources]
    outs = refs[1 + sources : 1 + sources + len(matrices)]
    small_ref = refs[1 + sources + len(matrices)]
    lin, stage, in_sem, out_sem = refs[2 + sources + len(matrices) :]
    me, core = index_ref[0], index_ref[1]

    def copy_piece(source, place):
        return pltpu.make_async_copy(
            source.at[pl.ds(0, half_rows)],
            lin.at[pl.ds(place * half_rows, half_rows)],
            in_sem.at[place],
        )

    if relative:
        pairs = piece_count // 4
        for side in range(2):
            for j in range(piece_count // 2):
                owner = jnp.bitwise_xor(me, j)
                half = core if side == 0 else 1 - core
                group, k, role = j // 8, j // 4 % 2, j % 4
                source = ins[side * (pairs // 4) + group]
                copy_piece(source.at[role * 2 + k], owner * 2 + half).start()
    else:
        for place in range(piece_count):
            copy_piece(ins[0].at[place], place).start()

    arrived = 0

    def wait_for(last, arrived):
        while arrived < piece_count and arrived * half_rows < last:
            copy_piece(ins[0].at[0], arrived).wait()
            arrived += 1
        return arrived

    copies = []
    for number, (at, first, size, columns, base) in enumerate(plan(shapes)):
        arrived = wait_for(base + size * (columns // LANES), arrived)
        slot = number % SLOTS
        if number >= SLOTS:
            copies[number - SLOTS].wait()
        move_block(lin, stage, slot, size, columns, base, True)
        copies.append(
            pltpu.make_async_copy(
                stage_view(stage, slot, size, columns),
                outs[at].at[pl.ds(first, size)],
                out_sem.at[slot],
            )
        )
        copies[-1].start()
    wait_for(piece_count * half_rows, arrived)
    small_ref[...] = jnp.zeros_like(small_ref)
    for i, (row, count) in enumerate(vectors):
        for t in range(count):
            small_ref[i : i + 1, t * LANES : (t + 1) * LANES] = lin[row + t : row + t + 1, :]
    for copy in copies[-SLOTS:]:
        copy.wait()


def unpack(index, sources, half_rows, piece_count, relative, shapes):
    matrices, vectors, _ = row_layout(shapes)
    any_spec = pl.BlockSpec(memory_space=pltpu.HBM)
    slots = -(-len(vectors) // 8) * 8
    total = piece_count * half_rows
    wide, flat = scratch_of(shapes, total)
    outs = pl.pallas_call(
        functools.partial(
            unpack_kernel, shapes, half_rows, piece_count, len(sources), relative
        ),
        out_shape=[jax.ShapeDtypeStruct(m[1:], jnp.float32) for m in matrices]
        + [jax.ShapeDtypeStruct((slots, SMALL), jnp.float32)],
        in_specs=[pl.BlockSpec(memory_space=pltpu.SMEM)] + [any_spec] * len(sources),
        out_specs=[any_spec] * len(matrices) + [pl.BlockSpec(memory_space=pltpu.VMEM)],
        scratch_shapes=[
            flat,
            wide,
            pltpu.SemaphoreType.DMA((piece_count,)),
            pltpu.SemaphoreType.DMA((SLOTS,)),
        ],
        compiler_params=pltpu.CompilerParams(vmem_limit_bytes=VMEM_LIMIT),
        cost_estimate=pl.CostEstimate(
            flops=0, bytes_accessed=8 * total * LANES, transcendentals=0
        ),
    )(index, *sources)
    small = outs[-1]
    pieces, matrix_at, vector_at = [], 0, 0
    for shape in shapes:
        if len(shape) == 2:
            pieces.append(outs[matrix_at])
            matrix_at += 1
        else:
            pieces.append(small[vector_at, : shape[0]])
            vector_at += 1
    return pieces


def scratch_of(shapes, total):
    blocks = plan(shapes)
    wide = pltpu.VMEM(
        (SLOTS, max(b[2] for b in blocks), max(b[3] for b in blocks)), jnp.float32
    )
    return wide, pltpu.VMEM((-(-total // 8) * 8, LANES), jnp.float32)


def pack_kernel(shapes, half_rows, piece_count, relative, *refs):
    matrices, vectors, used = row_layout(shapes)
    index_ref = refs[0]
    ins = refs[1 : 1 + len(matrices)]
    small_ref, tail_ref = refs[1 + len(matrices) : 3 + len(matrices)]
    outs = refs[3 + len(matrices) : -4]
    lin, stage, in_sem, out_sem = refs[-4:]
    me, core = index_ref[0], index_ref[1]
    tail_rows = tail_ref.shape[0]
    blocks = plan(shapes)

    def copy_in(number):
        at, first, size, columns, _ = blocks[number]
        slot = number % SLOTS
        return pltpu.make_async_copy(
            ins[at].at[pl.ds(first, size)],
            stage_view(stage, slot, size, columns),
            in_sem.at[slot],
        )

    for number in range(min(SLOTS - 1, len(blocks))):
        copy_in(number).start()

    for i, (row, count) in enumerate(vectors):
        for t in range(count):
            lin[row + t : row + t + 1, :] = small_ref[i : i + 1, t * LANES : (t + 1) * LANES]
    total = piece_count * half_rows
    if total > used:
        lin[used:total, :] = jnp.zeros((total - used, LANES), jnp.float32)

    def copies(place, target):
        return (
            pltpu.make_async_copy(
                lin.at[pl.ds(place * half_rows, half_rows)],
                target.at[pl.ds(0, half_rows)],
                out_sem.at[place, 0],
            ),
            pltpu.make_async_copy(
                tail_ref, target.at[pl.ds(half_rows, tail_rows)], out_sem.at[place, 1]
            ),
        )

    def send_piece(place):
        def start(target):
            for copy in copies(place, target):
                copy.start()

        if not relative:
            start(outs[0].at[place])
            return
        j = jnp.bitwise_xor(me, place // 2)
        within = lax.rem(j, 4) * 2 + lax.rem(lax.div(j, 4), 2)
        away = jnp.where(core == place % 2, 0, 2)
        corner = jnp.where(within < 6, 0, 1)
        target = lax.div(j, 8) * 4 + away + corner
        for number, out in enumerate(outs):

            @pl.when(target == number)
            def _(out=out, number=number):
                start(out.at[within - 6 if number % 2 else within])

    sent = 0
    for number, (at, first, size, columns, base) in enumerate(blocks):
        if number + SLOTS - 1 < len(blocks):
            copy_in(number + SLOTS - 1).start()
        copy_in(number).wait()
        move_block(lin, stage, number % SLOTS, size, columns, base, False)
        done = base + size * (columns // LANES)
        if number == len(blocks) - 1:
            done = total
        while (sent + 1) * half_rows <= done and sent < piece_count:
            send_piece(sent)
            sent += 1
    for place in range(piece_count):
        for copy in copies(place, outs[0].at[0]):
            copy.wait()


def padded_rows(half_rows, tail_rows):
    return -(-(half_rows + tail_rows) // 8) * 8


def pack(index, grads, tail, shapes, piece_count, half_rows, relative):
    matrices, vectors, _ = row_layout(shapes)
    padded = padded_rows(half_rows, tail.shape[0])
    tail = jnp.pad(tail, ((0, padded - half_rows - tail.shape[0]), (0, 0)))
    slots = -(-len(vectors) // 8) * 8
    mats = [g for g, s in zip(grads, shapes) if len(s) == 2]
    vecs = [jnp.pad(g, (0, SMALL - g.shape[0])) for g, s in zip(grads, shapes) if len(s) == 1]
    vecs += [jnp.zeros((SMALL,), jnp.float32)] * (slots - len(vecs))
    any_spec = pl.BlockSpec(memory_space=pltpu.HBM)
    vmem_spec = pl.BlockSpec(memory_space=pltpu.VMEM)
    total = piece_count * half_rows
    wide, flat = scratch_of(shapes, total)
    if relative:
        sizes = [6, 2, 6, 2] * (piece_count // 16)
    else:
        sizes = [piece_count]
    return pl.pallas_call(
        functools.partial(pack_kernel, shapes, half_rows, piece_count, relative),
        out_shape=[jax.ShapeDtypeStruct((n, padded, LANES), jnp.float32) for n in sizes],
        in_specs=[pl.BlockSpec(memory_space=pltpu.SMEM)]
        + [any_spec] * len(matrices)
        + [vmem_spec] * 2,
        out_specs=[any_spec] * len(sizes),
        scratch_shapes=[
            flat,
            wide,
            pltpu.SemaphoreType.DMA((SLOTS,)),
            pltpu.SemaphoreType.DMA((piece_count, 2)),
        ],
        compiler_params=pltpu.CompilerParams(vmem_limit_bytes=VMEM_LIMIT),
        cost_estimate=pl.CostEstimate(
            flops=0, bytes_accessed=8 * total * LANES, transcendentals=0
        ),
    )(index, *mats, jnp.stack(vecs), tail)


QUADS = FRAMES * GRID
GROUP = LANES // PATCH
STARTS = tuple(range(0, QUADS - 7, 8)) + ((QUADS - 8,) if QUADS % 8 else ())


def patch_kernel(mean_ref, inverse_ref, pixel_ref, patch_ref, moment_ref, scratch):
    band = pl.program_id(0)
    mean, inverse = mean_ref[band], inverse_ref[band]
    group = lax.broadcasted_iota(jnp.int32, (8, LANES), 1) // PATCH

    def sums(i, carry):
        one, two = carry
        value = pixel_ref[0, pl.ds(pl.multiple_of(i * 8, 8), 8), :]
        return one + value, two + value * value

    zero = jnp.zeros((8, LANES), jnp.float32)
    one, two = lax.fori_loop(0, pixel_ref.shape[1] // 8, sums, (zero, zero), unroll=7)
    moment_ref[0, 0] = one
    moment_ref[0, 1] = two
    for side in range(2):
        for first in STARTS:
            rows = []
            for k in range(GRID):
                start = 2 * GRID * first + GRID * side + k
                raw = pixel_ref[0, pl.ds(start, 8, stride=2 * GRID), :]
                rows.append((raw - mean) * inverse)
            for column in range(GRID):
                out = None
                for line in range(GROUP):
                    place = GRID * line + column
                    moved = pltpu.roll(rows[place // GROUP], PATCH * ((line - place) % GROUP), 1)
                    out = moved if out is None else jnp.where(group == line, moved, out)
                scratch[pl.ds(GRID * first + column, 8, stride=GRID), :] = out
        patch_ref[:, side * LANES : (side + 1) * LANES] = scratch[...]


def patchify(pixels, mean, inverse):
    rows = QUADS * 2 * GRID
    smem = pl.BlockSpec(memory_space=pltpu.SMEM)
    patches, moments = pl.pallas_call(
        patch_kernel,
        grid=(BANDS,),
        out_shape=[
            jax.ShapeDtypeStruct((TOK_ITEM, PIX), jnp.float32),
            jax.ShapeDtypeStruct((BANDS, 2, 8, LANES), jnp.float32),
        ],
        in_specs=[smem, smem, pl.BlockSpec((1, rows, LANES), lambda b: (b, 0, 0))],
        out_specs=[
            pl.BlockSpec((TOK_ITEM, 2 * LANES), lambda b: (0, b)),
            pl.BlockSpec((1, 2, 8, LANES), lambda b: (b, 0, 0, 0)),
        ],
        scratch_shapes=[pltpu.VMEM((TOK_ITEM, LANES), jnp.float32)],
        cost_estimate=pl.CostEstimate(
            flops=0, bytes_accessed=16 * TOK_ITEM * PIX, transcendentals=0
        ),
    )(mean, inverse, pixels.reshape(BANDS, rows, LANES))
    return patches, jnp.sum(moments, axis=(2, 3))


def pixel_kernel(inverse_ref, patch_ref, pixel_ref, scratch):
    inverse = inverse_ref[pl.program_id(0)]
    group = lax.broadcasted_iota(jnp.int32, (8, LANES), 1) // PATCH
    for side in range(2):
        scratch[...] = patch_ref[:, side * LANES : (side + 1) * LANES] * inverse
        for first in STARTS:
            columns = [
                scratch[pl.ds(GRID * first + column, 8, stride=GRID), :] for column in range(GRID)
            ]
            for k in range(GRID):
                out = None
                for slot in range(GROUP):
                    line, column = divmod(GROUP * k + slot, GRID)
                    moved = pltpu.roll(columns[column], PATCH * ((slot - line) % GROUP), 1)
                    out = moved if out is None else jnp.where(group == slot, moved, out)
                start = 2 * GRID * first + GRID * side + k
                pixel_ref[0, pl.ds(start, 8, stride=2 * GRID), :] = out


def unpatchify(grad_patches, inverse):
    rows = QUADS * 2 * GRID
    return pl.pallas_call(
        pixel_kernel,
        grid=(BANDS,),
        out_shape=jax.ShapeDtypeStruct((BANDS, rows, LANES), jnp.float32),
        in_specs=[
            pl.BlockSpec(memory_space=pltpu.SMEM),
            pl.BlockSpec((TOK_ITEM, 2 * LANES), lambda b: (0, b)),
        ],
        out_specs=pl.BlockSpec((1, rows, LANES), lambda b: (b, 0, 0)),
        scratch_shapes=[pltpu.VMEM((TOK_ITEM, LANES), jnp.float32)],
        cost_estimate=pl.CostEstimate(
            flops=0, bytes_accessed=16 * TOK_ITEM * PIX, transcendentals=0
        ),
    )(inverse, grad_patches)


def swap(value, distance, count):
    return lax.ppermute(value, "fsdp", [(i, i ^ distance) for i in range(count)])


def swap_cores(value):
    return lax.ppermute(value, "dp", [(0, 1), (1, 0)])


def split_row(rows):
    return rows // 16 * 8


class Scatter:
    def __init__(self, packed, count):
        self.count, self.groups = count, len(packed) // 4
        self.middle = split_row(packed[0].shape[1])
        self.keep_sides, self.keep_corners = packed[::4], packed[1::4]
        self.sides, self.corners = packed[2::4], packed[3::4]
        self.time = -1
        self.pending = {}
        self.own = {}
        self.landed = []

    def hold(self, value):
        value, self.pending = lax.optimization_barrier((value, self.pending))
        return value

    def step(self):
        count, groups, middle = self.count, self.groups, self.middle
        arrived, sent = self.pending, {}
        last, ready, new = groups + 1 - self.time, groups - self.time, groups - 1 - self.time
        if "turned" in arrived:
            near, turned = arrived["turned"]
            self.landed.append(swap(near + turned, 8 * (last + 1), count))
        if 0 <= last < groups:
            along_x, along_y = arrived["sides"]
            part = self.own[last] + along_x + along_y
            turned = swap(part[1], 4, count)
            if last:
                sent["turned"] = (part[0], turned)
            else:
                self.landed += [part[0], turned]
        if 0 <= ready < groups:
            first, second = arrived["corner"]
            own, for_x, for_y = [
                (self.keep_sides[ready] + arrived["core sides"])[2 * i : 2 * i + 2] for i in range(3)
            ]
            self.own[ready] = own
            for_x = jnp.concatenate([for_x[:, :middle] + first, for_x[:, middle:]], axis=1)
            for_y = jnp.concatenate([for_y[:, :middle], for_y[:, middle:] + second], axis=1)
            sent["sides"] = [swap(for_x, 1, count), swap(for_y, 2, count)]
        if 0 <= new < groups:
            corner = self.keep_corners[new] + arrived["core corner"]
            sent["corner"] = [
                swap(corner[:, :middle], 2, count),
                swap(corner[:, middle:], 1, count),
            ]
            sides, _ = lax.optimization_barrier((self.sides[new], corner))
            sent["core sides"] = swap_cores(sides)
        if 0 <= new - 1 < groups:
            sent["core corner"] = swap_cores(self.corners[new - 1])
        self.pending = sent
        self.time += 1

    def total(self):
        while self.time < self.groups + 2:
            self.step()
        return functools.reduce(jnp.add, self.landed)


def both_halves(half, rows, core):
    got = swap_cores(half)
    low = jnp.where(core == 0, half, got)[:rows]
    high = jnp.where(core == 0, got, half)[:rows]
    return jnp.concatenate([low, high]).reshape(-1)


def sincos_part(width, positions):
    frequency = 1.0 / 10000.0 ** (jnp.arange(width // 2).astype(jnp.float32) / (width / 2.0))
    angles = positions[:, None] * frequency[None, :]
    return jnp.concatenate([jnp.sin(angles), jnp.cos(angles)], axis=1)


def position_table(width):
    token_ids = jnp.arange(TOK_ITEM)
    frame_pos = (token_ids // (GRID * GRID)).astype(jnp.float32)
    row_pos = (token_ids // GRID % GRID).astype(jnp.float32)
    column_pos = (token_ids % GRID).astype(jnp.float32)
    return jnp.concatenate(
        [
            sincos_part(width // 16 * 4, frame_pos),
            sincos_part(width // 16 * 6, row_pos),
            sincos_part(width // 16 * 6, column_pos),
        ],
        axis=1,
    )


def layer_norm(values, gain, shift):
    centre = jnp.mean(values, axis=-1, keepdims=True)
    spread = jnp.mean(jnp.square(values - centre), axis=-1, keepdims=True)
    return (values - centre) * lax.rsqrt(spread + EPS_NORM) * gain + shift


QUERY_CHUNK = 640
KEY_CHUNK = 384


def split_two(value):
    high = value.astype(jnp.bfloat16)
    return high, (value - high.astype(jnp.float32)).astype(jnp.bfloat16)


def nt(left, right):
    return lax.dot_general(
        left, right, (((1,), (1,)), ((), ())), preferred_element_type=jnp.float32
    )


def nn(left, right):
    return jnp.dot(left, right, preferred_element_type=jnp.float32)


def chunks(rows, size):
    return [(at, min(size, rows - at)) for at in range(0, rows, size)]


def put_parts(ref, value, order):
    parts = split_two(value)
    for i, which in enumerate(order):
        ref[:, i * LANES : (i + 1) * LANES] = parts[which]


def put_turned(ref, value, size):
    for i, part in enumerate(split_two(value)):
        turned = part.astype(jnp.float32).T.astype(jnp.bfloat16)
        for head in range(LANES // size):
            ref[head, i * size : (i + 1) * size, :] = turned[head * size : (head + 1) * size, :]


def own_lanes(head, size, width):
    lane = lax.broadcasted_iota(jnp.int32, (1, width), 1)
    return (lax.rem(lane, LANES) // size == head).astype(jnp.float32).astype(jnp.bfloat16)


def hide_dead(scores, first, keep):
    if keep is None:
        return scores
    key = lax.broadcasted_iota(jnp.int32, scores.shape, 0) + first
    return jnp.where(key < keep, scores, MASKED_SCORE)


def turned_product(parts, high, low, size):
    both = nn(parts, high)
    return both[:size] + both[size:] + nn(parts[:size], low)


def attend_kernel(size, masked, keep_ref, q_ref, k_ref, v_ref, out_ref, lse_ref, q3, k3, v2t, out_t):
    head = pl.program_id(1)
    keep = keep_ref[0] if masked else None

    @pl.when(head == 0)
    def _():
        put_parts(q3, q_ref[...] * (1.0 / math.sqrt(size)), (0, 1, 0))
        put_parts(k3, k_ref[...], (0, 0, 1))
        put_turned(v2t, v_ref[...], size)

    lanes = own_lanes(head, size, 3 * LANES)
    values = v2t[head]
    for at, count in chunks(q_ref.shape[0], QUERY_CHUNK):
        place = slice(at, at + count)
        scores = hide_dead(nt(k3[...], q3[place, :] * lanes), 0, keep)
        top = jnp.max(scores, axis=0, keepdims=True)
        weights = jnp.exp(scores - top)
        total = jnp.sum(weights, axis=0, keepdims=True)
        high, low = split_two(weights)
        mixed = turned_product(values, high, low, size) / total
        out_t[pl.ds(pl.multiple_of(head * size, size), size), place] = mixed
        lse_ref[0, :, place] = top + jnp.log(total)

    @pl.when(head == LANES // size - 1)
    def _():
        out_ref[...] = out_t[...].T


def attend_forward(joined, keep, heads):
    rows, width = joined.shape[0], joined.shape[1] // 3
    size = width // heads
    blocks, per_block = width // LANES, LANES // size
    masked = keep is not None
    keep = keep if masked else jnp.zeros((1,), jnp.int32)

    def columns(first):
        return pl.BlockSpec((rows, LANES), lambda g, h: (0, first + g))

    return pl.pallas_call(
        functools.partial(attend_kernel, size, masked),
        grid=(blocks, per_block),
        out_shape=[
            jax.ShapeDtypeStruct((rows, width), jnp.float32),
            jax.ShapeDtypeStruct((heads, 1, rows), jnp.float32),
        ],
        in_specs=[
            pl.BlockSpec(memory_space=pltpu.SMEM),
            columns(0),
            columns(blocks),
            columns(2 * blocks),
        ],
        out_specs=[
            columns(0),
            pl.BlockSpec((1, 1, rows), lambda g, h: (g * per_block + h, 0, 0)),
        ],
        scratch_shapes=[
            pltpu.VMEM((rows, 3 * LANES), jnp.bfloat16),
            pltpu.VMEM((rows, 3 * LANES), jnp.bfloat16),
            pltpu.VMEM((per_block, 2 * size, rows), jnp.bfloat16),
            pltpu.VMEM((LANES, rows), jnp.float32),
        ],
        compiler_params=pltpu.CompilerParams(vmem_limit_bytes=VMEM_LIMIT),
        cost_estimate=pl.CostEstimate(
            flops=16 * rows * rows * width,
            bytes_accessed=16 * rows * width,
            transcendentals=heads * rows * rows,
        ),
    )(keep, joined, joined, joined)


def attend_back_kernel(
    size, masked, keep_ref, q_ref, k_ref, v_ref, g_ref, lse_ref, delta_ref, out_ref,
    q3, k3, v3, g3, q3m, g3m, k2t, dq_t, dq, dk, dv, sem,
):
    block, head = pl.program_id(0), pl.program_id(1)
    keep = keep_ref[0] if masked else None
    scale = 1.0 / math.sqrt(size)
    width = out_ref.shape[1] // 3

    @pl.when(head == 0)
    def _():
        put_parts(q3, q_ref[...] * scale, (0, 1, 0))
        put_parts(k3, k_ref[...], (0, 0, 1))
        put_parts(v3, v_ref[...], (0, 0, 1))
        put_parts(g3, g_ref[...], (0, 1, 0))
        put_turned(k2t, k_ref[...], size)
        dk[...] = jnp.zeros_like(dk)
        dv[...] = jnp.zeros_like(dv)

    lanes = own_lanes(head, size, 3 * LANES)
    q3m[...] = q3[...] * lanes
    g3m[...] = g3[...] * lanes
    lse, delta = lse_ref[0], delta_ref[0]
    turned = None
    for at, count in chunks(q_ref.shape[0], KEY_CHUNK):
        place = slice(at, at + count)
        scores = hide_dead(nt(k3[place, :], q3m[...]), at, keep)
        weights = jnp.exp(scores - lse)
        high, low = split_two(weights)
        both = nn(high, g3m[:, : 2 * LANES])
        dv[place, :] += both[:, :LANES] + both[:, LANES:] + nn(low, g3m[:, :LANES])
        change = weights * (nt(v3[place, :], g3m[...]) - delta)
        high, low = split_two(change)
        both = nn(high, q3m[:, : 2 * LANES])
        dk[place, :] += both[:, :LANES] + both[:, LANES:] + nn(low, q3m[:, :LANES])
        part = turned_product(k2t[head, :, place], high, low, size)
        turned = part if turned is None else turned + part
    dq_t[pl.ds(pl.multiple_of(head * size, size), size), :] = turned

    @pl.when(head == LANES // size - 1)
    def _():
        dq[...] = dq_t[...].T * scale
        copies = [
            pltpu.make_async_copy(
                source,
                out_ref.at[:, pl.ds(pl.multiple_of(i * width + block * LANES, LANES), LANES)],
                sem.at[i],
            )
            for i, source in enumerate((dq, dk, dv))
        ]
        for copy in copies:
            copy.start()
        for copy in copies:
            copy.wait()


def attend_backward(joined, keep, heads, grad, lse, delta):
    rows, width = joined.shape[0], joined.shape[1] // 3
    size = width // heads
    blocks, per_block = width // LANES, LANES // size
    masked = keep is not None
    keep = keep if masked else jnp.zeros((1,), jnp.int32)

    def columns(first):
        return pl.BlockSpec((rows, LANES), lambda g, h: (0, first + g))

    per_head = pl.BlockSpec((1, 1, rows), lambda g, h: (g * per_block + h, 0, 0))
    return pl.pallas_call(
        functools.partial(attend_back_kernel, size, masked),
        grid=(blocks, per_block),
        out_shape=jax.ShapeDtypeStruct((rows, 3 * width), jnp.float32),
        in_specs=[
            pl.BlockSpec(memory_space=pltpu.SMEM),
            columns(0),
            columns(blocks),
            columns(2 * blocks),
            columns(0),
            per_head,
            per_head,
        ],
        out_specs=pl.BlockSpec(memory_space=pltpu.HBM),
        scratch_shapes=[pltpu.VMEM((rows, 3 * LANES), jnp.bfloat16)] * 6
        + [
            pltpu.VMEM((per_block, 2 * size, rows), jnp.bfloat16),
            pltpu.VMEM((LANES, rows), jnp.float32),
        ]
        + [pltpu.VMEM((rows, LANES), jnp.float32)] * 3
        + [pltpu.SemaphoreType.DMA((3,))],
        compiler_params=pltpu.CompilerParams(vmem_limit_bytes=VMEM_LIMIT),
        cost_estimate=pl.CostEstimate(
            flops=40 * rows * rows * width,
            bytes_accessed=28 * rows * width,
            transcendentals=heads * rows * rows,
        ),
    )(keep, joined, joined, joined, grad, lse, delta)


@functools.partial(jax.custom_vjp, nondiff_argnums=(2,))
def attend(joined, keep, heads):
    return attend_forward(joined, keep, heads)[0]


def attend_keep(joined, keep, heads):
    out, lse = attend_forward(joined, keep, heads)
    return out, (joined, keep, out, lse)


def attend_pull(heads, kept, grad):
    joined, keep, out, lse = kept
    width = out.shape[1]
    owner = jnp.arange(width)[None, :] // (width // heads) == jnp.arange(heads)[:, None]
    delta = lax.dot_general(
        owner.astype(jnp.float32),
        grad * out,
        (((1,), (1,)), ((), ())),
        precision=lax.Precision.HIGHEST,
        preferred_element_type=jnp.float32,
    )
    return attend_backward(joined, keep, heads, grad, lse, delta[:, None, :]), None


attend.defvjp(attend_keep, attend_pull)


TAIL = (
    -1.26551223,
    1.00002368,
    0.37409196,
    0.09678418,
    -0.18628806,
    0.27886807,
    -1.13520398,
    1.48851587,
    -0.82215223,
    0.17087277,
)


def gelu_parts(value):
    scaled = jnp.abs(value) * math.sqrt(0.5)
    inverse = 1.0 / (1.0 + 0.5 * scaled)
    power = TAIL[-1]
    for factor in TAIL[-2::-1]:
        power = power * inverse + factor
    square = scaled * scaled
    below = 0.5 * inverse * jnp.exp(power - square)
    share = jnp.where(value >= 0.0, 1.0 - below, below)
    slope = share + value * (math.sqrt(0.5 / math.pi) * jnp.exp(-square))
    return value * share, slope


@jax.custom_vjp
def gelu(value):
    return gelu_parts(value)[0]


gelu.defvjp(lambda value: lax.optimization_barrier(gelu_parts(value)), lambda slope, grad: (grad * slope,))


@functools.partial(jax.custom_vjp, nondiff_argnums=(1,))
def mark(value, on_way_back):
    return value


def mark_keep(value, on_way_back):
    return value, None


def mark_pull(on_way_back, kept, grad):
    return (on_way_back(grad),)


mark.defvjp(mark_keep, mark_pull)


def marked(value, marks, number):
    return value if marks is None else mark(value, marks[number])


def transformer_block(stream, params, head_count, keep, marks):
    (
        first_gain,
        first_shift,
        qkv_weight,
        query_bias,
        value_bias,
        out_weight,
        out_bias,
        second_gain,
        second_shift,
        up_weight,
        up_bias,
        down_weight,
        down_bias,
    ) = params
    normed = layer_norm(stream, first_gain, first_shift)
    joined = matmul(normed, qkv_weight)
    joined = joined + jnp.concatenate([query_bias, jnp.zeros_like(query_bias), value_bias])
    mixed = marked(attend(marked(joined, marks, 3), keep, head_count), marks, 2)
    stream = marked(stream + matmul(mixed, out_weight) + out_bias, marks, 1)
    normed = layer_norm(stream, second_gain, second_shift)
    before = marked(matmul(normed, up_weight) + up_bias, marks, 0)
    hidden = gelu(before)
    return stream + matmul(hidden, down_weight) + down_bias


def encode_item(encoder, patch_one, places, chosen, keep_one, marks):
    visible = jnp.take(patch_one, chosen, axis=0)
    stream = matmul(visible, encoder[0]) + encoder[1] + places
    stream = transformer_block(stream, encoder[2:15], HEADS_E, keep_one[None], marks)
    return layer_norm(stream, encoder[15], encoder[16])


def decode_item(decoder, encoded, patch_one, table, chosen, keep_one):
    slots = jnp.arange(KEEP_MAX)
    live = (slots < keep_one).astype(jnp.float32)
    token_ids = jnp.arange(TOK_ITEM)
    placer = (chosen[:, None] == token_ids[None, :]).astype(jnp.float32) * live[:, None]
    hidden_mask = 1.0 - jnp.sum(placer, axis=0)
    latent = matmul(encoded, decoder[0]) + decoder[1]
    stream = jnp.einsum("st,sd->td", placer, latent, precision=PREC)
    stream = stream + hidden_mask[:, None] * decoder[2][None, :] + table
    stream = transformer_block(stream, decoder[3:16], HEADS_D, None, None)
    normed = layer_norm(stream, decoder[16], decoder[17])
    predicted = matmul(normed, decoder[18]) + decoder[19]
    error = predicted - patch_one
    squared = jnp.sum(hidden_mask[:, None] * error * error)
    return (squared / (PATCH * PATCH), squared)


def body(
    count,
    pixels,
    running_mean,
    running_variance,
    momentum,
    keep_count,
    visible_index,
    encoder_flat,
    decoder_flat,
):
    all_count = 2 * count
    core = lax.axis_index("dp")
    me = lax.axis_index("fsdp")
    index = jnp.stack([me, core]).astype(jnp.int32)
    inverse = lax.rsqrt(running_variance + EPS_NORM)
    chosen, keep_one = visible_index[0], keep_count[0]

    def own_half(flat):
        rows = flat.shape[0] // (2 * LANES)
        half = lax.dynamic_index_in_dim(flat.reshape(2, rows, LANES), core, 0, keepdims=False)
        return jnp.pad(half, ((0, -rows % 8), (0, 0))), rows

    encoder_half, encoder_rows = own_half(encoder_flat)
    decoder_half, decoder_rows = own_half(decoder_flat)
    encoder_all = lax.all_gather(encoder_half, ("fsdp", "dp"), axis=0, tiled=False)
    patches, moments = patchify(pixels[0], running_mean, inverse)
    encoder_all, decoder_half, patches, moments, places, table = lax.optimization_barrier(
        (
            encoder_all,
            decoder_half,
            patches,
            moments,
            jnp.take(position_table(D_ENC), chosen, axis=0),
            position_table(D_DEC),
        )
    )
    decoder_all = lax.all_gather(decoder_half, ("fsdp", "dp"), axis=0, tiled=False)

    scatters = []

    def go_on(grad):
        grad = scatters[0].hold(grad)
        scatters[0].step()
        return grad

    marks = [go_on] * 4
    encoder = unpack(index, [encoder_all], encoder_rows, all_count, False, encoder_shapes())
    encoded, encode_back = jax.vjp(
        lambda params, patch: encode_item(params, patch, places, chosen, keep_one, marks),
        encoder,
        patches,
    )
    decoder = unpack(index, [decoder_all], decoder_rows, all_count, False, decoder_shapes())
    objective, decode_back, squared = jax.vjp(
        lambda params, enc, patch: decode_item(params, enc, patch, table, chosen, keep_one),
        decoder,
        encoded,
        patches,
        has_aux=True,
    )
    grad_decoder, grad_encoded, grad_patches = decode_back(jnp.ones((), jnp.float32))
    masked_here = (TOK_ITEM - keep_one).astype(jnp.float32)
    stats = jnp.concatenate([moments[:, 0], moments[:, 1], jnp.stack([squared, masked_here])])
    place = jnp.arange(all_count)[:, None] == core * count + me
    tail = jnp.where(place, jnp.pad(stats, (0, 16 - stats.shape[0]))[None, :], 0.0)
    tail = tail.reshape(-1, LANES)
    packed = pack(
        index, grad_decoder, tail, decoder_shapes(), all_count, decoder_rows, True
    )
    scatters.append(Scatter(packed, count))
    scatters[0].step()
    grad_encoder, more_patches = encode_back(grad_encoded)
    decoder_sum = scatters[0].total()

    packed = pack(
        index, grad_encoder, tail, encoder_shapes(), all_count, encoder_rows, True
    )
    encoder_scatter = Scatter(packed, count)
    for _ in range(2):
        encoder_scatter.step()
    pixel_grad = unpatchify(grad_patches + more_patches, inverse)
    pixel_grad = encoder_scatter.hold(pixel_grad).reshape(pixels.shape)
    encoder_sum = encoder_scatter.total()
    totals = encoder_sum[encoder_rows : encoder_rows + tail.shape[0]].reshape(all_count, 16)
    totals = jnp.sum(totals, axis=0)

    pixel_count = float(all_count * FRAMES * IMG * IMG)
    band_mean = totals[:BANDS] / pixel_count
    band_var = totals[BANDS : 2 * BANDS] / pixel_count - band_mean * band_mean
    next_mean = (1.0 - momentum) * running_mean + momentum * band_mean
    next_variance = (1.0 - momentum) * running_variance + momentum * band_var
    masked_loss = totals[2 * BANDS] / (totals[2 * BANDS + 1] * PIX)
    return (
        masked_loss,
        pixel_grad,
        both_halves(encoder_sum, encoder_rows, core),
        both_halves(decoder_sum, decoder_rows, core),
        next_mean,
        next_variance,
    )


def solution(mesh):
    placed = (
        P(("dp", "fsdp"), None, None, None),
        P(),
        P(),
        P(),
        P(("dp", "fsdp")),
        P(("dp", "fsdp"), None),
        P("fsdp"),
        P("fsdp"),
    )
    return jax.shard_map(
        functools.partial(body, mesh.shape["fsdp"]),
        mesh=mesh,
        in_specs=placed,
        out_specs=(P(), P(("dp", "fsdp"), None, None, None), P("fsdp"), P("fsdp"), P(), P()),
        check_vma=False,
    )
```

```python
import functools
import math

import jax
import jax.numpy as jnp
from jax import lax
from jax.experimental import pallas as pl
from jax.experimental.pallas import tpu as pltpu
from jax.sharding import PartitionSpec as P

D_ENC = 768
HEADS_E = 12
MLP_E = 3072
D_DEC = 512
HEADS_D = 16
MLP_D = 2048
BANDS = 6
PATCH = 16
FRAMES = 3
GRID = 14
TOK_ITEM = 588
IMG = 224
PIX = 1536
KEEP_MAX = 236
LANES = 128
SMALL = 3072

EPS_NORM = 1e-06
MASKED_SCORE = -1e30
PREC = lax.Precision.HIGH
VMEM_LIMIT = 60 * 2**20


def matmul(left, right):
    return jnp.dot(left, right, precision=PREC, preferred_element_type=jnp.float32)


def block_shapes(width, hidden):
    return [
        (width,),
        (width,),
        (width, 3 * width),
        (width,),
        (width,),
        (width, width),
        (width,),
        (width,),
        (width,),
        (width, hidden),
        (hidden,),
        (hidden, width),
        (width,),
    ]


def encoder_shapes():
    return [(PIX, D_ENC), (D_ENC,)] + block_shapes(D_ENC, MLP_E) + [(D_ENC,), (D_ENC,)]


def decoder_shapes():
    return (
        [(D_ENC, D_DEC), (D_DEC,), (D_DEC,)]
        + block_shapes(D_DEC, MLP_D)
        + [(D_DEC,), (D_DEC,), (D_DEC, PIX), (PIX,)]
    )


def row_layout(shapes):
    matrices, vectors, row = [], [], 0
    for shape in shapes:
        if len(shape) == 2:
            matrices.append((row, shape[0], shape[1]))
        else:
            vectors.append((row, shape[0] // LANES))
        row += math.prod(shape) // LANES
    return matrices, vectors, row


SLOTS = 4
STAGE = 393216


def plan(shapes):
    blocks = []
    for at, (row, rows, columns) in enumerate(row_layout(shapes)[0]):
        size = max(r for r in range(8, rows + 1, 8) if rows % r == 0 and r * columns <= STAGE)
        for first in range(0, rows, size):
            blocks.append((at, first, size, columns, row + first * (columns // LANES)))
    return blocks


def stage_view(stage, slot, size, columns):
    return stage.at[slot, pl.ds(0, size), pl.ds(0, columns)]


def move_block(lin, stage, slot, size, columns, base, inward):
    tiles = columns // LANES
    groups = size // 8
    unroll = max(u for u in range(1, 9) if groups % u == 0 and u * tiles <= 48)

    def some(r, carry):
        for u in range(unroll):
            at = r * unroll + u
            for t in range(tiles):
                rows = pl.ds(base + at * (8 * tiles) + t, 8, stride=tiles)
                place = pl.ds(pl.multiple_of(at * 8, 8), 8)
                if inward:
                    stage[slot, place, t * LANES : (t + 1) * LANES] = lin[rows, :]
                else:
                    lin[rows, :] = stage[slot, place, t * LANES : (t + 1) * LANES]
        return carry

    lax.fori_loop(0, groups // unroll, some, 0)


def unpack_kernel(shapes, half_rows, piece_count, sources, relative, *refs):
    matrices, vectors, used = row_layout(shapes)
    index_ref = refs[0]
    ins = refs[1 : 1 + sources]
    outs = refs[1 + sources : 1 + sources + len(matrices)]
    small_ref = refs[1 + sources + len(matrices)]
    lin, stage, in_sem, out_sem = refs[2 + sources + len(matrices) :]
    me, core = index_ref[0], index_ref[1]

    def copy_piece(source, place):
        return pltpu.make_async_copy(
            source.at[pl.ds(0, half_rows)],
            lin.at[pl.ds(place * half_rows, half_rows)],
            in_sem.at[place],
        )

    if relative:
        pairs = piece_count // 4
        for side in range(2):
            for j in range(piece_count // 2):
                owner = jnp.bitwise_xor(me, j)
                half = core if side == 0 else 1 - core
                group, k, role = j // 8, j // 4 % 2, j % 4
                source = ins[side * (pairs // 4) + group]
                copy_piece(source.at[role * 2 + k], owner * 2 + half).start()
    else:
        for place in range(piece_count):
            copy_piece(ins[0].at[place], place).start()

    arrived = 0

    def wait_for(last, arrived):
        while arrived < piece_count and arrived * half_rows < last:
            copy_piece(ins[0].at[0], arrived).wait()
            arrived += 1
        return arrived

    copies = []
    for number, (at, first, size, columns, base) in enumerate(plan(shapes)):
        arrived = wait_for(base + size * (columns // LANES), arrived)
        slot = number % SLOTS
        if number >= SLOTS:
            copies[number - SLOTS].wait()
        move_block(lin, stage, slot, size, columns, base, True)
        copies.append(
            pltpu.make_async_copy(
                stage_view(stage, slot, size, columns),
                outs[at].at[pl.ds(first, size)],
                out_sem.at[slot],
            )
        )
        copies[-1].start()
    wait_for(piece_count * half_rows, arrived)
    small_ref[...] = jnp.zeros_like(small_ref)
    for i, (row, count) in enumerate(vectors):
        for t in range(count):
            small_ref[i : i + 1, t * LANES : (t + 1) * LANES] = lin[row + t : row + t + 1, :]
    for copy in copies[-SLOTS:]:
        copy.wait()


def unpack(index, sources, half_rows, piece_count, relative, shapes):
    matrices, vectors, _ = row_layout(shapes)
    any_spec = pl.BlockSpec(memory_space=pltpu.HBM)
    slots = -(-len(vectors) // 8) * 8
    total = piece_count * half_rows
    wide, flat = scratch_of(shapes, total)
    outs = pl.pallas_call(
        functools.partial(
            unpack_kernel, shapes, half_rows, piece_count, len(sources), relative
        ),
        out_shape=[jax.ShapeDtypeStruct(m[1:], jnp.float32) for m in matrices]
        + [jax.ShapeDtypeStruct((slots, SMALL), jnp.float32)],
        in_specs=[pl.BlockSpec(memory_space=pltpu.SMEM)] + [any_spec] * len(sources),
        out_specs=[any_spec] * len(matrices) + [pl.BlockSpec(memory_space=pltpu.VMEM)],
        scratch_shapes=[
            flat,
            wide,
            pltpu.SemaphoreType.DMA((piece_count,)),
            pltpu.SemaphoreType.DMA((SLOTS,)),
        ],
        compiler_params=pltpu.CompilerParams(vmem_limit_bytes=VMEM_LIMIT),
        cost_estimate=pl.CostEstimate(
            flops=0, bytes_accessed=8 * total * LANES, transcendentals=0
        ),
    )(index, *sources)
    small = outs[-1]
    pieces, matrix_at, vector_at = [], 0, 0
    for shape in shapes:
        if len(shape) == 2:
            pieces.append(outs[matrix_at])
            matrix_at += 1
        else:
            pieces.append(small[vector_at, : shape[0]])
            vector_at += 1
    return pieces


def scratch_of(shapes, total):
    blocks = plan(shapes)
    wide = pltpu.VMEM(
        (SLOTS, max(b[2] for b in blocks), max(b[3] for b in blocks)), jnp.float32
    )
    return wide, pltpu.VMEM((-(-total // 8) * 8, LANES), jnp.float32)


def pack_kernel(shapes, half_rows, piece_count, relative, *refs):
    matrices, vectors, used = row_layout(shapes)
    index_ref = refs[0]
    ins = refs[1 : 1 + len(matrices)]
    small_ref, tail_ref = refs[1 + len(matrices) : 3 + len(matrices)]
    outs = refs[3 + len(matrices) : -4]
    lin, stage, in_sem, out_sem = refs[-4:]
    me, core = index_ref[0], index_ref[1]
    tail_rows = tail_ref.shape[0]
    blocks = plan(shapes)

    def copy_in(number):
        at, first, size, columns, _ = blocks[number]
        slot = number % SLOTS
        return pltpu.make_async_copy(
            ins[at].at[pl.ds(first, size)],
            stage_view(stage, slot, size, columns),
            in_sem.at[slot],
        )

    for number in range(min(SLOTS - 1, len(blocks))):
        copy_in(number).start()

    for i, (row, count) in enumerate(vectors):
        for t in range(count):
            lin[row + t : row + t + 1, :] = small_ref[i : i + 1, t * LANES : (t + 1) * LANES]
    total = piece_count * half_rows
    if total > used:
        lin[used:total, :] = jnp.zeros((total - used, LANES), jnp.float32)

    def copies(place, target):
        return (
            pltpu.make_async_copy(
                lin.at[pl.ds(place * half_rows, half_rows)],
                target.at[pl.ds(0, half_rows)],
                out_sem.at[place, 0],
            ),
            pltpu.make_async_copy(
                tail_ref, target.at[pl.ds(half_rows, tail_rows)], out_sem.at[place, 1]
            ),
        )

    def send_piece(place):
        def start(target):
            for copy in copies(place, target):
                copy.start()

        if not relative:
            start(outs[0].at[place])
            return
        j = jnp.bitwise_xor(me, place // 2)
        within = lax.rem(j, 4) * 2 + lax.rem(lax.div(j, 4), 2)
        away = jnp.where(core == place % 2, 0, 2)
        corner = jnp.where(within < 6, 0, 1)
        target = lax.div(j, 8) * 4 + away + corner
        for number, out in enumerate(outs):

            @pl.when(target == number)
            def _(out=out, number=number):
                start(out.at[within - 6 if number % 2 else within])

    sent = 0
    for number, (at, first, size, columns, base) in enumerate(blocks):
        if number + SLOTS - 1 < len(blocks):
            copy_in(number + SLOTS - 1).start()
        copy_in(number).wait()
        move_block(lin, stage, number % SLOTS, size, columns, base, False)
        done = base + size * (columns // LANES)
        if number == len(blocks) - 1:
            done = total
        while (sent + 1) * half_rows <= done and sent < piece_count:
            send_piece(sent)
            sent += 1
    for place in range(piece_count):
        for copy in copies(place, outs[0].at[0]):
            copy.wait()


def padded_rows(half_rows, tail_rows):
    return -(-(half_rows + tail_rows) // 8) * 8


def pack(index, grads, tail, shapes, piece_count, half_rows, relative):
    matrices, vectors, _ = row_layout(shapes)
    padded = padded_rows(half_rows, tail.shape[0])
    tail = jnp.pad(tail, ((0, padded - half_rows - tail.shape[0]), (0, 0)))
    slots = -(-len(vectors) // 8) * 8
    mats = [g for g, s in zip(grads, shapes) if len(s) == 2]
    vecs = [jnp.pad(g, (0, SMALL - g.shape[0])) for g, s in zip(grads, shapes) if len(s) == 1]
    vecs += [jnp.zeros((SMALL,), jnp.float32)] * (slots - len(vecs))
    any_spec = pl.BlockSpec(memory_space=pltpu.HBM)
    vmem_spec = pl.BlockSpec(memory_space=pltpu.VMEM)
    total = piece_count * half_rows
    wide, flat = scratch_of(shapes, total)
    if relative:
        sizes = [6, 2, 6, 2] * (piece_count // 16)
    else:
        sizes = [piece_count]
    return pl.pallas_call(
        functools.partial(pack_kernel, shapes, half_rows, piece_count, relative),
        out_shape=[jax.ShapeDtypeStruct((n, padded, LANES), jnp.float32) for n in sizes],
        in_specs=[pl.BlockSpec(memory_space=pltpu.SMEM)]
        + [any_spec] * len(matrices)
        + [vmem_spec] * 2,
        out_specs=[any_spec] * len(sizes),
        scratch_shapes=[
            flat,
            wide,
            pltpu.SemaphoreType.DMA((SLOTS,)),
            pltpu.SemaphoreType.DMA((piece_count, 2)),
        ],
        compiler_params=pltpu.CompilerParams(vmem_limit_bytes=VMEM_LIMIT),
        cost_estimate=pl.CostEstimate(
            flops=0, bytes_accessed=8 * total * LANES, transcendentals=0
        ),
    )(index, *mats, jnp.stack(vecs), tail)


QUADS = FRAMES * GRID
GROUP = LANES // PATCH
STARTS = tuple(range(0, QUADS - 7, 8)) + ((QUADS - 8,) if QUADS % 8 else ())


def patch_kernel(mean_ref, inverse_ref, pixel_ref, patch_ref, moment_ref, scratch):
    band = pl.program_id(0)
    mean, inverse = mean_ref[band], inverse_ref[band]
    group = lax.broadcasted_iota(jnp.int32, (8, LANES), 1) // PATCH

    def sums(i, carry):
        one, two = carry
        value = pixel_ref[0, pl.ds(pl.multiple_of(i * 8, 8), 8), :]
        return one + value, two + value * value

    zero = jnp.zeros((8, LANES), jnp.float32)
    one, two = lax.fori_loop(0, pixel_ref.shape[1] // 8, sums, (zero, zero), unroll=7)
    moment_ref[0, 0] = one
    moment_ref[0, 1] = two
    for side in range(2):
        for first in STARTS:
            rows = []
            for k in range(GRID):
                start = 2 * GRID * first + GRID * side + k
                raw = pixel_ref[0, pl.ds(start, 8, stride=2 * GRID), :]
                rows.append((raw - mean) * inverse)
            for column in range(GRID):
                out = None
                for line in range(GROUP):
                    place = GRID * line + column
                    moved = pltpu.roll(rows[place // GROUP], PATCH * ((line - place) % GROUP), 1)
                    out = moved if out is None else jnp.where(group == line, moved, out)
                scratch[pl.ds(GRID * first + column, 8, stride=GRID), :] = out
        patch_ref[:, side * LANES : (side + 1) * LANES] = scratch[...]


def patchify(pixels, mean, inverse):
    rows = QUADS * 2 * GRID
    smem = pl.BlockSpec(memory_space=pltpu.SMEM)
    patches, moments = pl.pallas_call(
        patch_kernel,
        grid=(BANDS,),
        out_shape=[
            jax.ShapeDtypeStruct((TOK_ITEM, PIX), jnp.float32),
            jax.ShapeDtypeStruct((BANDS, 2, 8, LANES), jnp.float32),
        ],
        in_specs=[smem, smem, pl.BlockSpec((1, rows, LANES), lambda b: (b, 0, 0))],
        out_specs=[
            pl.BlockSpec((TOK_ITEM, 2 * LANES), lambda b: (0, b)),
            pl.BlockSpec((1, 2, 8, LANES), lambda b: (b, 0, 0, 0)),
        ],
        scratch_shapes=[pltpu.VMEM((TOK_ITEM, LANES), jnp.float32)],
        cost_estimate=pl.CostEstimate(
            flops=0, bytes_accessed=16 * TOK_ITEM * PIX, transcendentals=0
        ),
    )(mean, inverse, pixels.reshape(BANDS, rows, LANES))
    return patches, jnp.sum(moments, axis=(2, 3))


def pixel_kernel(inverse_ref, patch_ref, pixel_ref, scratch):
    inverse = inverse_ref[pl.program_id(0)]
    group = lax.broadcasted_iota(jnp.int32, (8, LANES), 1) // PATCH
    for side in range(2):
        scratch[...] = patch_ref[:, side * LANES : (side + 1) * LANES] * inverse
        for first in STARTS:
            columns = [
                scratch[pl.ds(GRID * first + column, 8, stride=GRID), :] for column in range(GRID)
            ]
            for k in range(GRID):
                out = None
                for slot in range(GROUP):
                    line, column = divmod(GROUP * k + slot, GRID)
                    moved = pltpu.roll(columns[column], PATCH * ((slot - line) % GROUP), 1)
                    out = moved if out is None else jnp.where(group == slot, moved, out)
                start = 2 * GRID * first + GRID * side + k
                pixel_ref[0, pl.ds(start, 8, stride=2 * GRID), :] = out


def unpatchify(grad_patches, inverse):
    rows = QUADS * 2 * GRID
    return pl.pallas_call(
        pixel_kernel,
        grid=(BANDS,),
        out_shape=jax.ShapeDtypeStruct((BANDS, rows, LANES), jnp.float32),
        in_specs=[
            pl.BlockSpec(memory_space=pltpu.SMEM),
            pl.BlockSpec((TOK_ITEM, 2 * LANES), lambda b: (0, b)),
        ],
        out_specs=pl.BlockSpec((1, rows, LANES), lambda b: (b, 0, 0)),
        scratch_shapes=[pltpu.VMEM((TOK_ITEM, LANES), jnp.float32)],
        cost_estimate=pl.CostEstimate(
            flops=0, bytes_accessed=16 * TOK_ITEM * PIX, transcendentals=0
        ),
    )(inverse, grad_patches)


def swap(value, distance, count):
    return lax.ppermute(value, "fsdp", [(i, i ^ distance) for i in range(count)])


def swap_cores(value):
    return lax.ppermute(value, "dp", [(0, 1), (1, 0)])


def split_row(rows):
    return rows // 16 * 8


class Scatter:
    def __init__(self, packed, count):
        self.count, self.groups = count, len(packed) // 4
        self.middle = split_row(packed[0].shape[1])
        self.keep_sides, self.keep_corners = packed[::4], packed[1::4]
        self.sides, self.corners = packed[2::4], packed[3::4]
        self.time = -1
        self.pending = {}
        self.own = {}
        self.landed = []

    def hold(self, value):
        value, self.pending = lax.optimization_barrier((value, self.pending))
        return value

    def step(self):
        count, groups, middle = self.count, self.groups, self.middle
        arrived, sent = self.pending, {}
        last, ready, new = groups + 1 - self.time, groups - self.time, groups - 1 - self.time
        if "turned" in arrived:
            near, turned = arrived["turned"]
            self.landed.append(swap(near + turned, 8 * (last + 1), count))
        if 0 <= last < groups:
            along_x, along_y = arrived["sides"]
            part = self.own[last] + along_x + along_y
            turned = swap(part[1], 4, count)
            if last:
                sent["turned"] = (part[0], turned)
            else:
                self.landed += [part[0], turned]
        if 0 <= ready < groups:
            first, second = arrived["corner"]
            own, for_x, for_y = [
                (self.keep_sides[ready] + arrived["core sides"])[2 * i : 2 * i + 2] for i in range(3)
            ]
            self.own[ready] = own
            for_x = jnp.concatenate([for_x[:, :middle] + first, for_x[:, middle:]], axis=1)
            for_y = jnp.concatenate([for_y[:, :middle], for_y[:, middle:] + second], axis=1)
            sent["sides"] = [swap(for_x, 1, count), swap(for_y, 2, count)]
        if 0 <= new < groups:
            corner = self.keep_corners[new] + arrived["core corner"]
            sent["corner"] = [
                swap(corner[:, :middle], 2, count),
                swap(corner[:, middle:], 1, count),
            ]
            sides, _ = lax.optimization_barrier((self.sides[new], corner))
            sent["core sides"] = swap_cores(sides)
        if 0 <= new - 1 < groups:
            sent["core corner"] = swap_cores(self.corners[new - 1])
        self.pending = sent
        self.time += 1

    def total(self):
        while self.time < self.groups + 2:
            self.step()
        return functools.reduce(jnp.add, self.landed)


def both_halves(half, rows, core):
    got = swap_cores(half)
    low = jnp.where(core == 0, half, got)[:rows]
    high = jnp.where(core == 0, got, half)[:rows]
    return jnp.concatenate([low, high]).reshape(-1)


def sincos_part(width, positions):
    frequency = 1.0 / 10000.0 ** (jnp.arange(width // 2).astype(jnp.float32) / (width / 2.0))
    angles = positions[:, None] * frequency[None, :]
    return jnp.concatenate([jnp.sin(angles), jnp.cos(angles)], axis=1)


def position_table(width):
    token_ids = jnp.arange(TOK_ITEM)
    frame_pos = (token_ids // (GRID * GRID)).astype(jnp.float32)
    row_pos = (token_ids // GRID % GRID).astype(jnp.float32)
    column_pos = (token_ids % GRID).astype(jnp.float32)
    return jnp.concatenate(
        [
            sincos_part(width // 16 * 4, frame_pos),
            sincos_part(width // 16 * 6, row_pos),
            sincos_part(width // 16 * 6, column_pos),
        ],
        axis=1,
    )


def layer_norm(values, gain, shift):
    centre = jnp.mean(values, axis=-1, keepdims=True)
    spread = jnp.mean(jnp.square(values - centre), axis=-1, keepdims=True)
    return (values - centre) * lax.rsqrt(spread + EPS_NORM) * gain + shift


QUERY_CHUNK = 640
KEY_CHUNK = 384


def split_two(value):
    high = value.astype(jnp.bfloat16)
    return high, (value - high.astype(jnp.float32)).astype(jnp.bfloat16)


def nt(left, right):
    return lax.dot_general(
        left, right, (((1,), (1,)), ((), ())), preferred_element_type=jnp.float32
    )


def nn(left, right):
    return jnp.dot(left, right, preferred_element_type=jnp.float32)


def chunks(rows, size):
    return [(at, min(size, rows - at)) for at in range(0, rows, size)]


def put_parts(ref, value, order):
    parts = split_two(value)
    for i, which in enumerate(order):
        ref[:, i * LANES : (i + 1) * LANES] = parts[which]


def put_turned(ref, value, size):
    for i, part in enumerate(split_two(value)):
        turned = part.astype(jnp.float32).T.astype(jnp.bfloat16)
        for head in range(LANES // size):
            ref[head, i * size : (i + 1) * size, :] = turned[head * size : (head + 1) * size, :]


def own_lanes(head, size, width):
    lane = lax.broadcasted_iota(jnp.int32, (1, width), 1)
    return (lax.rem(lane, LANES) // size == head).astype(jnp.float32).astype(jnp.bfloat16)


def hide_dead(scores, first, keep):
    if keep is None:
        return scores
    key = lax.broadcasted_iota(jnp.int32, scores.shape, 0) + first
    return jnp.where(key < keep, scores, MASKED_SCORE)


def turned_product(parts, high, low, size):
    both = nn(parts, high)
    return both[:size] + both[size:] + nn(parts[:size], low)


def attend_kernel(size, masked, keep_ref, q_ref, k_ref, v_ref, out_ref, lse_ref, q3, k3, v2t, out_t):
    head = pl.program_id(1)
    keep = keep_ref[0] if masked else None

    @pl.when(head == 0)
    def _():
        put_parts(q3, q_ref[...] * (1.0 / math.sqrt(size)), (0, 1, 0))
        put_parts(k3, k_ref[...], (0, 0, 1))
        put_turned(v2t, v_ref[...], size)

    lanes = own_lanes(head, size, 3 * LANES)
    values = v2t[head]
    for at, count in chunks(q_ref.shape[0], QUERY_CHUNK):
        place = slice(at, at + count)
        scores = hide_dead(nt(k3[...], q3[place, :] * lanes), 0, keep)
        top = jnp.max(scores, axis=0, keepdims=True)
        weights = jnp.exp(scores - top)
        total = jnp.sum(weights, axis=0, keepdims=True)
        high, low = split_two(weights)
        mixed = turned_product(values, high, low, size) / total
        out_t[pl.ds(pl.multiple_of(head * size, size), size), place] = mixed
        lse_ref[0, :, place] = top + jnp.log(total)

    @pl.when(head == LANES // size - 1)
    def _():
        out_ref[...] = out_t[...].T


def attend_forward(joined, keep, heads):
    rows, width = joined.shape[0], joined.shape[1] // 3
    size = width // heads
    blocks, per_block = width // LANES, LANES // size
    masked = keep is not None
    keep = keep if masked else jnp.zeros((1,), jnp.int32)

    def columns(first):
        return pl.BlockSpec((rows, LANES), lambda g, h: (0, first + g))

    return pl.pallas_call(
        functools.partial(attend_kernel, size, masked),
        grid=(blocks, per_block),
        out_shape=[
            jax.ShapeDtypeStruct((rows, width), jnp.float32),
            jax.ShapeDtypeStruct((heads, 1, rows), jnp.float32),
        ],
        in_specs=[
            pl.BlockSpec(memory_space=pltpu.SMEM),
            columns(0),
            columns(blocks),
            columns(2 * blocks),
        ],
        out_specs=[
            columns(0),
            pl.BlockSpec((1, 1, rows), lambda g, h: (g * per_block + h, 0, 0)),
        ],
        scratch_shapes=[
            pltpu.VMEM((rows, 3 * LANES), jnp.bfloat16),
            pltpu.VMEM((rows, 3 * LANES), jnp.bfloat16),
            pltpu.VMEM((per_block, 2 * size, rows), jnp.bfloat16),
            pltpu.VMEM((LANES, rows), jnp.float32),
        ],
        compiler_params=pltpu.CompilerParams(vmem_limit_bytes=VMEM_LIMIT),
        cost_estimate=pl.CostEstimate(
            flops=16 * rows * rows * width,
            bytes_accessed=16 * rows * width,
            transcendentals=heads * rows * rows,
        ),
    )(keep, joined, joined, joined)


def attend_back_kernel(
    size, masked, keep_ref, q_ref, k_ref, v_ref, g_ref, lse_ref, delta_ref, out_ref,
    q3, k3, v3, g3, q3m, g3m, k2t, dq_t, dq, dk, dv, sem,
):
    block, head = pl.program_id(0), pl.program_id(1)
    keep = keep_ref[0] if masked else None
    scale = 1.0 / math.sqrt(size)
    width = out_ref.shape[1] // 3

    @pl.when(head == 0)
    def _():
        put_parts(q3, q_ref[...] * scale, (0, 1, 0))
        put_parts(k3, k_ref[...], (0, 0, 1))
        put_parts(v3, v_ref[...], (0, 0, 1))
        put_parts(g3, g_ref[...], (0, 1, 0))
        put_turned(k2t, k_ref[...], size)
        dk[...] = jnp.zeros_like(dk)
        dv[...] = jnp.zeros_like(dv)

    lanes = own_lanes(head, size, 3 * LANES)
    q3m[...] = q3[...] * lanes
    g3m[...] = g3[...] * lanes
    lse, delta = lse_ref[0], delta_ref[0]
    turned = None
    for at, count in chunks(q_ref.shape[0], KEY_CHUNK):
        place = slice(at, at + count)
        scores = hide_dead(nt(k3[place, :], q3m[...]), at, keep)
        weights = jnp.exp(scores - lse)
        high, low = split_two(weights)
        both = nn(high, g3m[:, : 2 * LANES])
        dv[place, :] += both[:, :LANES] + both[:, LANES:] + nn(low, g3m[:, :LANES])
        change = weights * (nt(v3[place, :], g3m[...]) - delta)
        high, low = split_two(change)
        both = nn(high, q3m[:, : 2 * LANES])
        dk[place, :] += both[:, :LANES] + both[:, LANES:] + nn(low, q3m[:, :LANES])
        part = turned_product(k2t[head, :, place], high, low, size)
        turned = part if turned is None else turned + part
    dq_t[pl.ds(pl.multiple_of(head * size, size), size), :] = turned

    @pl.when(head == LANES // size - 1)
    def _():
        dq[...] = dq_t[...].T * scale
        copies = [
            pltpu.make_async_copy(
                source,
                out_ref.at[:, pl.ds(pl.multiple_of(i * width + block * LANES, LANES), LANES)],
                sem.at[i],
            )
            for i, source in enumerate((dq, dk, dv))
        ]
        for copy in copies:
            copy.start()
        for copy in copies:
            copy.wait()


def attend_backward(joined, keep, heads, grad, lse, delta):
    rows, width = joined.shape[0], joined.shape[1] // 3
    size = width // heads
    blocks, per_block = width // LANES, LANES // size
    masked = keep is not None
    keep = keep if masked else jnp.zeros((1,), jnp.int32)

    def columns(first):
        return pl.BlockSpec((rows, LANES), lambda g, h: (0, first + g))

    per_head = pl.BlockSpec((1, 1, rows), lambda g, h: (g * per_block + h, 0, 0))
    return pl.pallas_call(
        functools.partial(attend_back_kernel, size, masked),
        grid=(blocks, per_block),
        out_shape=jax.ShapeDtypeStruct((rows, 3 * width), jnp.float32),
        in_specs=[
            pl.BlockSpec(memory_space=pltpu.SMEM),
            columns(0),
            columns(blocks),
            columns(2 * blocks),
            columns(0),
            per_head,
            per_head,
        ],
        out_specs=pl.BlockSpec(memory_space=pltpu.HBM),
        scratch_shapes=[pltpu.VMEM((rows, 3 * LANES), jnp.bfloat16)] * 6
        + [
            pltpu.VMEM((per_block, 2 * size, rows), jnp.bfloat16),
            pltpu.VMEM((LANES, rows), jnp.float32),
        ]
        + [pltpu.VMEM((rows, LANES), jnp.float32)] * 3
        + [pltpu.SemaphoreType.DMA((3,))],
        compiler_params=pltpu.CompilerParams(vmem_limit_bytes=VMEM_LIMIT),
        cost_estimate=pl.CostEstimate(
            flops=40 * rows * rows * width,
            bytes_accessed=28 * rows * width,
            transcendentals=heads * rows * rows,
        ),
    )(keep, joined, joined, joined, grad, lse, delta)


@functools.partial(jax.custom_vjp, nondiff_argnums=(2,))
def attend(joined, keep, heads):
    return attend_forward(joined, keep, heads)[0]


def attend_keep(joined, keep, heads):
    out, lse = attend_forward(joined, keep, heads)
    return out, (joined, keep, out, lse)


def attend_pull(heads, kept, grad):
    joined, keep, out, lse = kept
    width = out.shape[1]
    owner = jnp.arange(width)[None, :] // (width // heads) == jnp.arange(heads)[:, None]
    delta = lax.dot_general(
        owner.astype(jnp.float32),
        grad * out,
        (((1,), (1,)), ((), ())),
        precision=lax.Precision.HIGHEST,
        preferred_element_type=jnp.float32,
    )
    return attend_backward(joined, keep, heads, grad, lse, delta[:, None, :]), None


attend.defvjp(attend_keep, attend_pull)


TAIL = (
    -1.26551223,
    1.00002368,
    0.37409196,
    0.09678418,
    -0.18628806,
    0.27886807,
    -1.13520398,
    1.48851587,
    -0.82215223,
    0.17087277,
)


def gelu_parts(value):
    scaled = jnp.abs(value) * math.sqrt(0.5)
    inverse = 1.0 / (1.0 + 0.5 * scaled)
    power = TAIL[-1]
    for factor in TAIL[-2::-1]:
        power = power * inverse + factor
    square = scaled * scaled
    below = 0.5 * inverse * jnp.exp(power - square)
    share = jnp.where(value >= 0.0, 1.0 - below, below)
    slope = share + value * (math.sqrt(0.5 / math.pi) * jnp.exp(-square))
    return value * share, slope


@jax.custom_vjp
def gelu(value):
    return gelu_parts(value)[0]


gelu.defvjp(lambda value: lax.optimization_barrier(gelu_parts(value)), lambda slope, grad: (grad * slope,))


@functools.partial(jax.custom_vjp, nondiff_argnums=(1,))
def mark(value, on_way_back):
    return value


def mark_keep(value, on_way_back):
    return value, None


def mark_pull(on_way_back, kept, grad):
    return (on_way_back(grad),)


mark.defvjp(mark_keep, mark_pull)


def marked(value, marks, number):
    return value if marks is None or marks[number] is None else mark(value, marks[number])


def transformer_block(stream, params, head_count, keep, marks):
    (
        first_gain,
        first_shift,
        qkv_weight,
        query_bias,
        value_bias,
        out_weight,
        out_bias,
        second_gain,
        second_shift,
        up_weight,
        up_bias,
        down_weight,
        down_bias,
    ) = params
    normed = layer_norm(stream, first_gain, first_shift)
    joined = matmul(normed, qkv_weight)
    joined = joined + jnp.concatenate([query_bias, jnp.zeros_like(query_bias), value_bias])
    mixed = marked(attend(marked(joined, marks, 3), keep, head_count), marks, 2)
    stream = marked(stream + matmul(mixed, out_weight) + out_bias, marks, 1)
    normed = layer_norm(stream, second_gain, second_shift)
    before = marked(matmul(normed, up_weight) + up_bias, marks, 0)
    hidden = gelu(before)
    return stream + matmul(hidden, down_weight) + down_bias


def encode_item(encoder, patch_one, places, chosen, keep_one, marks):
    visible = jnp.take(patch_one, chosen, axis=0)
    stream = matmul(visible, encoder[0]) + encoder[1] + places
    stream = transformer_block(stream, encoder[2:15], HEADS_E, keep_one[None], marks)
    return layer_norm(stream, encoder[15], encoder[16])


def decode_item(decoder, encoded, patch_one, table, chosen, keep_one):
    slots = jnp.arange(KEEP_MAX)
    live = (slots < keep_one).astype(jnp.float32)
    token_ids = jnp.arange(TOK_ITEM)
    placer = (chosen[:, None] == token_ids[None, :]).astype(jnp.float32) * live[:, None]
    hidden_mask = 1.0 - jnp.sum(placer, axis=0)
    latent = matmul(encoded, decoder[0]) + decoder[1]
    stream = jnp.einsum("st,sd->td", placer, latent, precision=PREC)
    stream = stream + hidden_mask[:, None] * decoder[2][None, :] + table
    stream = transformer_block(stream, decoder[3:16], HEADS_D, None, None)
    normed = layer_norm(stream, decoder[16], decoder[17])
    predicted = matmul(normed, decoder[18]) + decoder[19]
    error = predicted - patch_one
    squared = jnp.sum(hidden_mask[:, None] * error * error)
    return (squared / (PATCH * PATCH), squared)


def body(
    count,
    pixels,
    running_mean,
    running_variance,
    momentum,
    keep_count,
    visible_index,
    encoder_flat,
    decoder_flat,
):
    all_count = 2 * count
    core = lax.axis_index("dp")
    me = lax.axis_index("fsdp")
    index = jnp.stack([me, core]).astype(jnp.int32)
    inverse = lax.rsqrt(running_variance + EPS_NORM)
    chosen, keep_one = visible_index[0], keep_count[0]

    def own_half(flat):
        rows = flat.shape[0] // (2 * LANES)
        half = lax.dynamic_index_in_dim(flat.reshape(2, rows, LANES), core, 0, keepdims=False)
        return jnp.pad(half, ((0, -rows % 8), (0, 0))), rows

    encoder_half, encoder_rows = own_half(encoder_flat)
    decoder_half, decoder_rows = own_half(decoder_flat)
    encoder_all = lax.all_gather(encoder_half, ("fsdp", "dp"), axis=0, tiled=False)
    patches, moments = patchify(pixels[0], running_mean, inverse)
    encoder_all, decoder_half, patches, moments, places, table = lax.optimization_barrier(
        (
            encoder_all,
            decoder_half,
            patches,
            moments,
            jnp.take(position_table(D_ENC), chosen, axis=0),
            position_table(D_DEC),
        )
    )
    decoder_all = lax.all_gather(decoder_half, ("fsdp", "dp"), axis=0, tiled=False)

    scatters = []

    def go_on(grad):
        grad = scatters[0].hold(grad)
        scatters[0].step()
        return grad

    marks = [go_on, None, go_on, None]
    encoder = unpack(index, [encoder_all], encoder_rows, all_count, False, encoder_shapes())
    encoded, encode_back = jax.vjp(
        lambda params, patch: encode_item(params, patch, places, chosen, keep_one, marks),
        encoder,
        patches,
    )
    decoder = unpack(index, [decoder_all], decoder_rows, all_count, False, decoder_shapes())
    objective, decode_back, squared = jax.vjp(
        lambda params, enc, patch: decode_item(params, enc, patch, table, chosen, keep_one),
        decoder,
        encoded,
        patches,
        has_aux=True,
    )
    grad_decoder, grad_encoded, grad_patches = decode_back(jnp.ones((), jnp.float32))
    masked_here = (TOK_ITEM - keep_one).astype(jnp.float32)
    stats = jnp.concatenate([moments[:, 0], moments[:, 1], jnp.stack([squared, masked_here])])
    place = jnp.arange(all_count)[:, None] == core * count + me
    tail = jnp.where(place, jnp.pad(stats, (0, 16 - stats.shape[0]))[None, :], 0.0)
    tail = tail.reshape(-1, LANES)
    packed = pack(
        index, grad_decoder, tail, decoder_shapes(), all_count, decoder_rows, True
    )
    scatters.append(Scatter(packed, count))
    scatters[0].step()
    grad_encoder, more_patches = encode_back(grad_encoded)
    grad_encoder = go_on(grad_encoder)

    packed = pack(
        index, grad_encoder, tail, encoder_shapes(), all_count, encoder_rows, True
    )
    packed = go_on(packed)
    decoder_sum = scatters[0].total()
    encoder_scatter = Scatter(packed, count)
    for _ in range(2):
        encoder_scatter.step()
    pixel_grad = unpatchify(grad_patches + more_patches, inverse)
    pixel_grad = encoder_scatter.hold(pixel_grad).reshape(pixels.shape)
    encoder_sum = encoder_scatter.total()
    totals = encoder_sum[encoder_rows : encoder_rows + tail.shape[0]].reshape(all_count, 16)
    totals = jnp.sum(totals, axis=0)

    pixel_count = float(all_count * FRAMES * IMG * IMG)
    band_mean = totals[:BANDS] / pixel_count
    band_var = totals[BANDS : 2 * BANDS] / pixel_count - band_mean * band_mean
    next_mean = (1.0 - momentum) * running_mean + momentum * band_mean
    next_variance = (1.0 - momentum) * running_variance + momentum * band_var
    masked_loss = totals[2 * BANDS] / (totals[2 * BANDS + 1] * PIX)
    return (
        masked_loss,
        pixel_grad,
        both_halves(encoder_sum, encoder_rows, core),
        both_halves(decoder_sum, decoder_rows, core),
        next_mean,
        next_variance,
    )


def solution(mesh):
    placed = (
        P(("dp", "fsdp"), None, None, None),
        P(),
        P(),
        P(),
        P(("dp", "fsdp")),
        P(("dp", "fsdp"), None),
        P("fsdp"),
        P("fsdp"),
    )
    return jax.shard_map(
        functools.partial(body, mesh.shape["fsdp"]),
        mesh=mesh,
        in_specs=placed,
        out_specs=(P(), P(("dp", "fsdp"), None, None, None), P("fsdp"), P("fsdp"), P(), P()),
        check_vma=False,
    )
```

```python
import functools
import math

import jax
import jax.numpy as jnp
from jax import lax
from jax.experimental import pallas as pl
from jax.experimental.pallas import tpu as pltpu
from jax.sharding import PartitionSpec as P

D_ENC = 768
HEADS_E = 12
MLP_E = 3072
D_DEC = 512
HEADS_D = 16
MLP_D = 2048
BANDS = 6
PATCH = 16
FRAMES = 3
GRID = 14
TOK_ITEM = 588
IMG = 224
PIX = 1536
KEEP_MAX = 236
LANES = 128
SMALL = 3072

EPS_NORM = 1e-06
MASKED_SCORE = -1e30
PREC = lax.Precision.HIGH
VMEM_LIMIT = 60 * 2**20


def matmul(left, right):
    return jnp.dot(left, right, precision=PREC, preferred_element_type=jnp.float32)


def block_shapes(width, hidden):
    return [
        (width,),
        (width,),
        (width, 3 * width),
        (width,),
        (width,),
        (width, width),
        (width,),
        (width,),
        (width,),
        (width, hidden),
        (hidden,),
        (hidden, width),
        (width,),
    ]


def encoder_shapes():
    return [(PIX, D_ENC), (D_ENC,)] + block_shapes(D_ENC, MLP_E) + [(D_ENC,), (D_ENC,)]


def decoder_shapes():
    return (
        [(D_ENC, D_DEC), (D_DEC,), (D_DEC,)]
        + block_shapes(D_DEC, MLP_D)
        + [(D_DEC,), (D_DEC,), (D_DEC, PIX), (PIX,)]
    )


def row_layout(shapes):
    matrices, vectors, row = [], [], 0
    for shape in shapes:
        if len(shape) == 2:
            matrices.append((row, shape[0], shape[1]))
        else:
            vectors.append((row, shape[0] // LANES))
        row += math.prod(shape) // LANES
    return matrices, vectors, row


SLOTS = 4
STAGE = 393216


def plan(shapes):
    blocks = []
    for at, (row, rows, columns) in enumerate(row_layout(shapes)[0]):
        size = max(r for r in range(8, rows + 1, 8) if rows % r == 0 and r * columns <= STAGE)
        for first in range(0, rows, size):
            blocks.append((at, first, size, columns, row + first * (columns // LANES)))
    return blocks


def stage_view(stage, slot, size, columns):
    return stage.at[slot, pl.ds(0, size), pl.ds(0, columns)]


def move_block(lin, stage, slot, size, columns, base, inward):
    tiles = columns // LANES
    groups = size // 8
    unroll = max(u for u in range(1, 9) if groups % u == 0 and u * tiles <= 48)

    def some(r, carry):
        for u in range(unroll):
            at = r * unroll + u
            for t in range(tiles):
                rows = pl.ds(base + at * (8 * tiles) + t, 8, stride=tiles)
                place = pl.ds(pl.multiple_of(at * 8, 8), 8)
                if inward:
                    stage[slot, place, t * LANES : (t + 1) * LANES] = lin[rows, :]
                else:
                    lin[rows, :] = stage[slot, place, t * LANES : (t + 1) * LANES]
        return carry

    lax.fori_loop(0, groups // unroll, some, 0)


def unpack_kernel(shapes, half_rows, piece_count, sources, relative, *refs):
    matrices, vectors, used = row_layout(shapes)
    index_ref = refs[0]
    ins = refs[1 : 1 + sources]
    outs = refs[1 + sources : 1 + sources + len(matrices)]
    small_ref = refs[1 + sources + len(matrices)]
    lin, stage, in_sem, out_sem = refs[2 + sources + len(matrices) :]
    me, core = index_ref[0], index_ref[1]

    def copy_piece(source, place):
        return pltpu.make_async_copy(
            source.at[pl.ds(0, half_rows)],
            lin.at[pl.ds(place * half_rows, half_rows)],
            in_sem.at[place],
        )

    if relative:
        pairs = piece_count // 4
        for side in range(2):
            for j in range(piece_count // 2):
                owner = jnp.bitwise_xor(me, j)
                half = core if side == 0 else 1 - core
                group, k, role = j // 8, j // 4 % 2, j % 4
                source = ins[side * (pairs // 4) + group]
                copy_piece(source.at[role * 2 + k], owner * 2 + half).start()
    else:
        for place in range(piece_count):
            copy_piece(ins[0].at[place], place).start()

    arrived = 0

    def wait_for(last, arrived):
        while arrived < piece_count and arrived * half_rows < last:
            copy_piece(ins[0].at[0], arrived).wait()
            arrived += 1
        return arrived

    copies = []
    for number, (at, first, size, columns, base) in enumerate(plan(shapes)):
        arrived = wait_for(base + size * (columns // LANES), arrived)
        slot = number % SLOTS
        if number >= SLOTS:
            copies[number - SLOTS].wait()
        move_block(lin, stage, slot, size, columns, base, True)
        copies.append(
            pltpu.make_async_copy(
                stage_view(stage, slot, size, columns),
                outs[at].at[pl.ds(first, size)],
                out_sem.at[slot],
            )
        )
        copies[-1].start()
    wait_for(piece_count * half_rows, arrived)
    small_ref[...] = jnp.zeros_like(small_ref)
    for i, (row, count) in enumerate(vectors):
        for t in range(count):
            small_ref[i : i + 1, t * LANES : (t + 1) * LANES] = lin[row + t : row + t + 1, :]
    for copy in copies[-SLOTS:]:
        copy.wait()


def unpack(index, sources, half_rows, piece_count, relative, shapes):
    matrices, vectors, _ = row_layout(shapes)
    any_spec = pl.BlockSpec(memory_space=pltpu.HBM)
    slots = -(-len(vectors) // 8) * 8
    total = piece_count * half_rows
    wide, flat = scratch_of(shapes, total)
    outs = pl.pallas_call(
        functools.partial(
            unpack_kernel, shapes, half_rows, piece_count, len(sources), relative
        ),
        out_shape=[jax.ShapeDtypeStruct(m[1:], jnp.float32) for m in matrices]
        + [jax.ShapeDtypeStruct((slots, SMALL), jnp.float32)],
        in_specs=[pl.BlockSpec(memory_space=pltpu.SMEM)] + [any_spec] * len(sources),
        out_specs=[any_spec] * len(matrices) + [pl.BlockSpec(memory_space=pltpu.VMEM)],
        scratch_shapes=[
            flat,
            wide,
            pltpu.SemaphoreType.DMA((piece_count,)),
            pltpu.SemaphoreType.DMA((SLOTS,)),
        ],
        compiler_params=pltpu.CompilerParams(vmem_limit_bytes=VMEM_LIMIT),
        cost_estimate=pl.CostEstimate(
            flops=0, bytes_accessed=8 * total * LANES, transcendentals=0
        ),
    )(index, *sources)
    small = outs[-1]
    pieces, matrix_at, vector_at = [], 0, 0
    for shape in shapes:
        if len(shape) == 2:
            pieces.append(outs[matrix_at])
            matrix_at += 1
        else:
            pieces.append(small[vector_at, : shape[0]])
            vector_at += 1
    return pieces


def scratch_of(shapes, total):
    blocks = plan(shapes)
    wide = pltpu.VMEM(
        (SLOTS, max(b[2] for b in blocks), max(b[3] for b in blocks)), jnp.float32
    )
    return wide, pltpu.VMEM((-(-total // 8) * 8, LANES), jnp.float32)


def pack_kernel(shapes, half_rows, piece_count, relative, *refs):
    matrices, vectors, used = row_layout(shapes)
    index_ref = refs[0]
    ins = refs[1 : 1 + len(matrices)]
    small_ref, tail_ref = refs[1 + len(matrices) : 3 + len(matrices)]
    outs = refs[3 + len(matrices) : -4]
    lin, stage, in_sem, out_sem = refs[-4:]
    me, core = index_ref[0], index_ref[1]
    tail_rows = tail_ref.shape[0]
    blocks = plan(shapes)

    def copy_in(number):
        at, first, size, columns, _ = blocks[number]
        slot = number % SLOTS
        return pltpu.make_async_copy(
            ins[at].at[pl.ds(first, size)],
            stage_view(stage, slot, size, columns),
            in_sem.at[slot],
        )

    for number in range(min(SLOTS - 1, len(blocks))):
        copy_in(number).start()

    for i, (row, count) in enumerate(vectors):
        for t in range(count):
            lin[row + t : row + t + 1, :] = small_ref[i : i + 1, t * LANES : (t + 1) * LANES]
    total = piece_count * half_rows
    if total > used:
        lin[used:total, :] = jnp.zeros((total - used, LANES), jnp.float32)

    def copies(place, target):
        return (
            pltpu.make_async_copy(
                lin.at[pl.ds(place * half_rows, half_rows)],
                target.at[pl.ds(0, half_rows)],
                out_sem.at[place, 0],
            ),
            pltpu.make_async_copy(
                tail_ref, target.at[pl.ds(half_rows, tail_rows)], out_sem.at[place, 1]
            ),
        )

    def send_piece(place):
        def start(target):
            for copy in copies(place, target):
                copy.start()

        if not relative:
            start(outs[0].at[place])
            return
        j = jnp.bitwise_xor(me, place // 2)
        within = lax.rem(j, 4) * 2 + lax.rem(lax.div(j, 4), 2)
        away = jnp.where(core == place % 2, 0, 2)
        corner = jnp.where(within < 6, 0, 1)
        target = lax.div(j, 8) * 4 + away + corner
        for number, out in enumerate(outs):

            @pl.when(target == number)
            def _(out=out, number=number):
                start(out.at[within - 6 if number % 2 else within])

    sent = 0
    for number, (at, first, size, columns, base) in enumerate(blocks):
        if number + SLOTS - 1 < len(blocks):
            copy_in(number + SLOTS - 1).start()
        copy_in(number).wait()
        move_block(lin, stage, number % SLOTS, size, columns, base, False)
        done = base + size * (columns // LANES)
        if number == len(blocks) - 1:
            done = total
        while (sent + 1) * half_rows <= done and sent < piece_count:
            send_piece(sent)
            sent += 1
    for place in range(piece_count):
        for copy in copies(place, outs[0].at[0]):
            copy.wait()


def padded_rows(half_rows, tail_rows):
    return -(-(half_rows + tail_rows) // 8) * 8


def pack(index, grads, tail, shapes, piece_count, half_rows, relative):
    matrices, vectors, _ = row_layout(shapes)
    padded = padded_rows(half_rows, tail.shape[0])
    tail = jnp.pad(tail, ((0, padded - half_rows - tail.shape[0]), (0, 0)))
    slots = -(-len(vectors) // 8) * 8
    mats = [g for g, s in zip(grads, shapes) if len(s) == 2]
    vecs = [jnp.pad(g, (0, SMALL - g.shape[0])) for g, s in zip(grads, shapes) if len(s) == 1]
    vecs += [jnp.zeros((SMALL,), jnp.float32)] * (slots - len(vecs))
    any_spec = pl.BlockSpec(memory_space=pltpu.HBM)
    vmem_spec = pl.BlockSpec(memory_space=pltpu.VMEM)
    total = piece_count * half_rows
    wide, flat = scratch_of(shapes, total)
    if relative:
        sizes = [6, 2, 6, 2] * (piece_count // 16)
    else:
        sizes = [piece_count]
    return pl.pallas_call(
        functools.partial(pack_kernel, shapes, half_rows, piece_count, relative),
        out_shape=[jax.ShapeDtypeStruct((n, padded, LANES), jnp.float32) for n in sizes],
        in_specs=[pl.BlockSpec(memory_space=pltpu.SMEM)]
        + [any_spec] * len(matrices)
        + [vmem_spec] * 2,
        out_specs=[any_spec] * len(sizes),
        scratch_shapes=[
            flat,
            wide,
            pltpu.SemaphoreType.DMA((SLOTS,)),
            pltpu.SemaphoreType.DMA((piece_count, 2)),
        ],
        compiler_params=pltpu.CompilerParams(vmem_limit_bytes=VMEM_LIMIT),
        cost_estimate=pl.CostEstimate(
            flops=0, bytes_accessed=8 * total * LANES, transcendentals=0
        ),
    )(index, *mats, jnp.stack(vecs), tail)


QUADS = FRAMES * GRID
GROUP = LANES // PATCH
STARTS = tuple(range(0, QUADS - 7, 8)) + ((QUADS - 8,) if QUADS % 8 else ())


def patch_kernel(mean_ref, inverse_ref, pixel_ref, patch_ref, moment_ref, scratch):
    band = pl.program_id(0)
    mean, inverse = mean_ref[band], inverse_ref[band]
    group = lax.broadcasted_iota(jnp.int32, (8, LANES), 1) // PATCH

    def sums(i, carry):
        one, two = carry
        value = pixel_ref[0, pl.ds(pl.multiple_of(i * 8, 8), 8), :]
        return one + value, two + value * value

    zero = jnp.zeros((8, LANES), jnp.float32)
    one, two = lax.fori_loop(0, pixel_ref.shape[1] // 8, sums, (zero, zero), unroll=7)
    moment_ref[0, 0] = one
    moment_ref[0, 1] = two
    for side in range(2):
        for first in STARTS:
            rows = []
            for k in range(GRID):
                start = 2 * GRID * first + GRID * side + k
                raw = pixel_ref[0, pl.ds(start, 8, stride=2 * GRID), :]
                rows.append((raw - mean) * inverse)
            for column in range(GRID):
                out = None
                for line in range(GROUP):
                    place = GRID * line + column
                    moved = pltpu.roll(rows[place // GROUP], PATCH * ((line - place) % GROUP), 1)
                    out = moved if out is None else jnp.where(group == line, moved, out)
                scratch[pl.ds(GRID * first + column, 8, stride=GRID), :] = out
        patch_ref[:, side * LANES : (side + 1) * LANES] = scratch[...]


def patchify(pixels, mean, inverse):
    rows = QUADS * 2 * GRID
    smem = pl.BlockSpec(memory_space=pltpu.SMEM)
    patches, moments = pl.pallas_call(
        patch_kernel,
        grid=(BANDS,),
        out_shape=[
            jax.ShapeDtypeStruct((TOK_ITEM, PIX), jnp.float32),
            jax.ShapeDtypeStruct((BANDS, 2, 8, LANES), jnp.float32),
        ],
        in_specs=[smem, smem, pl.BlockSpec((1, rows, LANES), lambda b: (b, 0, 0))],
        out_specs=[
            pl.BlockSpec((TOK_ITEM, 2 * LANES), lambda b: (0, b)),
            pl.BlockSpec((1, 2, 8, LANES), lambda b: (b, 0, 0, 0)),
        ],
        scratch_shapes=[pltpu.VMEM((TOK_ITEM, LANES), jnp.float32)],
        cost_estimate=pl.CostEstimate(
            flops=0, bytes_accessed=16 * TOK_ITEM * PIX, transcendentals=0
        ),
    )(mean, inverse, pixels.reshape(BANDS, rows, LANES))
    return patches, jnp.sum(moments, axis=(2, 3))


def pixel_kernel(inverse_ref, patch_ref, pixel_ref, scratch):
    inverse = inverse_ref[pl.program_id(0)]
    group = lax.broadcasted_iota(jnp.int32, (8, LANES), 1) // PATCH
    for side in range(2):
        scratch[...] = patch_ref[:, side * LANES : (side + 1) * LANES] * inverse
        for first in STARTS:
            columns = [
                scratch[pl.ds(GRID * first + column, 8, stride=GRID), :] for column in range(GRID)
            ]
            for k in range(GRID):
                out = None
                for slot in range(GROUP):
                    line, column = divmod(GROUP * k + slot, GRID)
                    moved = pltpu.roll(columns[column], PATCH * ((slot - line) % GROUP), 1)
                    out = moved if out is None else jnp.where(group == slot, moved, out)
                start = 2 * GRID * first + GRID * side + k
                pixel_ref[0, pl.ds(start, 8, stride=2 * GRID), :] = out


def unpatchify(grad_patches, inverse):
    rows = QUADS * 2 * GRID
    return pl.pallas_call(
        pixel_kernel,
        grid=(BANDS,),
        out_shape=jax.ShapeDtypeStruct((BANDS, rows, LANES), jnp.float32),
        in_specs=[
            pl.BlockSpec(memory_space=pltpu.SMEM),
            pl.BlockSpec((TOK_ITEM, 2 * LANES), lambda b: (0, b)),
        ],
        out_specs=pl.BlockSpec((1, rows, LANES), lambda b: (b, 0, 0)),
        scratch_shapes=[pltpu.VMEM((TOK_ITEM, LANES), jnp.float32)],
        cost_estimate=pl.CostEstimate(
            flops=0, bytes_accessed=16 * TOK_ITEM * PIX, transcendentals=0
        ),
    )(inverse, grad_patches)


def swap(value, distance, count):
    return lax.ppermute(value, "fsdp", [(i, i ^ distance) for i in range(count)])


def swap_cores(value):
    return lax.ppermute(value, "dp", [(0, 1), (1, 0)])


def split_row(rows):
    return rows // 16 * 8


class Scatter:
    def __init__(self, packed, count, fine):
        self.count, self.groups = count, len(packed) // 4
        self.middle = split_row(packed[0].shape[1])
        self.keep_sides, self.keep_corners = packed[::4], packed[1::4]
        self.sides, self.corners = packed[2::4], packed[3::4]
        self.fine = fine
        self.time = -1
        self.pending = {}
        self.own = {}
        self.landed = []

    def hold(self, value):
        value, self.pending = lax.optimization_barrier((value, self.pending))
        return value

    def step(self):
        count, groups, middle = self.count, self.groups, self.middle
        arrived, sent = self.pending, {}
        last, ready, new = groups + 1 - self.time, groups - self.time, groups - 1 - self.time
        if "turned" in arrived:
            near, turned = arrived["turned"]
            self.landed.append(swap(near + turned, 8 * (last + 1), count))
        if "late" in arrived:
            along_x, along_y = arrived["late"]
            self.landed.append(self.own[0][0] + along_x + along_y)
        if last == 0 and self.fine:
            along_x, along_y = arrived["sides"]
            self.landed.append(swap(self.own[0][1] + along_x + along_y, 4, count))
            for_x, for_y = self.late
            sent["late"] = [swap(for_x, 1, count), swap(for_y, 2, count)]
        elif 0 <= last < groups:
            along_x, along_y = arrived["sides"]
            part = self.own[last] + along_x + along_y
            turned = swap(part[1], 4, count)
            if last:
                sent["turned"] = (part[0], turned)
            else:
                self.landed += [part[0], turned]
        if 0 <= ready < groups:
            first, second = arrived["corner"]
            own, for_x, for_y = [
                (self.keep_sides[ready] + arrived["core sides"])[2 * i : 2 * i + 2] for i in range(3)
            ]
            self.own[ready] = own
            for_x = jnp.concatenate([for_x[:, :middle] + first, for_x[:, middle:]], axis=1)
            for_y = jnp.concatenate([for_y[:, :middle], for_y[:, middle:] + second], axis=1)
            if ready == 0 and self.fine:
                self.late = (for_x[0], for_y[0])
                for_x, for_y = for_x[1], for_y[1]
            sent["sides"] = [swap(for_x, 1, count), swap(for_y, 2, count)]
        if 0 <= new < groups:
            corner = self.keep_corners[new] + arrived["core corner"]
            sent["corner"] = [
                swap(corner[:, :middle], 2, count),
                swap(corner[:, middle:], 1, count),
            ]
            sides, _ = lax.optimization_barrier((self.sides[new], corner))
            sent["core sides"] = swap_cores(sides)
        if 0 <= new - 1 < groups:
            sent["core corner"] = swap_cores(self.corners[new - 1])
        self.pending = sent
        self.time += 1

    def total(self):
        while self.time < self.groups + (3 if self.fine else 2):
            self.step()
        return functools.reduce(jnp.add, self.landed)


def both_halves(half, rows, core):
    got = swap_cores(half)
    low = jnp.where(core == 0, half, got)[:rows]
    high = jnp.where(core == 0, got, half)[:rows]
    return jnp.concatenate([low, high]).reshape(-1)


def sincos_part(width, positions):
    frequency = 1.0 / 10000.0 ** (jnp.arange(width // 2).astype(jnp.float32) / (width / 2.0))
    angles = positions[:, None] * frequency[None, :]
    return jnp.concatenate([jnp.sin(angles), jnp.cos(angles)], axis=1)


def position_table(width):
    token_ids = jnp.arange(TOK_ITEM)
    frame_pos = (token_ids // (GRID * GRID)).astype(jnp.float32)
    row_pos = (token_ids // GRID % GRID).astype(jnp.float32)
    column_pos = (token_ids % GRID).astype(jnp.float32)
    return jnp.concatenate(
        [
            sincos_part(width // 16 * 4, frame_pos),
            sincos_part(width // 16 * 6, row_pos),
            sincos_part(width // 16 * 6, column_pos),
        ],
        axis=1,
    )


def layer_norm(values, gain, shift):
    centre = jnp.mean(values, axis=-1, keepdims=True)
    spread = jnp.mean(jnp.square(values - centre), axis=-1, keepdims=True)
    return (values - centre) * lax.rsqrt(spread + EPS_NORM) * gain + shift


QUERY_CHUNK = 640
KEY_CHUNK = 384


def split_two(value):
    high = value.astype(jnp.bfloat16)
    return high, (value - high.astype(jnp.float32)).astype(jnp.bfloat16)


def nt(left, right):
    return lax.dot_general(
        left, right, (((1,), (1,)), ((), ())), preferred_element_type=jnp.float32
    )


def nn(left, right):
    return jnp.dot(left, right, preferred_element_type=jnp.float32)


def chunks(rows, size):
    return [(at, min(size, rows - at)) for at in range(0, rows, size)]


def put_parts(ref, value, order):
    parts = split_two(value)
    for i, which in enumerate(order):
        ref[:, i * LANES : (i + 1) * LANES] = parts[which]


def put_turned(ref, value, size):
    for i, part in enumerate(split_two(value)):
        turned = part.astype(jnp.float32).T.astype(jnp.bfloat16)
        for head in range(LANES // size):
            ref[head, i * size : (i + 1) * size, :] = turned[head * size : (head + 1) * size, :]


def own_lanes(head, size, width):
    lane = lax.broadcasted_iota(jnp.int32, (1, width), 1)
    return (lax.rem(lane, LANES) // size == head).astype(jnp.float32).astype(jnp.bfloat16)


def hide_dead(scores, first, keep):
    if keep is None:
        return scores
    key = lax.broadcasted_iota(jnp.int32, scores.shape, 0) + first
    return jnp.where(key < keep, scores, MASKED_SCORE)


def turned_product(parts, high, low, size):
    both = nn(parts, high)
    return both[:size] + both[size:] + nn(parts[:size], low)


def attend_kernel(size, masked, keep_ref, q_ref, k_ref, v_ref, out_ref, lse_ref, q3, k3, v2t, out_t):
    head = pl.program_id(1)
    keep = keep_ref[0] if masked else None

    @pl.when(head == 0)
    def _():
        put_parts(q3, q_ref[...] * (1.0 / math.sqrt(size)), (0, 1, 0))
        put_parts(k3, k_ref[...], (0, 0, 1))
        put_turned(v2t, v_ref[...], size)

    lanes = own_lanes(head, size, 3 * LANES)
    values = v2t[head]
    for at, count in chunks(q_ref.shape[0], QUERY_CHUNK):
        place = slice(at, at + count)
        scores = hide_dead(nt(k3[...], q3[place, :] * lanes), 0, keep)
        top = jnp.max(scores, axis=0, keepdims=True)
        weights = jnp.exp(scores - top)
        total = jnp.sum(weights, axis=0, keepdims=True)
        high, low = split_two(weights)
        mixed = turned_product(values, high, low, size) / total
        out_t[pl.ds(pl.multiple_of(head * size, size), size), place] = mixed
        lse_ref[0, :, place] = top + jnp.log(total)

    @pl.when(head == LANES // size - 1)
    def _():
        out_ref[...] = out_t[...].T


def attend_forward(joined, keep, heads):
    rows, width = joined.shape[0], joined.shape[1] // 3
    size = width // heads
    blocks, per_block = width // LANES, LANES // size
    masked = keep is not None
    keep = keep if masked else jnp.zeros((1,), jnp.int32)

    def columns(first):
        return pl.BlockSpec((rows, LANES), lambda g, h: (0, first + g))

    return pl.pallas_call(
        functools.partial(attend_kernel, size, masked),
        grid=(blocks, per_block),
        out_shape=[
            jax.ShapeDtypeStruct((rows, width), jnp.float32),
            jax.ShapeDtypeStruct((heads, 1, rows), jnp.float32),
        ],
        in_specs=[
            pl.BlockSpec(memory_space=pltpu.SMEM),
            columns(0),
            columns(blocks),
            columns(2 * blocks),
        ],
        out_specs=[
            columns(0),
            pl.BlockSpec((1, 1, rows), lambda g, h: (g * per_block + h, 0, 0)),
        ],
        scratch_shapes=[
            pltpu.VMEM((rows, 3 * LANES), jnp.bfloat16),
            pltpu.VMEM((rows, 3 * LANES), jnp.bfloat16),
            pltpu.VMEM((per_block, 2 * size, rows), jnp.bfloat16),
            pltpu.VMEM((LANES, rows), jnp.float32),
        ],
        compiler_params=pltpu.CompilerParams(vmem_limit_bytes=VMEM_LIMIT),
        cost_estimate=pl.CostEstimate(
            flops=16 * rows * rows * width,
            bytes_accessed=16 * rows * width,
            transcendentals=heads * rows * rows,
        ),
    )(keep, joined, joined, joined)


def attend_back_kernel(
    size, masked, keep_ref, q_ref, k_ref, v_ref, g_ref, lse_ref, delta_ref, out_ref,
    q3, k3, v3, g3, q3m, g3m, k2t, dq_t, dq, dk, dv, sem,
):
    block, head = pl.program_id(0), pl.program_id(1)
    keep = keep_ref[0] if masked else None
    scale = 1.0 / math.sqrt(size)
    width = out_ref.shape[1] // 3

    @pl.when(head == 0)
    def _():
        put_parts(q3, q_ref[...] * scale, (0, 1, 0))
        put_parts(k3, k_ref[...], (0, 0, 1))
        put_parts(v3, v_ref[...], (0, 0, 1))
        put_parts(g3, g_ref[...], (0, 1, 0))
        put_turned(k2t, k_ref[...], size)
        dk[...] = jnp.zeros_like(dk)
        dv[...] = jnp.zeros_like(dv)

    lanes = own_lanes(head, size, 3 * LANES)
    q3m[...] = q3[...] * lanes
    g3m[...] = g3[...] * lanes
    lse, delta = lse_ref[0], delta_ref[0]
    turned = None
    for at, count in chunks(q_ref.shape[0], KEY_CHUNK):
        place = slice(at, at + count)
        scores = hide_dead(nt(k3[place, :], q3m[...]), at, keep)
        weights = jnp.exp(scores - lse)
        high, low = split_two(weights)
        both = nn(high, g3m[:, : 2 * LANES])
        dv[place, :] += both[:, :LANES] + both[:, LANES:] + nn(low, g3m[:, :LANES])
        change = weights * (nt(v3[place, :], g3m[...]) - delta)
        high, low = split_two(change)
        both = nn(high, q3m[:, : 2 * LANES])
        dk[place, :] += both[:, :LANES] + both[:, LANES:] + nn(low, q3m[:, :LANES])
        part = turned_product(k2t[head, :, place], high, low, size)
        turned = part if turned is None else turned + part
    dq_t[pl.ds(pl.multiple_of(head * size, size), size), :] = turned

    @pl.when(head == LANES // size - 1)
    def _():
        dq[...] = dq_t[...].T * scale
        copies = [
            pltpu.make_async_copy(
                source,
                out_ref.at[:, pl.ds(pl.multiple_of(i * width + block * LANES, LANES), LANES)],
                sem.at[i],
            )
            for i, source in enumerate((dq, dk, dv))
        ]
        for copy in copies:
            copy.start()
        for copy in copies:
            copy.wait()


def attend_backward(joined, keep, heads, grad, lse, delta):
    rows, width = joined.shape[0], joined.shape[1] // 3
    size = width // heads
    blocks, per_block = width // LANES, LANES // size
    masked = keep is not None
    keep = keep if masked else jnp.zeros((1,), jnp.int32)

    def columns(first):
        return pl.BlockSpec((rows, LANES), lambda g, h: (0, first + g))

    per_head = pl.BlockSpec((1, 1, rows), lambda g, h: (g * per_block + h, 0, 0))
    return pl.pallas_call(
        functools.partial(attend_back_kernel, size, masked),
        grid=(blocks, per_block),
        out_shape=jax.ShapeDtypeStruct((rows, 3 * width), jnp.float32),
        in_specs=[
            pl.BlockSpec(memory_space=pltpu.SMEM),
            columns(0),
            columns(blocks),
            columns(2 * blocks),
            columns(0),
            per_head,
            per_head,
        ],
        out_specs=pl.BlockSpec(memory_space=pltpu.HBM),
        scratch_shapes=[pltpu.VMEM((rows, 3 * LANES), jnp.bfloat16)] * 6
        + [
            pltpu.VMEM((per_block, 2 * size, rows), jnp.bfloat16),
            pltpu.VMEM((LANES, rows), jnp.float32),
        ]
        + [pltpu.VMEM((rows, LANES), jnp.float32)] * 3
        + [pltpu.SemaphoreType.DMA((3,))],
        compiler_params=pltpu.CompilerParams(vmem_limit_bytes=VMEM_LIMIT),
        cost_estimate=pl.CostEstimate(
            flops=40 * rows * rows * width,
            bytes_accessed=28 * rows * width,
            transcendentals=heads * rows * rows,
        ),
    )(keep, joined, joined, joined, grad, lse, delta)


@functools.partial(jax.custom_vjp, nondiff_argnums=(2,))
def attend(joined, keep, heads):
    return attend_forward(joined, keep, heads)[0]


def attend_keep(joined, keep, heads):
    out, lse = attend_forward(joined, keep, heads)
    return out, (joined, keep, out, lse)


def attend_pull(heads, kept, grad):
    joined, keep, out, lse = kept
    width = out.shape[1]
    owner = jnp.arange(width)[None, :] // (width // heads) == jnp.arange(heads)[:, None]
    delta = lax.dot_general(
        owner.astype(jnp.float32),
        grad * out,
        (((1,), (1,)), ((), ())),
        precision=lax.Precision.HIGHEST,
        preferred_element_type=jnp.float32,
    )
    return attend_backward(joined, keep, heads, grad, lse, delta[:, None, :]), None


attend.defvjp(attend_keep, attend_pull)


TAIL = (
    -1.26551223,
    1.00002368,
    0.37409196,
    0.09678418,
    -0.18628806,
    0.27886807,
    -1.13520398,
    1.48851587,
    -0.82215223,
    0.17087277,
)


def gelu_parts(value):
    scaled = jnp.abs(value) * math.sqrt(0.5)
    inverse = 1.0 / (1.0 + 0.5 * scaled)
    power = TAIL[-1]
    for factor in TAIL[-2::-1]:
        power = power * inverse + factor
    square = scaled * scaled
    below = 0.5 * inverse * jnp.exp(power - square)
    share = jnp.where(value >= 0.0, 1.0 - below, below)
    slope = share + value * (math.sqrt(0.5 / math.pi) * jnp.exp(-square))
    return value * share, slope


@jax.custom_vjp
def gelu(value):
    return gelu_parts(value)[0]


gelu.defvjp(lambda value: lax.optimization_barrier(gelu_parts(value)), lambda slope, grad: (grad * slope,))


@functools.partial(jax.custom_vjp, nondiff_argnums=(1,))
def mark(value, on_way_back):
    return value


def mark_keep(value, on_way_back):
    return value, None


def mark_pull(on_way_back, kept, grad):
    return (on_way_back(grad),)


mark.defvjp(mark_keep, mark_pull)


def marked(value, marks, number):
    return value if marks is None or marks[number] is None else mark(value, marks[number])


def transformer_block(stream, params, head_count, keep, marks):
    (
        first_gain,
        first_shift,
        qkv_weight,
        query_bias,
        value_bias,
        out_weight,
        out_bias,
        second_gain,
        second_shift,
        up_weight,
        up_bias,
        down_weight,
        down_bias,
    ) = params
    normed = layer_norm(stream, first_gain, first_shift)
    joined = matmul(normed, qkv_weight)
    joined = joined + jnp.concatenate([query_bias, jnp.zeros_like(query_bias), value_bias])
    mixed = marked(attend(marked(joined, marks, 3), keep, head_count), marks, 2)
    stream = marked(stream + matmul(mixed, out_weight) + out_bias, marks, 1)
    normed = layer_norm(stream, second_gain, second_shift)
    before = marked(matmul(normed, up_weight) + up_bias, marks, 0)
    hidden = gelu(before)
    return stream + matmul(hidden, down_weight) + down_bias


def encode_item(encoder, patch_one, places, chosen, keep_one, marks):
    visible = jnp.take(patch_one, chosen, axis=0)
    stream = matmul(visible, encoder[0]) + encoder[1] + places
    stream = transformer_block(stream, encoder[2:15], HEADS_E, keep_one[None], marks)
    return layer_norm(stream, encoder[15], encoder[16])


def decode_item(decoder, encoded, patch_one, table, chosen, keep_one):
    slots = jnp.arange(KEEP_MAX)
    live = (slots < keep_one).astype(jnp.float32)
    token_ids = jnp.arange(TOK_ITEM)
    placer = (chosen[:, None] == token_ids[None, :]).astype(jnp.float32) * live[:, None]
    hidden_mask = 1.0 - jnp.sum(placer, axis=0)
    latent = matmul(encoded, decoder[0]) + decoder[1]
    stream = jnp.einsum("st,sd->td", placer, latent, precision=PREC)
    stream = stream + hidden_mask[:, None] * decoder[2][None, :] + table
    stream = transformer_block(stream, decoder[3:16], HEADS_D, None, None)
    normed = layer_norm(stream, decoder[16], decoder[17])
    predicted = matmul(normed, decoder[18]) + decoder[19]
    error = predicted - patch_one
    squared = jnp.sum(hidden_mask[:, None] * error * error)
    return (squared / (PATCH * PATCH), squared)


def body(
    count,
    pixels,
    running_mean,
    running_variance,
    momentum,
    keep_count,
    visible_index,
    encoder_flat,
    decoder_flat,
):
    all_count = 2 * count
    core = lax.axis_index("dp")
    me = lax.axis_index("fsdp")
    index = jnp.stack([me, core]).astype(jnp.int32)
    inverse = lax.rsqrt(running_variance + EPS_NORM)
    chosen, keep_one = visible_index[0], keep_count[0]

    def own_half(flat):
        rows = flat.shape[0] // (2 * LANES)
        half = lax.dynamic_index_in_dim(flat.reshape(2, rows, LANES), core, 0, keepdims=False)
        return jnp.pad(half, ((0, -rows % 8), (0, 0))), rows

    encoder_half, encoder_rows = own_half(encoder_flat)
    decoder_half, decoder_rows = own_half(decoder_flat)
    encoder_all = lax.all_gather(encoder_half, ("fsdp", "dp"), axis=0, tiled=False)
    patches, moments = patchify(pixels[0], running_mean, inverse)
    encoder_all, decoder_half, patches, moments, places, table = lax.optimization_barrier(
        (
            encoder_all,
            decoder_half,
            patches,
            moments,
            jnp.take(position_table(D_ENC), chosen, axis=0),
            position_table(D_DEC),
        )
    )
    decoder_all = lax.all_gather(decoder_half, ("fsdp", "dp"), axis=0, tiled=False)

    scatters = []

    def go_on(grad):
        grad = scatters[0].hold(grad)
        scatters[0].step()
        return grad

    marks = [go_on, None, go_on, None]
    encoder = unpack(index, [encoder_all], encoder_rows, all_count, False, encoder_shapes())
    encoded, encode_back = jax.vjp(
        lambda params, patch: encode_item(params, patch, places, chosen, keep_one, marks),
        encoder,
        patches,
    )
    decoder = unpack(index, [decoder_all], decoder_rows, all_count, False, decoder_shapes())
    objective, decode_back, squared = jax.vjp(
        lambda params, enc, patch: decode_item(params, enc, patch, table, chosen, keep_one),
        decoder,
        encoded,
        patches,
        has_aux=True,
    )
    grad_decoder, grad_encoded, grad_patches = decode_back(jnp.ones((), jnp.float32))
    masked_here = (TOK_ITEM - keep_one).astype(jnp.float32)
    stats = jnp.concatenate([moments[:, 0], moments[:, 1], jnp.stack([squared, masked_here])])
    place = jnp.arange(all_count)[:, None] == core * count + me
    tail = jnp.where(place, jnp.pad(stats, (0, 16 - stats.shape[0]))[None, :], 0.0)
    tail = tail.reshape(-1, LANES)
    packed = pack(
        index, grad_decoder, tail, decoder_shapes(), all_count, decoder_rows, True
    )
    scatters.append(Scatter(packed, count, False))
    scatters[0].step()
    grad_encoder, more_patches = encode_back(grad_encoded)
    grad_encoder = go_on(grad_encoder)

    packed = pack(
        index, grad_encoder, tail, encoder_shapes(), all_count, encoder_rows, True
    )
    packed = go_on(packed)
    decoder_sum = scatters[0].total()
    encoder_scatter = Scatter(packed, count, True)
    for _ in range(2):
        encoder_scatter.step()
    pixel_grad = unpatchify(grad_patches + more_patches, inverse)
    pixel_grad = encoder_scatter.hold(pixel_grad).reshape(pixels.shape)
    encoder_sum = encoder_scatter.total()
    totals = encoder_sum[encoder_rows : encoder_rows + tail.shape[0]].reshape(all_count, 16)
    totals = jnp.sum(totals, axis=0)

    pixel_count = float(all_count * FRAMES * IMG * IMG)
    band_mean = totals[:BANDS] / pixel_count
    band_var = totals[BANDS : 2 * BANDS] / pixel_count - band_mean * band_mean
    next_mean = (1.0 - momentum) * running_mean + momentum * band_mean
    next_variance = (1.0 - momentum) * running_variance + momentum * band_var
    masked_loss = totals[2 * BANDS] / (totals[2 * BANDS + 1] * PIX)
    return (
        masked_loss,
        pixel_grad,
        both_halves(encoder_sum, encoder_rows, core),
        both_halves(decoder_sum, decoder_rows, core),
        next_mean,
        next_variance,
    )


def solution(mesh):
    placed = (
        P(("dp", "fsdp"), None, None, None),
        P(),
        P(),
        P(),
        P(("dp", "fsdp")),
        P(("dp", "fsdp"), None),
        P("fsdp"),
        P("fsdp"),
    )
    return jax.shard_map(
        functools.partial(body, mesh.shape["fsdp"]),
        mesh=mesh,
        in_specs=placed,
        out_specs=(P(), P(("dp", "fsdp"), None, None, None), P("fsdp"), P("fsdp"), P(), P()),
        check_vma=False,
    )
```

```python
import functools
import math

import jax
import jax.numpy as jnp
from jax import lax
from jax.experimental import pallas as pl
from jax.experimental.pallas import tpu as pltpu
from jax.sharding import PartitionSpec as P

D_ENC = 768
HEADS_E = 12
MLP_E = 3072
D_DEC = 512
HEADS_D = 16
MLP_D = 2048
BANDS = 6
PATCH = 16
FRAMES = 3
GRID = 14
TOK_ITEM = 588
IMG = 224
PIX = 1536
KEEP_MAX = 236
LANES = 128
SMALL = 3072

EPS_NORM = 1e-06
MASKED_SCORE = -1e30
PREC = lax.Precision.HIGH
VMEM_LIMIT = 60 * 2**20


def matmul(left, right):
    return jnp.dot(left, right, precision=PREC, preferred_element_type=jnp.float32)


def block_shapes(width, hidden):
    return [
        (width,),
        (width,),
        (width, 3 * width),
        (width,),
        (width,),
        (width, width),
        (width,),
        (width,),
        (width,),
        (width, hidden),
        (hidden,),
        (hidden, width),
        (width,),
    ]


def encoder_shapes():
    return [(PIX, D_ENC), (D_ENC,)] + block_shapes(D_ENC, MLP_E) + [(D_ENC,), (D_ENC,)]


def decoder_shapes():
    return (
        [(D_ENC, D_DEC), (D_DEC,), (D_DEC,)]
        + block_shapes(D_DEC, MLP_D)
        + [(D_DEC,), (D_DEC,), (D_DEC, PIX), (PIX,)]
    )


def row_layout(shapes):
    matrices, vectors, row = [], [], 0
    for shape in shapes:
        if len(shape) == 2:
            matrices.append((row, shape[0], shape[1]))
        else:
            vectors.append((row, shape[0] // LANES))
        row += math.prod(shape) // LANES
    return matrices, vectors, row


SLOTS = 4
STAGE = 393216


def plan(shapes):
    blocks = []
    for at, (row, rows, columns) in enumerate(row_layout(shapes)[0]):
        size = max(r for r in range(8, rows + 1, 8) if rows % r == 0 and r * columns <= STAGE)
        for first in range(0, rows, size):
            blocks.append((at, first, size, columns, row + first * (columns // LANES)))
    return blocks


def stage_view(stage, slot, size, columns):
    return stage.at[slot, pl.ds(0, size), pl.ds(0, columns)]


def move_block(lin, stage, slot, size, columns, base, inward):
    tiles = columns // LANES
    groups = size // 8
    unroll = max(u for u in range(1, 9) if groups % u == 0 and u * tiles <= 48)

    def some(r, carry):
        for u in range(unroll):
            at = r * unroll + u
            for t in range(tiles):
                rows = pl.ds(base + at * (8 * tiles) + t, 8, stride=tiles)
                place = pl.ds(pl.multiple_of(at * 8, 8), 8)
                if inward:
                    stage[slot, place, t * LANES : (t + 1) * LANES] = lin[rows, :]
                else:
                    lin[rows, :] = stage[slot, place, t * LANES : (t + 1) * LANES]
        return carry

    lax.fori_loop(0, groups // unroll, some, 0)


def unpack_kernel(shapes, half_rows, piece_count, sources, relative, *refs):
    matrices, vectors, used = row_layout(shapes)
    index_ref = refs[0]
    ins = refs[1 : 1 + sources]
    outs = refs[1 + sources : 1 + sources + len(matrices)]
    small_ref = refs[1 + sources + len(matrices)]
    lin, stage, in_sem, out_sem = refs[2 + sources + len(matrices) :]
    me, core = index_ref[0], index_ref[1]

    def copy_piece(source, place):
        return pltpu.make_async_copy(
            source.at[pl.ds(0, half_rows)],
            lin.at[pl.ds(place * half_rows, half_rows)],
            in_sem.at[place],
        )

    if relative:
        pairs = piece_count // 4
        for side in range(2):
            for j in range(piece_count // 2):
                owner = jnp.bitwise_xor(me, j)
                half = core if side == 0 else 1 - core
                group, k, role = j // 8, j // 4 % 2, j % 4
                source = ins[side * (pairs // 4) + group]
                copy_piece(source.at[role * 2 + k], owner * 2 + half).start()
    else:
        for place in range(piece_count):
            copy_piece(ins[0].at[place], place).start()

    arrived = 0

    def wait_for(last, arrived):
        while arrived < piece_count and arrived * half_rows < last:
            copy_piece(ins[0].at[0], arrived).wait()
            arrived += 1
        return arrived

    copies = []
    for number, (at, first, size, columns, base) in enumerate(plan(shapes)):
        arrived = wait_for(base + size * (columns // LANES), arrived)
        slot = number % SLOTS
        if number >= SLOTS:
            copies[number - SLOTS].wait()
        move_block(lin, stage, slot, size, columns, base, True)
        copies.append(
            pltpu.make_async_copy(
                stage_view(stage, slot, size, columns),
                outs[at].at[pl.ds(first, size)],
                out_sem.at[slot],
            )
        )
        copies[-1].start()
    wait_for(piece_count * half_rows, arrived)
    small_ref[...] = jnp.zeros_like(small_ref)
    for i, (row, count) in enumerate(vectors):
        for t in range(count):
            small_ref[i : i + 1, t * LANES : (t + 1) * LANES] = lin[row + t : row + t + 1, :]
    for copy in copies[-SLOTS:]:
        copy.wait()


def unpack(index, sources, half_rows, piece_count, relative, shapes):
    matrices, vectors, _ = row_layout(shapes)
    any_spec = pl.BlockSpec(memory_space=pltpu.HBM)
    slots = -(-len(vectors) // 8) * 8
    total = piece_count * half_rows
    wide, flat = scratch_of(shapes, total)
    outs = pl.pallas_call(
        functools.partial(
            unpack_kernel, shapes, half_rows, piece_count, len(sources), relative
        ),
        out_shape=[jax.ShapeDtypeStruct(m[1:], jnp.float32) for m in matrices]
        + [jax.ShapeDtypeStruct((slots, SMALL), jnp.float32)],
        in_specs=[pl.BlockSpec(memory_space=pltpu.SMEM)] + [any_spec] * len(sources),
        out_specs=[any_spec] * len(matrices) + [pl.BlockSpec(memory_space=pltpu.VMEM)],
        scratch_shapes=[
            flat,
            wide,
            pltpu.SemaphoreType.DMA((piece_count,)),
            pltpu.SemaphoreType.DMA((SLOTS,)),
        ],
        compiler_params=pltpu.CompilerParams(vmem_limit_bytes=VMEM_LIMIT),
        cost_estimate=pl.CostEstimate(
            flops=0, bytes_accessed=8 * total * LANES, transcendentals=0
        ),
    )(index, *sources)
    small = outs[-1]
    pieces, matrix_at, vector_at = [], 0, 0
    for shape in shapes:
        if len(shape) == 2:
            pieces.append(outs[matrix_at])
            matrix_at += 1
        else:
            pieces.append(small[vector_at, : shape[0]])
            vector_at += 1
    return pieces


def scratch_of(shapes, total):
    blocks = plan(shapes)
    wide = pltpu.VMEM(
        (SLOTS, max(b[2] for b in blocks), max(b[3] for b in blocks)), jnp.float32
    )
    return wide, pltpu.VMEM((-(-total // 8) * 8, LANES), jnp.float32)


def pack_kernel(shapes, half_rows, piece_count, relative, *refs):
    matrices, vectors, used = row_layout(shapes)
    index_ref = refs[0]
    ins = refs[1 : 1 + len(matrices)]
    small_ref, tail_ref = refs[1 + len(matrices) : 3 + len(matrices)]
    outs = refs[3 + len(matrices) : -4]
    lin, stage, in_sem, out_sem = refs[-4:]
    me, core = index_ref[0], index_ref[1]
    tail_rows = tail_ref.shape[0]
    blocks = plan(shapes)

    def copy_in(number):
        at, first, size, columns, _ = blocks[number]
        slot = number % SLOTS
        return pltpu.make_async_copy(
            ins[at].at[pl.ds(first, size)],
            stage_view(stage, slot, size, columns),
            in_sem.at[slot],
        )

    for number in range(min(SLOTS - 1, len(blocks))):
        copy_in(number).start()

    for i, (row, count) in enumerate(vectors):
        for t in range(count):
            lin[row + t : row + t + 1, :] = small_ref[i : i + 1, t * LANES : (t + 1) * LANES]
    total = piece_count * half_rows
    if total > used:
        lin[used:total, :] = jnp.zeros((total - used, LANES), jnp.float32)

    def copies(place, target):
        return (
            pltpu.make_async_copy(
                lin.at[pl.ds(place * half_rows, half_rows)],
                target.at[pl.ds(0, half_rows)],
                out_sem.at[place, 0],
            ),
            pltpu.make_async_copy(
                tail_ref, target.at[pl.ds(half_rows, tail_rows)], out_sem.at[place, 1]
            ),
        )

    def send_piece(place):
        def start(target):
            for copy in copies(place, target):
                copy.start()

        if not relative:
            start(outs[0].at[place])
            return
        j = jnp.bitwise_xor(me, place // 2)
        within = lax.rem(j, 4) * 2 + lax.rem(lax.div(j, 4), 2)
        away = jnp.where(core == place % 2, 0, 2)
        corner = jnp.where(within < 6, 0, 1)
        target = lax.div(j, 8) * 4 + away + corner
        for number, out in enumerate(outs):

            @pl.when(target == number)
            def _(out=out, number=number):
                start(out.at[within - 6 if number % 2 else within])

    sent = 0
    for number, (at, first, size, columns, base) in enumerate(blocks):
        if number + SLOTS - 1 < len(blocks):
            copy_in(number + SLOTS - 1).start()
        copy_in(number).wait()
        move_block(lin, stage, number % SLOTS, size, columns, base, False)
        done = base + size * (columns // LANES)
        if number == len(blocks) - 1:
            done = total
        while (sent + 1) * half_rows <= done and sent < piece_count:
            send_piece(sent)
            sent += 1
    for place in range(piece_count):
        for copy in copies(place, outs[0].at[0]):
            copy.wait()


def padded_rows(half_rows, tail_rows):
    return -(-(half_rows + tail_rows) // 8) * 8


def pack(index, grads, tail, shapes, piece_count, half_rows, relative):
    matrices, vectors, _ = row_layout(shapes)
    padded = padded_rows(half_rows, tail.shape[0])
    tail = jnp.pad(tail, ((0, padded - half_rows - tail.shape[0]), (0, 0)))
    slots = -(-len(vectors) // 8) * 8
    mats = [g for g, s in zip(grads, shapes) if len(s) == 2]
    vecs = [jnp.pad(g, (0, SMALL - g.shape[0])) for g, s in zip(grads, shapes) if len(s) == 1]
    vecs += [jnp.zeros((SMALL,), jnp.float32)] * (slots - len(vecs))
    any_spec = pl.BlockSpec(memory_space=pltpu.HBM)
    vmem_spec = pl.BlockSpec(memory_space=pltpu.VMEM)
    total = piece_count * half_rows
    wide, flat = scratch_of(shapes, total)
    if relative:
        sizes = [6, 2, 6, 2] * (piece_count // 16)
    else:
        sizes = [piece_count]
    return pl.pallas_call(
        functools.partial(pack_kernel, shapes, half_rows, piece_count, relative),
        out_shape=[jax.ShapeDtypeStruct((n, padded, LANES), jnp.float32) for n in sizes],
        in_specs=[pl.BlockSpec(memory_space=pltpu.SMEM)]
        + [any_spec] * len(matrices)
        + [vmem_spec] * 2,
        out_specs=[any_spec] * len(sizes),
        scratch_shapes=[
            flat,
            wide,
            pltpu.SemaphoreType.DMA((SLOTS,)),
            pltpu.SemaphoreType.DMA((piece_count, 2)),
        ],
        compiler_params=pltpu.CompilerParams(vmem_limit_bytes=VMEM_LIMIT),
        cost_estimate=pl.CostEstimate(
            flops=0, bytes_accessed=8 * total * LANES, transcendentals=0
        ),
    )(index, *mats, jnp.stack(vecs), tail)


QUADS = FRAMES * GRID
GROUP = LANES // PATCH
STARTS = tuple(range(0, QUADS - 7, 8)) + ((QUADS - 8,) if QUADS % 8 else ())


def patch_kernel(mean_ref, inverse_ref, pixel_ref, patch_ref, moment_ref, scratch):
    band = pl.program_id(0)
    mean, inverse = mean_ref[band], inverse_ref[band]
    group = lax.broadcasted_iota(jnp.int32, (8, LANES), 1) // PATCH

    def sums(i, carry):
        one, two = carry
        value = pixel_ref[0, pl.ds(pl.multiple_of(i * 8, 8), 8), :]
        return one + value, two + value * value

    zero = jnp.zeros((8, LANES), jnp.float32)
    one, two = lax.fori_loop(0, pixel_ref.shape[1] // 8, sums, (zero, zero), unroll=7)
    moment_ref[0, 0] = one
    moment_ref[0, 1] = two
    for side in range(2):
        for first in STARTS:
            rows = []
            for k in range(GRID):
                start = 2 * GRID * first + GRID * side + k
                raw = pixel_ref[0, pl.ds(start, 8, stride=2 * GRID), :]
                rows.append((raw - mean) * inverse)
            for column in range(GRID):
                out = None
                for line in range(GROUP):
                    place = GRID * line + column
                    moved = pltpu.roll(rows[place // GROUP], PATCH * ((line - place) % GROUP), 1)
                    out = moved if out is None else jnp.where(group == line, moved, out)
                scratch[pl.ds(GRID * first + column, 8, stride=GRID), :] = out
        patch_ref[:, side * LANES : (side + 1) * LANES] = scratch[...]


def patchify(pixels, mean, inverse):
    rows = QUADS * 2 * GRID
    smem = pl.BlockSpec(memory_space=pltpu.SMEM)
    patches, moments = pl.pallas_call(
        patch_kernel,
        grid=(BANDS,),
        out_shape=[
            jax.ShapeDtypeStruct((TOK_ITEM, PIX), jnp.float32),
            jax.ShapeDtypeStruct((BANDS, 2, 8, LANES), jnp.float32),
        ],
        in_specs=[smem, smem, pl.BlockSpec((1, rows, LANES), lambda b: (b, 0, 0))],
        out_specs=[
            pl.BlockSpec((TOK_ITEM, 2 * LANES), lambda b: (0, b)),
            pl.BlockSpec((1, 2, 8, LANES), lambda b: (b, 0, 0, 0)),
        ],
        scratch_shapes=[pltpu.VMEM((TOK_ITEM, LANES), jnp.float32)],
        cost_estimate=pl.CostEstimate(
            flops=0, bytes_accessed=16 * TOK_ITEM * PIX, transcendentals=0
        ),
    )(mean, inverse, pixels.reshape(BANDS, rows, LANES))
    return patches, jnp.sum(moments, axis=(2, 3))


def pixel_kernel(inverse_ref, patch_ref, pixel_ref, scratch):
    inverse = inverse_ref[pl.program_id(0)]
    group = lax.broadcasted_iota(jnp.int32, (8, LANES), 1) // PATCH
    for side in range(2):
        scratch[...] = patch_ref[:, side * LANES : (side + 1) * LANES] * inverse
        for first in STARTS:
            columns = [
                scratch[pl.ds(GRID * first + column, 8, stride=GRID), :] for column in range(GRID)
            ]
            for k in range(GRID):
                out = None
                for slot in range(GROUP):
                    line, column = divmod(GROUP * k + slot, GRID)
                    moved = pltpu.roll(columns[column], PATCH * ((slot - line) % GROUP), 1)
                    out = moved if out is None else jnp.where(group == slot, moved, out)
                start = 2 * GRID * first + GRID * side + k
                pixel_ref[0, pl.ds(start, 8, stride=2 * GRID), :] = out


def unpatchify(grad_patches, inverse):
    rows = QUADS * 2 * GRID
    return pl.pallas_call(
        pixel_kernel,
        grid=(BANDS,),
        out_shape=jax.ShapeDtypeStruct((BANDS, rows, LANES), jnp.float32),
        in_specs=[
            pl.BlockSpec(memory_space=pltpu.SMEM),
            pl.BlockSpec((TOK_ITEM, 2 * LANES), lambda b: (0, b)),
        ],
        out_specs=pl.BlockSpec((1, rows, LANES), lambda b: (b, 0, 0)),
        scratch_shapes=[pltpu.VMEM((TOK_ITEM, LANES), jnp.float32)],
        cost_estimate=pl.CostEstimate(
            flops=0, bytes_accessed=16 * TOK_ITEM * PIX, transcendentals=0
        ),
    )(inverse, grad_patches)


def swap(value, distance, count):
    return lax.ppermute(value, "fsdp", [(i, i ^ distance) for i in range(count)])


def swap_cores(value):
    return lax.ppermute(value, "dp", [(0, 1), (1, 0)])


def split_row(rows):
    return rows // 16 * 8


class Scatter:
    def __init__(self, packed, count, fine):
        self.count, self.groups = count, len(packed) // 4
        self.middle = split_row(packed[0].shape[1])
        self.keep_sides, self.keep_corners = packed[::4], packed[1::4]
        self.sides, self.corners = packed[2::4], packed[3::4]
        self.fine = fine
        self.time = -1
        self.pending = {}
        self.own = {}
        self.landed = []

    def hold(self, value):
        value, self.pending = lax.optimization_barrier((value, self.pending))
        return value

    def step(self):
        count, groups, middle = self.count, self.groups, self.middle
        arrived, sent = self.pending, {}
        last, ready, new = groups + 1 - self.time, groups - self.time, groups - 1 - self.time
        if "turned" in arrived:
            near, turned = arrived["turned"]
            self.landed.append(swap(near + turned, 8 * (last + 1), count))
        if "late" in arrived:
            along_x, along_y = arrived["late"]
            self.landed.append(self.own[0][0] + along_x + along_y)
        if last == 0 and self.fine:
            along_x, along_y = arrived["sides"]
            self.landed.append(swap(self.own[0][1] + along_x + along_y, 4, count))
            for_x, for_y = self.late
            sent["late"] = [swap(for_x, 1, count), swap(for_y, 2, count)]
        elif 0 <= last < groups:
            along_x, along_y = arrived["sides"]
            part = self.own[last] + along_x + along_y
            turned = swap(part[1], 4, count)
            if last:
                sent["turned"] = (part[0], turned)
            else:
                self.landed += [part[0], turned]
        if 0 <= ready < groups:
            first, second = arrived["corner"]
            own, for_x, for_y = [
                (self.keep_sides[ready] + arrived["core sides"])[2 * i : 2 * i + 2] for i in range(3)
            ]
            self.own[ready] = own
            for_x = jnp.concatenate([for_x[:, :middle] + first, for_x[:, middle:]], axis=1)
            for_y = jnp.concatenate([for_y[:, :middle], for_y[:, middle:] + second], axis=1)
            if ready == 0 and self.fine:
                self.late = (for_x[0], for_y[0])
                for_x, for_y = for_x[1], for_y[1]
            sent["sides"] = [swap(for_x, 1, count), swap(for_y, 2, count)]
        if 0 <= new < groups:
            corner = self.keep_corners[new] + arrived["core corner"]
            sent["corner"] = [
                swap(corner[:, :middle], 2, count),
                swap(corner[:, middle:], 1, count),
            ]
            sides, _ = lax.optimization_barrier((self.sides[new], corner))
            sent["core sides"] = swap_cores(sides)
        if 0 <= new - 1 < groups:
            sent["core corner"] = swap_cores(self.corners[new - 1])
        self.pending = sent
        self.time += 1

    def total(self):
        while self.time < self.groups + (3 if self.fine else 2):
            self.step()
        return functools.reduce(jnp.add, self.landed)


def both_halves(half, rows, core):
    got = swap_cores(half)
    low = jnp.where(core == 0, half, got)[:rows]
    high = jnp.where(core == 0, got, half)[:rows]
    return jnp.concatenate([low, high]).reshape(-1)


def sincos_part(width, positions):
    frequency = 1.0 / 10000.0 ** (jnp.arange(width // 2).astype(jnp.float32) / (width / 2.0))
    angles = positions[:, None] * frequency[None, :]
    return jnp.concatenate([jnp.sin(angles), jnp.cos(angles)], axis=1)


def position_table(width):
    token_ids = jnp.arange(TOK_ITEM)
    frame_pos = (token_ids // (GRID * GRID)).astype(jnp.float32)
    row_pos = (token_ids // GRID % GRID).astype(jnp.float32)
    column_pos = (token_ids % GRID).astype(jnp.float32)
    return jnp.concatenate(
        [
            sincos_part(width // 16 * 4, frame_pos),
            sincos_part(width // 16 * 6, row_pos),
            sincos_part(width // 16 * 6, column_pos),
        ],
        axis=1,
    )


def layer_norm(values, gain, shift):
    centre = jnp.mean(values, axis=-1, keepdims=True)
    spread = jnp.mean(jnp.square(values - centre), axis=-1, keepdims=True)
    return (values - centre) * lax.rsqrt(spread + EPS_NORM) * gain + shift


QUERY_CHUNK = 640
KEY_CHUNK = 384


def split_two(value):
    high = value.astype(jnp.bfloat16)
    return high, (value - high.astype(jnp.float32)).astype(jnp.bfloat16)


def nt(left, right):
    return lax.dot_general(
        left, right, (((1,), (1,)), ((), ())), preferred_element_type=jnp.float32
    )


def nn(left, right):
    return jnp.dot(left, right, preferred_element_type=jnp.float32)


def chunks(rows, size):
    return [(at, min(size, rows - at)) for at in range(0, rows, size)]


def put_parts(ref, value, order):
    parts = split_two(value)
    for i, which in enumerate(order):
        ref[:, i * LANES : (i + 1) * LANES] = parts[which]


def put_turned(ref, value, size):
    for i, part in enumerate(split_two(value)):
        turned = part.astype(jnp.float32).T.astype(jnp.bfloat16)
        for head in range(LANES // size):
            ref[head, i * size : (i + 1) * size, :] = turned[head * size : (head + 1) * size, :]


def own_lanes(head, size, width):
    lane = lax.broadcasted_iota(jnp.int32, (1, width), 1)
    return (lax.rem(lane, LANES) // size == head).astype(jnp.float32).astype(jnp.bfloat16)


def hide_dead(scores, first, keep):
    if keep is None:
        return scores
    key = lax.broadcasted_iota(jnp.int32, scores.shape, 0) + first
    return jnp.where(key < keep, scores, MASKED_SCORE)


def turned_product(parts, high, low, size):
    both = nn(parts, high)
    return both[:size] + both[size:] + nn(parts[:size], low)


def attend_kernel(size, masked, keep_ref, q_ref, k_ref, v_ref, out_ref, lse_ref, q3, k3, v2t, out_t):
    head = pl.program_id(1)
    keep = keep_ref[0] if masked else None

    @pl.when(head == 0)
    def _():
        put_parts(q3, q_ref[...] * (1.0 / math.sqrt(size)), (0, 1, 0))
        put_parts(k3, k_ref[...], (0, 0, 1))
        put_turned(v2t, v_ref[...], size)

    lanes = own_lanes(head, size, 3 * LANES)
    values = v2t[head]
    for at, count in chunks(q_ref.shape[0], QUERY_CHUNK):
        place = slice(at, at + count)
        scores = hide_dead(nt(k3[...], q3[place, :] * lanes), 0, keep)
        top = jnp.max(scores, axis=0, keepdims=True)
        weights = jnp.exp(scores - top)
        total = jnp.sum(weights, axis=0, keepdims=True)
        high, low = split_two(weights)
        mixed = turned_product(values, high, low, size) / total
        out_t[pl.ds(pl.multiple_of(head * size, size), size), place] = mixed
        lse_ref[0, :, place] = top + jnp.log(total)

    @pl.when(head == LANES // size - 1)
    def _():
        out_ref[...] = out_t[...].T


def attend_forward(joined, keep, heads):
    rows, width = joined.shape[0], joined.shape[1] // 3
    size = width // heads
    blocks, per_block = width // LANES, LANES // size
    masked = keep is not None
    keep = keep if masked else jnp.zeros((1,), jnp.int32)

    def columns(first):
        return pl.BlockSpec((rows, LANES), lambda g, h: (0, first + g))

    return pl.pallas_call(
        functools.partial(attend_kernel, size, masked),
        grid=(blocks, per_block),
        out_shape=[
            jax.ShapeDtypeStruct((rows, width), jnp.float32),
            jax.ShapeDtypeStruct((heads, 1, rows), jnp.float32),
        ],
        in_specs=[
            pl.BlockSpec(memory_space=pltpu.SMEM),
            columns(0),
            columns(blocks),
            columns(2 * blocks),
        ],
        out_specs=[
            columns(0),
            pl.BlockSpec((1, 1, rows), lambda g, h: (g * per_block + h, 0, 0)),
        ],
        scratch_shapes=[
            pltpu.VMEM((rows, 3 * LANES), jnp.bfloat16),
            pltpu.VMEM((rows, 3 * LANES), jnp.bfloat16),
            pltpu.VMEM((per_block, 2 * size, rows), jnp.bfloat16),
            pltpu.VMEM((LANES, rows), jnp.float32),
        ],
        compiler_params=pltpu.CompilerParams(vmem_limit_bytes=VMEM_LIMIT),
        cost_estimate=pl.CostEstimate(
            flops=16 * rows * rows * width,
            bytes_accessed=16 * rows * width,
            transcendentals=heads * rows * rows,
        ),
    )(keep, joined, joined, joined)


def attend_back_kernel(
    size, masked, keep_ref, q_ref, k_ref, v_ref, g_ref, lse_ref, delta_ref, out_ref,
    q3, k3, v3, g3, q3m, g3m, k2t, dq_t, dq, dk, dv, sem,
):
    block, head = pl.program_id(0), pl.program_id(1)
    keep = keep_ref[0] if masked else None
    scale = 1.0 / math.sqrt(size)
    width = out_ref.shape[1] // 3

    @pl.when(head == 0)
    def _():
        put_parts(q3, q_ref[...] * scale, (0, 1, 0))
        put_parts(k3, k_ref[...], (0, 0, 1))
        put_parts(v3, v_ref[...], (0, 0, 1))
        put_parts(g3, g_ref[...], (0, 1, 0))
        put_turned(k2t, k_ref[...], size)
        dk[...] = jnp.zeros_like(dk)
        dv[...] = jnp.zeros_like(dv)

    lanes = own_lanes(head, size, 3 * LANES)
    q3m[...] = q3[...] * lanes
    g3m[...] = g3[...] * lanes
    lse, delta = lse_ref[0], delta_ref[0]
    turned = None
    for at, count in chunks(q_ref.shape[0], KEY_CHUNK):
        place = slice(at, at + count)
        scores = hide_dead(nt(k3[place, :], q3m[...]), at, keep)
        weights = jnp.exp(scores - lse)
        high, low = split_two(weights)
        both = nn(high, g3m[:, : 2 * LANES])
        dv[place, :] += both[:, :LANES] + both[:, LANES:] + nn(low, g3m[:, :LANES])
        change = weights * (nt(v3[place, :], g3m[...]) - delta)
        high, low = split_two(change)
        both = nn(high, q3m[:, : 2 * LANES])
        dk[place, :] += both[:, :LANES] + both[:, LANES:] + nn(low, q3m[:, :LANES])
        part = turned_product(k2t[head, :, place], high, low, size)
        turned = part if turned is None else turned + part
    dq_t[pl.ds(pl.multiple_of(head * size, size), size), :] = turned

    @pl.when(head == LANES // size - 1)
    def _():
        dq[...] = dq_t[...].T * scale
        copies = [
            pltpu.make_async_copy(
                source,
                out_ref.at[:, pl.ds(pl.multiple_of(i * width + block * LANES, LANES), LANES)],
                sem.at[i],
            )
            for i, source in enumerate((dq, dk, dv))
        ]
        for copy in copies:
            copy.start()
        for copy in copies:
            copy.wait()


def attend_backward(joined, keep, heads, grad, lse, delta):
    rows, width = joined.shape[0], joined.shape[1] // 3
    size = width // heads
    blocks, per_block = width // LANES, LANES // size
    masked = keep is not None
    keep = keep if masked else jnp.zeros((1,), jnp.int32)

    def columns(first):
        return pl.BlockSpec((rows, LANES), lambda g, h: (0, first + g))

    per_head = pl.BlockSpec((1, 1, rows), lambda g, h: (g * per_block + h, 0, 0))
    return pl.pallas_call(
        functools.partial(attend_back_kernel, size, masked),
        grid=(blocks, per_block),
        out_shape=jax.ShapeDtypeStruct((rows, 3 * width), jnp.float32),
        in_specs=[
            pl.BlockSpec(memory_space=pltpu.SMEM),
            columns(0),
            columns(blocks),
            columns(2 * blocks),
            columns(0),
            per_head,
            per_head,
        ],
        out_specs=pl.BlockSpec(memory_space=pltpu.HBM),
        scratch_shapes=[pltpu.VMEM((rows, 3 * LANES), jnp.bfloat16)] * 6
        + [
            pltpu.VMEM((per_block, 2 * size, rows), jnp.bfloat16),
            pltpu.VMEM((LANES, rows), jnp.float32),
        ]
        + [pltpu.VMEM((rows, LANES), jnp.float32)] * 3
        + [pltpu.SemaphoreType.DMA((3,))],
        compiler_params=pltpu.CompilerParams(vmem_limit_bytes=VMEM_LIMIT),
        cost_estimate=pl.CostEstimate(
            flops=40 * rows * rows * width,
            bytes_accessed=28 * rows * width,
            transcendentals=heads * rows * rows,
        ),
    )(keep, joined, joined, joined, grad, lse, delta)


@functools.partial(jax.custom_vjp, nondiff_argnums=(2,))
def attend(joined, keep, heads):
    return attend_forward(joined, keep, heads)[0]


def attend_keep(joined, keep, heads):
    out, lse = attend_forward(joined, keep, heads)
    return out, (joined, keep, out, lse)


def attend_pull(heads, kept, grad):
    joined, keep, out, lse = kept
    width = out.shape[1]
    owner = jnp.arange(width)[None, :] // (width // heads) == jnp.arange(heads)[:, None]
    delta = lax.dot_general(
        owner.astype(jnp.float32),
        grad * out,
        (((1,), (1,)), ((), ())),
        precision=lax.Precision.HIGHEST,
        preferred_element_type=jnp.float32,
    )
    return attend_backward(joined, keep, heads, grad, lse, delta[:, None, :]), None


attend.defvjp(attend_keep, attend_pull)


TAIL = (
    -1.26551223,
    1.00002368,
    0.37409196,
    0.09678418,
    -0.18628806,
    0.27886807,
    -1.13520398,
    1.48851587,
    -0.82215223,
    0.17087277,
)


def gelu_parts(value):
    scaled = jnp.abs(value) * math.sqrt(0.5)
    inverse = 1.0 / (1.0 + 0.5 * scaled)
    power = TAIL[-1]
    for factor in TAIL[-2::-1]:
        power = power * inverse + factor
    square = scaled * scaled
    below = 0.5 * inverse * jnp.exp(power - square)
    share = jnp.where(value >= 0.0, 1.0 - below, below)
    slope = share + value * (math.sqrt(0.5 / math.pi) * jnp.exp(-square))
    return value * share, slope


@jax.custom_vjp
def gelu(value):
    return gelu_parts(value)[0]


gelu.defvjp(lambda value: lax.optimization_barrier(gelu_parts(value)), lambda slope, grad: (grad * slope,))


@functools.partial(jax.custom_vjp, nondiff_argnums=(1,))
def mark(value, on_way_back):
    return value


def mark_keep(value, on_way_back):
    return value, None


def mark_pull(on_way_back, kept, grad):
    return (on_way_back(grad),)


mark.defvjp(mark_keep, mark_pull)


def marked(value, marks, number):
    return value if marks is None or marks[number] is None else mark(value, marks[number])


def transformer_block(stream, params, head_count, keep, marks):
    (
        first_gain,
        first_shift,
        qkv_weight,
        query_bias,
        value_bias,
        out_weight,
        out_bias,
        second_gain,
        second_shift,
        up_weight,
        up_bias,
        down_weight,
        down_bias,
    ) = params
    normed = layer_norm(stream, first_gain, first_shift)
    joined = matmul(normed, qkv_weight)
    joined = joined + jnp.concatenate([query_bias, jnp.zeros_like(query_bias), value_bias])
    mixed = marked(attend(marked(joined, marks, 3), keep, head_count), marks, 2)
    stream = marked(stream + matmul(mixed, out_weight) + out_bias, marks, 1)
    normed = layer_norm(stream, second_gain, second_shift)
    before = marked(matmul(normed, up_weight) + up_bias, marks, 0)
    hidden = gelu(before)
    return stream + matmul(hidden, down_weight) + down_bias


def encode_item(encoder, patch_one, places, chosen, keep_one, marks):
    visible = jnp.take(patch_one, chosen, axis=0)
    stream = matmul(visible, encoder[0]) + encoder[1] + places
    stream = transformer_block(stream, encoder[2:15], HEADS_E, keep_one[None], marks)
    return layer_norm(stream, encoder[15], encoder[16])


def decode_item(decoder, encoded, patch_one, table, chosen, keep_one):
    slots = jnp.arange(KEEP_MAX)
    live = (slots < keep_one).astype(jnp.float32)
    token_ids = jnp.arange(TOK_ITEM)
    placer = (chosen[:, None] == token_ids[None, :]).astype(jnp.float32) * live[:, None]
    hidden_mask = 1.0 - jnp.sum(placer, axis=0)
    latent = matmul(encoded, decoder[0]) + decoder[1]
    stream = jnp.einsum("st,sd->td", placer, latent, precision=PREC)
    stream = stream + hidden_mask[:, None] * decoder[2][None, :] + table
    stream = transformer_block(stream, decoder[3:16], HEADS_D, None, None)
    normed = layer_norm(stream, decoder[16], decoder[17])
    predicted = matmul(normed, decoder[18]) + decoder[19]
    error = predicted - patch_one
    squared = jnp.sum(hidden_mask[:, None] * error * error)
    return (squared / (PATCH * PATCH), squared)


def body(
    count,
    pixels,
    running_mean,
    running_variance,
    momentum,
    keep_count,
    visible_index,
    encoder_flat,
    decoder_flat,
):
    all_count = 2 * count
    core = lax.axis_index("dp")
    me = lax.axis_index("fsdp")
    index = jnp.stack([me, core]).astype(jnp.int32)
    inverse = lax.rsqrt(running_variance + EPS_NORM)
    chosen, keep_one = visible_index[0], keep_count[0]

    def own_half(flat):
        rows = flat.shape[0] // (2 * LANES)
        half = lax.dynamic_index_in_dim(flat.reshape(2, rows, LANES), core, 0, keepdims=False)
        return jnp.pad(half, ((0, -rows % 8), (0, 0))), rows

    encoder_half, encoder_rows = own_half(encoder_flat)
    decoder_half, decoder_rows = own_half(decoder_flat)
    encoder_all = lax.all_gather(encoder_half, ("fsdp", "dp"), axis=0, tiled=False)
    patches, moments = patchify(pixels[0], running_mean, inverse)
    encoder_all, decoder_half, patches, moments, places, table = lax.optimization_barrier(
        (
            encoder_all,
            decoder_half,
            patches,
            moments,
            jnp.take(position_table(D_ENC), chosen, axis=0),
            position_table(D_DEC),
        )
    )
    decoder_all = lax.all_gather(decoder_half, ("fsdp", "dp"), axis=0, tiled=False)

    scatters = []

    def go_on(grad):
        grad = scatters[0].hold(grad)
        scatters[0].step()
        return grad

    marks = [go_on, None, go_on, None]
    encoder = unpack(index, [encoder_all], encoder_rows, all_count, False, encoder_shapes())
    encoded, encode_back = jax.vjp(
        lambda params, patch: encode_item(params, patch, places, chosen, keep_one, marks),
        encoder,
        patches,
    )
    decoder = unpack(index, [decoder_all], decoder_rows, all_count, False, decoder_shapes())
    objective, decode_back, squared = jax.vjp(
        lambda params, enc, patch: decode_item(params, enc, patch, table, chosen, keep_one),
        decoder,
        encoded,
        patches,
        has_aux=True,
    )
    grad_decoder, grad_encoded, grad_patches = decode_back(jnp.ones((), jnp.float32))
    masked_here = (TOK_ITEM - keep_one).astype(jnp.float32)
    stats = jnp.concatenate([moments[:, 0], moments[:, 1], jnp.stack([squared, masked_here])])
    place = jnp.arange(all_count)[:, None] == core * count + me
    tail = jnp.where(place, jnp.pad(stats, (0, 16 - stats.shape[0]))[None, :], 0.0)
    tail = tail.reshape(-1, LANES)
    packed = pack(
        index, grad_decoder, tail, decoder_shapes(), all_count, decoder_rows, True
    )
    scatters.append(Scatter(packed, count, True))
    scatters[0].step()
    grad_encoder, more_patches = encode_back(grad_encoded)
    grad_encoder = go_on(grad_encoder)

    packed = pack(
        index, grad_encoder, tail, encoder_shapes(), all_count, encoder_rows, True
    )
    packed = go_on(packed)
    decoder_sum = scatters[0].total()
    encoder_scatter = Scatter(packed, count, True)
    for _ in range(2):
        encoder_scatter.step()
    pixel_grad = unpatchify(grad_patches + more_patches, inverse)
    pixel_grad = encoder_scatter.hold(pixel_grad).reshape(pixels.shape)
    encoder_sum = encoder_scatter.total()
    totals = encoder_sum[encoder_rows : encoder_rows + tail.shape[0]].reshape(all_count, 16)
    totals = jnp.sum(totals, axis=0)

    pixel_count = float(all_count * FRAMES * IMG * IMG)
    band_mean = totals[:BANDS] / pixel_count
    band_var = totals[BANDS : 2 * BANDS] / pixel_count - band_mean * band_mean
    next_mean = (1.0 - momentum) * running_mean + momentum * band_mean
    next_variance = (1.0 - momentum) * running_variance + momentum * band_var
    masked_loss = totals[2 * BANDS] / (totals[2 * BANDS + 1] * PIX)
    return (
        masked_loss,
        pixel_grad,
        both_halves(encoder_sum, encoder_rows, core),
        both_halves(decoder_sum, decoder_rows, core),
        next_mean,
        next_variance,
    )


def solution(mesh):
    placed = (
        P(("dp", "fsdp"), None, None, None),
        P(),
        P(),
        P(),
        P(("dp", "fsdp")),
        P(("dp", "fsdp"), None),
        P("fsdp"),
        P("fsdp"),
    )
    return jax.shard_map(
        functools.partial(body, mesh.shape["fsdp"]),
        mesh=mesh,
        in_specs=placed,
        out_specs=(P(), P(("dp", "fsdp"), None, None, None), P("fsdp"), P("fsdp"), P(), P()),
        check_vma=False,
    )
```
